32 devices in a mesh: dp: 2 (over x), row: 4 (over y, core), col: 4 (over z).
Axes of the slice: x: 2, y: 2, z: 4, core: 2. Of those that a mesh axis runs over, the one named last changes fastest.
Arguments:
- block_input: bfloat16 [4096, 1536], P(('dp', 'row'), 'col'), may hold values from -6 to 6
- deal_order: int32 [2, 2048], P('dp'), may hold values from 0 to 2047, each once within a row
- lengths: int32 [2, 6], P('dp'), may hold values from 1 to 1024, 2048 in all within a row
- routes: int32 [4096, 8], P('dp'), may hold values from 0 to 39, all different within a row; in each aligned block of 2048 rows (0 to 2047, 2048 to 4095, ...) at most 512 rows name the same one
- first_gain: bfloat16 [1536], P('col'), may hold values from 0.5 to 1.5
- w_query: bfloat16 [1536, 1536], P('col', 'row'), may hold values from -0.15625 to 0.15625
- key_weight: bfloat16 [1536, 512], P('col', 'row'), may hold values from -0.15625 to 0.15625
- value_weight: bfloat16 [1536, 512], P('col', 'row'), may hold values from -0.15625 to 0.15625
- w_out: bfloat16 [1536, 1536], P('row', 'col'), may hold values from -1.25 to 1.25
- gain_two: bfloat16 [1536], P('col'), may hold values from 0.5 to 1.5
- w_router: bfloat16 [1536, 40], P('col'), may hold values from -0.078125 to 0.078125
- w_gate: bfloat16 [40, 1536, 512], P(None, 'col', 'row'), may hold values from -0.15625 to 0.15625
- w_up: bfloat16 [40, 1536, 512], P(None, 'col', 'row'), may hold values from -0.15625 to 0.15625
- w_down: bfloat16 [40, 512, 1536], P(None, 'row', 'col'), may hold values from -1 to 1
- cotangent: bfloat16 [4096, 1536], P(('dp', 'row'), 'col'), may hold values from -6 to 6
Outputs:
- block_output: bfloat16 [4096, 1536], P(('dp', 'row'), 'col')
- input_gradient: float32 [4096, 1536], P(('dp', 'row'), 'col')
- first_gain_gradient: float32 [1536], P('col')
- d_query: float32 [1536, 1536], P('col', 'row')
- d_key: float32 [1536, 512], P('col', 'row')
- d_value: float32 [1536, 512], P('col', 'row')
- d_out: float32 [1536, 1536], P('row', 'col')
- d_gain_two: float32 [1536], P('col')
- d_router: float32 [1536, 40], P('col')
- d_gate: float32 [40, 1536, 512], P(None, 'col', 'row')
- d_up: float32 [40, 1536, 512], P(None, 'col', 'row')
- d_down: float32 [40, 512, 1536], P(None, 'row', 'col')
The draws below stay inside these ranges and needn't reach their ends.
Inputs may be any that keep to these rules, and one draw needn't show every extreme that they name: Each row of deal_order is a permutation of the 2048 packed positions of its group. `lengths`: each row sums to 2048; its largest entry is exactly 1024. `routes`: A row names 8 different experts. Within the rows of one group (aligned blocks of 2048 rows) no expert is named by more than 512 rows, a bound that some block reaches.
All inputs are finite; a program needn't handle non-finite values.
Results may differ from the reference program's by a relative error of at most 0.025.
Values may be sent and summed in bfloat16 or wider, within the bound.
A program may use at most 256 MiB of HBM per device.

```python
import math
import jax
import jax.numpy as jnp
import numpy as np
from jax import lax

MODEL_WIDTH = 1536
QUERY_HEADS = 24
KEY_VALUE_HEADS = 8
HEAD_SIZE = 64
FFE = 512
EXPERTS = 40
TOPK = 8
SEQS = 6
GROUP_TOK = 2048
TOKENS = 4096
CAP = 512
N_DP = 2


def level_of(key, shape, shards, low, top_value):
    def one(position, parts):
        draws = jax.random.uniform(jax.random.fold_in(jax.random.fold_in(key, 6), position), (parts,), jnp.float32, low / len(shards), top_value / len(shards))
        return jnp.repeat(jnp.exp(draws), shape[position] // parts).reshape((-1,) + (1,) * (len(shape) - position - 1))

    factor_of = one(*shards[0])
    for cut in shards[1:]:
        factor_of = factor_of * one(*cut)
    return factor_of


def split_up(amount, total, bound, lean):
    loads = [(1 << 20) // math.isqrt(grade ** lean) + 1 for grade in range(2, amount + 1)]
    surplus, holding = total - bound - (amount - 1), [1] * (amount - 1)
    while surplus > 0:
        candidates = [i for i in range(amount - 1) if holding[i] < bound]
        whole, left = sum([loads[i] for i in candidates]), surplus
        for i in candidates:
            addition = min(bound - holding[i], max(1, left * loads[i] // whole), surplus)
            holding[i] = holding[i] + addition
            surplus = surplus - addition
    return np.array([bound] + holding)


def uneven_parts(stream_key, amount, total, reach, slope):
    if amount == 2:
        one = jax.random.randint(stream_key, (), max(1, total - reach), min(reach, total - 1) + 1)
        return jnp.stack([one, total - one])
    sizes = jnp.asarray(split_up(amount, total, reach, slope), jnp.int32)
    pairs = (amount - 1) // 2
    source_of, sink = sizes[1:1 + 2 * pairs:2], sizes[2:2 + 2 * pairs:2]
    slack = jnp.minimum(source_of - 1, reach - sink)
    passed = jax.random.randint(jax.random.fold_in(stream_key, 1), (pairs,), 0, 1 << 20) % (slack + 1)
    sizes = sizes.at[1:1 + 2 * pairs:2].set(source_of - passed).at[2:2 + 2 * pairs:2].set(sink + passed)
    return sizes[jax.random.permutation(jax.random.fold_in(stream_key, 2), amount)]


def deal_out(own_key, own, number, rows, number_of, top, bound, slope):
    ranking = jax.random.permutation(own_key, number_of)
    crowded, ordinary = portions_of(number_of, rows * top, bound, slope, True), portions_of(number_of, rows * top, bound, slope, False)
    places = jnp.arange(number_of)

    def named(sizes, rotation):
        used = int((sizes > 0).sum())
        fixed = max(1, used // 4)
        passed = fixed + (places - fixed + rotation * (used - fixed)) % max(1, number_of - fixed)
        return jnp.zeros((number_of,), jnp.int32).at[ranking[jnp.where(places < fixed, places, passed)]].set(jnp.asarray(sizes, jnp.int32))

    sizes = jnp.where(number % 4 == 0, named(crowded, number // 4), named(ordinary, number - number // 4 - 1))
    mixed = jax.random.permutation(jax.random.fold_in(own, 3), number_of)
    source_of, receiver = mixed[0:number_of // 2 * 2:2], mixed[1:number_of // 2 * 2:2]
    room = jnp.minimum(sizes[source_of] - 1, bound - sizes[receiver]) // 2
    room = jnp.where((source_of == ranking[0]) | (receiver == ranking[0]) | (sizes[receiver] == 0), 0, jnp.maximum(room, 0))
    passed = jax.random.randint(jax.random.fold_in(own, 4), (number_of // 2,), 0, 1 << 20) % (room + 1)
    sizes = sizes.at[source_of].add(-passed).at[receiver].add(passed)
    items = jnp.searchsorted(jnp.cumsum(sizes), jnp.arange(rows * top), side="right").astype(jnp.int32)
    table = items.reshape(top, rows).T
    table = table[jax.random.permutation(jax.random.fold_in(own, 1), rows)]
    rotation = jax.random.randint(jax.random.fold_in(own, 2), (rows, 1), 0, top)
    return jnp.take_along_axis(table, (jnp.arange(top)[None, :] + rotation) % top, axis=1)


def portions_of(number_of, total, bound, slope, full):
    portions = [(1 << 20) // math.isqrt(standing ** slope) + 1 for standing in range(1, number_of + 1)]
    largest = bound if full else min(bound, max(-(-total // number_of), total * portions[0] // sum(portions)))
    least = 1 if total - largest >= number_of - 1 else 0
    given, rest = [largest] + [least] * (number_of - 1), total - largest - least * (number_of - 1)
    while rest > 0:
        free = [i for i in range(1, number_of) if given[i] < largest] or [i for i in range(1, number_of) if given[i] < bound]
        pool, left = sum([portions[i] for i in free]), rest
        for i in free:
            extra = min(bound - given[i], max(1, left * portions[i] // pool), rest)
            given[i] = given[i] + extra
            rest = rest - extra
    return np.array(given)


def noise(stream_key, extent, scale, bound, pieces=(), kind=jnp.bfloat16):
    array = jax.random.normal(stream_key, extent, jnp.float32) * scale
    if len(pieces) > 0:
        array = level_of(stream_key, extent, pieces, -0.22, 0.18) * array
    return jnp.clip(array, min=-bound, max=bound).astype(kind)


def setup_inputs(seed: int = 0) -> dict:
    keys = jax.random.split(jax.random.key(seed), 16)
    block_input = noise(keys[0], (TOKENS, MODEL_WIDTH), 1.0, 6.0, ((0, 8), (1, 4)))
    deal_order = jax.vmap(lambda own: jax.random.permutation(own, GROUP_TOK))(jax.random.split(keys[1], N_DP)).reshape((N_DP, GROUP_TOK)).astype(jnp.int32)
    lengths = jax.vmap(lambda own: uneven_parts(own, SEQS, GROUP_TOK, GROUP_TOK // 2, 2))(jax.random.split(keys[2], N_DP)).reshape((N_DP, SEQS)).astype(jnp.int32)
    routes_keys = jax.random.split(jax.random.fold_in(keys[3], 1), TOKENS // GROUP_TOK)
    routes_turns = jax.random.permutation(jax.random.fold_in(keys[3], 3), TOKENS // GROUP_TOK)
    routes = jax.vmap(lambda own, number: deal_out(jax.random.fold_in(keys[3], 2), own, number, GROUP_TOK, EXPERTS, TOPK, CAP, 1))(routes_keys, routes_turns).reshape((TOKENS, TOPK))
    first_gain = jnp.clip(1.0 + 0.1 * jax.random.normal(keys[4], (MODEL_WIDTH,), jnp.float32), 0.5, 1.5).astype(jnp.bfloat16)
    w_query = noise(keys[5], (MODEL_WIDTH, QUERY_HEADS * HEAD_SIZE), MODEL_WIDTH ** -0.5, 0.15625, ((0, 4), (1, 4)))
    key_weight = noise(keys[6], (MODEL_WIDTH, KEY_VALUE_HEADS * HEAD_SIZE), MODEL_WIDTH ** -0.5, 0.15625, ((0, 4), (1, 4)))
    value_weight = noise(keys[7], (MODEL_WIDTH, KEY_VALUE_HEADS * HEAD_SIZE), MODEL_WIDTH ** -0.5, 0.15625, ((0, 4), (1, 4)))
    w_out = noise(keys[8], (QUERY_HEADS * HEAD_SIZE, MODEL_WIDTH), (QUERY_HEADS * HEAD_SIZE // 64) ** -0.5, 1.25, ((0, 4), (1, 4)))
    gain_two = jnp.clip(1.0 + 0.1 * jax.random.normal(keys[9], (MODEL_WIDTH,), jnp.float32), 0.5, 1.5).astype(jnp.bfloat16)
    w_router = noise(keys[10], (MODEL_WIDTH, EXPERTS), (4 * MODEL_WIDTH) ** -0.5, 0.078125, ((0, 4),))
    w_gate = noise(keys[11], (EXPERTS, MODEL_WIDTH, FFE), MODEL_WIDTH ** -0.5, 0.15625, ((1, 4), (2, 4)))
    w_up = noise(keys[12], (EXPERTS, MODEL_WIDTH, FFE), MODEL_WIDTH ** -0.5, 0.15625, ((1, 4), (2, 4)))
    w_down = noise(keys[13], (EXPERTS, FFE, MODEL_WIDTH), (FFE // 16) ** -0.5, 1.0, ((1, 4), (2, 4)))
    cotangent = noise(keys[14], (TOKENS, MODEL_WIDTH), 1.0, 6.0, ((0, 8), (1, 4)))
    return dict(block_input=block_input, deal_order=deal_order, lengths=lengths, routes=routes, first_gain=first_gain, w_query=w_query, key_weight=key_weight, value_weight=value_weight, w_out=w_out, gain_two=gain_two, w_router=w_router, w_gate=w_gate, w_up=w_up, w_down=w_down, cotangent=cotangent)


NORM_EPSILON = 1e-06
THETA = 10000.0
FILLER = -1e+30
HIGH = lax.Precision.HIGHEST

@jax.custom_vjp
def lower_precision(v):
    return lax.optimization_barrier(v.astype(jnp.bfloat16)).astype(jnp.float32)

@jax.custom_vjp
def lower_precision_back(v):
    return v

def low_keep(v):
    return (lower_precision(v), None)

def low_pass(kept, grad):
    return (grad,)

def back_keep(v):
    return (v, None)

def back_low(kept, grad):
    return (lower_precision(grad),)
lower_precision.defvjp(low_keep, low_pass)
lower_precision_back.defvjp(back_keep, back_low)

def product_result(left, right):
    return jnp.dot(left, right, precision=HIGH, preferred_element_type=jnp.float32)

def rope_tables(positions):
    half_head = HEAD_SIZE // 2
    frequency = THETA ** (-(2.0 / HEAD_SIZE) * jnp.arange(half_head).astype(jnp.float32))
    angles = positions.astype(jnp.float32)[:, None] * frequency[None, :]
    return (jnp.cos(angles), jnp.sin(angles))

def apply_rotation(vector, cosine_table, sine_table):
    half_head = vector.shape[-1] // 2
    first = vector[..., :half_head]
    second = vector[..., half_head:]
    cos_b = cosine_table[:, None, :]
    sin_b = sine_table[:, None, :]
    return jnp.concatenate([first * cos_b - second * sin_b, second * cos_b + first * sin_b], axis=-1)

def places(orders, lengths):
    ends = jnp.cumsum(lengths)
    starts = ends - lengths
    inside = ((orders[:, None] >= starts[None, :]) & (orders[:, None] < ends[None, :])).astype(jnp.int32)
    seq_ids = lax.optimization_barrier(jnp.sum(inside * jnp.arange(lengths.shape[0], dtype=jnp.int32)[None, :], axis=1))
    positions = orders - lax.optimization_barrier(jnp.sum(inside * starts[None, :], axis=1))
    return (seq_ids, positions)

def slots(routes, experts, capacity):
    group_width_count = routes.shape[0]
    onehot = (routes[:, :, None] == jnp.arange(experts, dtype=jnp.int32)[None, None, :]).astype(jnp.int32)
    per_token = lax.optimization_barrier(jnp.sum(onehot, axis=1))
    earlier = jnp.cumsum(per_token, axis=0) - per_token
    slot_ids = lax.optimization_barrier(jnp.sum(onehot * earlier[:, None, :], axis=2))
    slot_index = routes * capacity + slot_ids
    tokens = jnp.repeat(jnp.arange(group_width_count, dtype=jnp.int32), routes.shape[1])
    owner = jnp.full((experts * capacity,), group_width_count, jnp.int32).at[slot_index.reshape(-1)].set(tokens)
    return (slot_index, owner)

def attention(queries, rotated_key_rows, value_rows, orders, seq_ids):
    group_width_count = queries.shape[0]
    score_scale = 1.0 / math.sqrt(HEAD_SIZE)
    block_rows = math.gcd(group_width_count, 512)
    widened_keys = jnp.repeat(rotated_key_rows, QUERY_HEADS // KEY_VALUE_HEADS, axis=1)
    widened_values = jnp.repeat(value_rows, QUERY_HEADS // KEY_VALUE_HEADS, axis=1)
    blocks_q = queries.reshape(group_width_count // block_rows, block_rows, QUERY_HEADS, HEAD_SIZE)
    blocks_o = orders.reshape(group_width_count // block_rows, block_rows)
    blocks_s = seq_ids.reshape(group_width_count // block_rows, block_rows)

    @jax.checkpoint
    def one_block(element):
        q_rows, o_rows, s_rows = element
        visible = (s_rows[:, None] == seq_ids[None, :]) & (orders[None, :] <= o_rows[:, None])
        raw_scores = jnp.einsum('bhd,nhd->hbn', q_rows, widened_keys, precision=HIGH)
        scores = jnp.where(visible[None], lower_precision_back(raw_scores * score_scale), FILLER)
        highest = lax.optimization_barrier(jnp.max(scores, axis=2, keepdims=True))
        weights = jnp.exp(scores - highest)
        chances = lower_precision(weights / lax.optimization_barrier(jnp.sum(weights, axis=2, keepdims=True)))
        return jnp.einsum('hbn,nhd->bhd', chances, widened_values, precision=HIGH)
    outputs = lax.map(one_block, (blocks_q, blocks_o, blocks_s))
    return outputs.reshape(group_width_count, QUERY_HEADS, HEAD_SIZE)

def layer(params, input_rows, orders, lengths, routes):
    w_query, key_weight, value_weight, w_out, first_gain, gain_two, w_router, w_gate, w_up, w_down = params
    group_width_count = input_rows.shape[0]
    seq_ids, positions = places(orders, lengths)
    cosine_table, sine_table = rope_tables(positions)
    first_normalized_input = input_rows * lax.rsqrt(lax.optimization_barrier(jnp.mean(input_rows * input_rows, axis=1, keepdims=True)) + NORM_EPSILON)
    normed_rows = lower_precision(first_normalized_input * first_gain)
    queries = lower_precision(apply_rotation(lower_precision_back(product_result(normed_rows, w_query)).reshape(group_width_count, QUERY_HEADS, HEAD_SIZE), cosine_table, sine_table))
    rotated_key_rows = lower_precision(apply_rotation(lower_precision_back(product_result(normed_rows, key_weight)).reshape(group_width_count, KEY_VALUE_HEADS, HEAD_SIZE), cosine_table, sine_table))
    value_rows = lower_precision(lower_precision_back(product_result(normed_rows, value_weight))).reshape(group_width_count, KEY_VALUE_HEADS, HEAD_SIZE)
    mixed = lower_precision(lower_precision_back(attention(queries, rotated_key_rows, value_rows, orders, seq_ids))).reshape(group_width_count, QUERY_HEADS * HEAD_SIZE)
    hidden = input_rows + lower_precision_back(product_result(mixed, w_out))
    hidden_hat = hidden * lax.rsqrt(lax.optimization_barrier(jnp.mean(hidden * hidden, axis=1, keepdims=True)) + NORM_EPSILON)
    normed_two = lower_precision(hidden_hat * gain_two)
    logits = lower_precision_back(product_result(normed_two, w_router))
    slot_index, owner = slots(routes, EXPERTS, CAP)
    gates = jax.nn.softmax(jnp.take_along_axis(logits, routes, axis=1), axis=1)
    padded = jnp.concatenate([normed_two, jnp.zeros((1, MODEL_WIDTH), jnp.float32)], axis=0)
    expert_in = padded[owner].reshape(EXPERTS, CAP, MODEL_WIDTH)
    gate_slot = jnp.zeros((EXPERTS * CAP,), jnp.float32).at[slot_index.reshape(-1)].set(gates.reshape(-1)).reshape(EXPERTS, CAP, 1)
    gate_act = lower_precision_back(jnp.einsum('ecd,edf->ecf', expert_in, w_gate, precision=HIGH))
    up_act = lower_precision_back(jnp.einsum('ecd,edf->ecf', expert_in, w_up, precision=HIGH))
    activated = lower_precision(jax.nn.silu(gate_act) * up_act * gate_slot)
    expert_out = jnp.einsum('ecf,efd->ecd', activated, w_down, precision=HIGH).reshape(EXPERTS * CAP, MODEL_WIDTH)
    routed_out = jnp.zeros((group_width_count + 1, MODEL_WIDTH), jnp.float32).at[owner].add(expert_out)[:group_width_count]
    return hidden + routed_out

def reference(block_input, deal_order, lengths, routes, first_gain, w_query, key_weight, value_weight, w_out, gain_two, w_router, w_gate, w_up, w_down, cotangent):
    params = tuple((weight.astype(jnp.float32) for weight in (w_query, key_weight, value_weight, w_out, first_gain, gain_two, w_router, w_gate, w_up, w_down)))
    input_rows = block_input.astype(jnp.float32).reshape(N_DP, GROUP_TOK, MODEL_WIDTH)
    pulls = cotangent.astype(jnp.float32).reshape(N_DP, GROUP_TOK, MODEL_WIDTH)
    route_groups = routes.reshape(N_DP, GROUP_TOK, TOPK)

    def one_group(totals, element):
        x_group, orders, length_row, route_rows, pull_rows = element
        outputs, backward = jax.vjp(lambda weights, rows_in: layer(weights, rows_in, orders, length_row, route_rows), params, x_group)
        d_params, d_rows = backward(pull_rows)
        totals = jax.tree.map(lambda first, second: first + second, totals, d_params)
        return (totals, (outputs, d_rows))
    starting = jax.tree.map(jnp.zeros_like, params)
    totals, (outputs, d_inputs) = lax.scan(one_group, starting, (input_rows, deal_order, lengths, route_groups, pulls))
    return (outputs.reshape(TOKENS, MODEL_WIDTH).astype(jnp.bfloat16), d_inputs.reshape(TOKENS, MODEL_WIDTH), totals[4], totals[0], totals[1], totals[2], totals[3], totals[5], totals[6], totals[7], totals[8], totals[9])
```

```python
import math

import jax
import jax.numpy as jnp
from jax import lax
from jax.sharding import PartitionSpec as P

HEAD_SIZE = 64
TOPK = 8
NORM_EPSILON = 1e-06
THETA = 10000.0
FILLER = -1e30
BF = jnp.bfloat16
F32 = jnp.float32


def dot(a, b, dims):
    return lax.dot_general(a, b, (dims, ((), ())), preferred_element_type=F32)


def nn(a, b):
    return dot(a, b, ((1,), (0,)))


def nt(a, b):
    return dot(a, b, ((1,), (1,)))


def tn(a, b):
    return dot(a, b, ((0,), (0,)))


def rope_tables(positions):
    half_head = HEAD_SIZE // 2
    frequency = THETA ** (-(2.0 / HEAD_SIZE) * jnp.arange(half_head).astype(F32))
    angles = positions.astype(F32)[:, None] * frequency[None, :]
    return (jnp.cos(angles), jnp.sin(angles))


def apply_rotation(vector, cosine_table, sine_table):
    half_head = vector.shape[-1] // 2
    first = vector[..., :half_head]
    second = vector[..., half_head:]
    cos_b = cosine_table[:, None, :]
    sin_b = sine_table[:, None, :]
    return jnp.concatenate(
        [first * cos_b - second * sin_b, second * cos_b + first * sin_b], axis=-1
    )


def places(orders, lengths):
    ends = jnp.cumsum(lengths)
    starts = ends - lengths
    inside = ((orders[:, None] >= starts[None, :]) & (orders[:, None] < ends[None, :])).astype(
        jnp.int32
    )
    seq_ids = jnp.sum(inside * jnp.arange(lengths.shape[0], dtype=jnp.int32)[None, :], axis=1)
    positions = orders - jnp.sum(inside * starts[None, :], axis=1)
    return (seq_ids, positions)


def visible_mask(o_rows, s_rows, orders, seq_ids):
    return (s_rows[:, None] == seq_ids[None, :]) & (orders[None, :] <= o_rows[:, None])


def head_scores(q_part, keys_head, visible, score_scale):
    scores = (
        jnp.einsum("bgd,nd->gbn", q_part, keys_head, preferred_element_type=F32) * score_scale
    )
    return jnp.where(visible[None], scores, FILLER)


def attend(q_rows, keys_all, values_all, visible, score_scale):
    kv_heads = keys_all.shape[1]
    per_kv = q_rows.shape[1] // kv_heads
    outputs = []
    lse_parts = []
    for kv_head in range(kv_heads):
        q_part = q_rows[:, kv_head * per_kv : (kv_head + 1) * per_kv, :]
        scores = head_scores(q_part, keys_all[:, kv_head, :], visible, score_scale)
        highest = jnp.max(scores, axis=2, keepdims=True)
        weights = jnp.exp(scores - highest)
        totals = jnp.sum(weights, axis=2, keepdims=True)
        chances = (weights / totals).astype(BF)
        outputs.append(
            jnp.einsum(
                "gbn,nd->bgd", chances, values_all[:, kv_head, :], preferred_element_type=F32
            )
        )
        lse_parts.append((highest + jnp.log(totals))[:, :, 0])
    return (jnp.concatenate(outputs, axis=1), jnp.concatenate(lse_parts, axis=0))


def attend_back(q_rows, d_rows, lse_rows, keys_all, values_all, visible, score_scale):
    kv_heads = keys_all.shape[1]
    per_kv = q_rows.shape[1] // kv_heads
    d_queries = []
    d_keys = []
    d_values = []
    for kv_head in range(kv_heads):
        q_part = q_rows[:, kv_head * per_kv : (kv_head + 1) * per_kv, :]
        d_part = d_rows[:, kv_head * per_kv : (kv_head + 1) * per_kv, :]
        scores = head_scores(q_part, keys_all[:, kv_head, :], visible, score_scale)
        probs_full = jnp.exp(scores - lse_rows[kv_head * per_kv : (kv_head + 1) * per_kv, :, None])
        chances = probs_full.astype(BF)
        d_values.append(
            jnp.einsum("gbn,bgd->nd", chances, d_part, preferred_element_type=F32)
        )
        d_chances = jnp.einsum(
            "bgd,nd->gbn", d_part, values_all[:, kv_head, :], preferred_element_type=F32
        )
        d_scores = (
            probs_full * (d_chances - jnp.sum(probs_full * d_chances, axis=2, keepdims=True))
        ).astype(BF)
        d_queries.append(
            jnp.einsum(
                "gbn,nd->bgd", d_scores, keys_all[:, kv_head, :], preferred_element_type=F32
            )
            * score_scale
        )
        d_keys.append(
            jnp.einsum("gbn,bgd->nd", d_scores, q_part, preferred_element_type=F32) * score_scale
        )
    return (
        jnp.concatenate(d_queries, axis=1),
        jnp.stack(d_keys, axis=1),
        jnp.stack(d_values, axis=1),
    )


def swap(operand, axis, bit):
    n = lax.axis_size(axis)
    return lax.ppermute(operand, axis, [(i, i ^ bit) for i in range(n)])


def col_gather(operand):
    return lax.all_gather(operand, "col", axis=0, tiled=True)


def col_scatter(operand):
    return lax.psum_scatter(operand, "col", scatter_dimension=0, tiled=True)


def row_gather(operand):
    return lax.all_gather(operand, "row", axis=0, tiled=True)


def row_scatter(operand):
    return lax.psum_scatter(operand, "row", scatter_dimension=0, tiled=True)


def pick(stack, index):
    return lax.dynamic_index_in_dim(stack, index, 0, keepdims=False)


def spread_weights(pieces, ci, nc):
    out = jnp.zeros_like(pieces)
    out = lax.dynamic_update_index_in_dim(out, pick(pieces, ci), ci, 0)
    for k in range(1, nc):
        got = swap(pick(pieces, ci ^ k), "col", k)
        out = lax.dynamic_update_index_in_dim(out, got, ci ^ k, 0)
    return out


def row_blocks(block):
    second = swap(block, "row", 2)
    both = swap(jnp.stack([block, second]), "row", 1)
    return [block, both[0], second, both[1]]


def row_sum(blocks):
    got = swap(jnp.stack([blocks[1], blocks[3]]), "row", 1)
    keep = (blocks[0].astype(F32) + got[0].astype(F32)).astype(BF)
    send = (blocks[2].astype(F32) + got[1].astype(F32)).astype(BF)
    return (keep.astype(F32) + swap(send, "row", 2).astype(F32)).astype(BF)


def dense_gates(normed, router, routes):
    experts = router.shape[1]
    logits = nn(normed, router)
    chosen = jnp.any(
        routes[:, :, None] == jnp.arange(experts, dtype=jnp.int32)[None, None, :], axis=1
    )
    top = jnp.max(jnp.where(chosen, logits, FILLER), axis=1, keepdims=True)
    weights = jnp.where(chosen, jnp.exp(jnp.where(chosen, logits - top, 0.0)), 0.0)
    return weights / jnp.sum(weights, axis=1, keepdims=True)


def expert_pass(rows_in, rows_dy, gate_cols, gate_blocks, up_blocks, down_blocks):
    local = gate_cols.shape[1]
    count = rows_in.shape[0]
    out = 0.0
    d_in = 0.0
    d_gate = 0.0
    kept = []
    for w_g, w_u, w_d in zip(gate_blocks, up_blocks, down_blocks):
        width = w_g.shape[1]
        spread = jnp.broadcast_to(gate_cols[:, :, None], (count, local, width // local)).reshape(
            count, width
        )
        g = nn(rows_in, w_g)
        u = nn(rows_in, w_u)
        d_act = nt(rows_dy, w_d)
        sig = jax.nn.sigmoid(g)
        swish = g * sig
        act = (swish * u * spread).astype(BF)
        d_gate = d_gate + jnp.sum((d_act * swish * u).reshape(count, local, -1), axis=2)
        middle = d_act * spread
        d_u = (middle * swish).astype(BF)
        d_g = (middle * u * sig * (1.0 + g * (1.0 - sig))).astype(BF)
        out = out + nn(act, w_d)
        d_in = d_in + nt(d_g, w_g) + nt(d_u, w_u)
        kept.append((act, d_g, d_u))
    return out, d_in, d_gate, kept


def body(
    block_input,
    deal_order,
    lengths,
    routes,
    first_gain,
    w_query,
    key_weight,
    value_weight,
    w_out,
    gain_two,
    w_router,
    w_gate,
    w_up,
    w_down,
    cotangent,
):
    nc, nr, ndp = lax.axis_size("col"), lax.axis_size("row"), lax.axis_size("dp")
    ci, ri, di = lax.axis_index("col"), lax.axis_index("row"), lax.axis_index("dp")
    rows, feat = block_input.shape
    width = feat * nc
    share = rows // nc
    group = rows * nr
    experts, _, hid = w_gate.shape
    halves = 2
    half = di % halves
    local = experts // (nc * halves)
    q_width = w_query.shape[1]
    kv_width = key_weight.shape[1]
    q_heads = q_width // HEAD_SIZE
    kv_heads = kv_width // HEAD_SIZE
    score_scale = 1.0 / math.sqrt(HEAD_SIZE)

    def my_half(w):
        return pick(w.reshape((halves, nc * local) + w.shape[1:]), half)

    def up_pieces(w):
        return (
            my_half(w)
            .reshape(nc, local, feat, hid)
            .transpose(0, 2, 1, 3)
            .reshape(nc, feat, local * hid)
        )

    down_pieces = my_half(w_down).reshape(nc, local * hid, feat)
    gate_full = spread_weights(up_pieces(w_gate), ci, nc).reshape(width, local * hid)
    up_full = spread_weights(up_pieces(w_up), ci, nc).reshape(width, local * hid)
    down_full = (
        spread_weights(down_pieces, ci, nc).transpose(1, 0, 2).reshape(local * hid, width)
    )
    gate_blocks = row_blocks(gate_full)
    up_blocks = row_blocks(up_full)
    down_blocks = row_blocks(down_full)

    seq_ids, positions = places(deal_order[0], lengths[0])

    def dealt(a):
        return a.reshape(nr, nc, share).transpose(1, 0, 2).reshape(nc, nr * share)

    orders_all, seq_all = dealt(deal_order[0]), dealt(seq_ids)
    cosine_table, sine_table = rope_tables(pick(dealt(positions), ci))
    visible = visible_mask(
        pick(orders_all, ci), pick(seq_all, ci), orders_all.reshape(-1), seq_all.reshape(-1)
    )

    gains = lax.all_gather(jnp.stack([first_gain, gain_two]), "col", axis=1, tiled=True).astype(F32)
    x_tok = lax.all_to_all(block_input, "col", 0, 1, tiled=True).astype(F32)
    inv_one = lax.rsqrt(jnp.mean(x_tok * x_tok, axis=1, keepdims=True) + NORM_EPSILON)
    x_hat = x_tok * inv_one
    normed = row_gather((x_hat * gains[0]).astype(BF))
    w_qkv = col_gather(jnp.concatenate([w_query, key_weight, value_weight], axis=1))
    w_tail = col_gather(jnp.concatenate([w_out.T, w_router], axis=1))
    w_out_t = w_tail[:, : w_out.shape[0]]
    router = w_tail[:, w_out.shape[0] :]

    qkv = nn(normed, w_qkv)
    count = nr * share
    queries = apply_rotation(
        qkv[:, :q_width].reshape(count, q_heads, HEAD_SIZE), cosine_table, sine_table
    ).astype(BF)
    keys = apply_rotation(
        qkv[:, q_width : q_width + kv_width].reshape(count, kv_heads, HEAD_SIZE),
        cosine_table,
        sine_table,
    ).astype(BF)
    pairs = col_gather(
        jnp.concatenate(
            [keys.reshape(count, kv_width), qkv[:, q_width + kv_width :].astype(BF)], axis=1
        )
    )
    keys_all = pairs[:, :kv_width].reshape(group, kv_heads, HEAD_SIZE)
    values_all = pairs[:, kv_width:].reshape(group, kv_heads, HEAD_SIZE)
    attn, lse = attend(queries, keys_all, values_all, visible, score_scale)
    mixed = attn.reshape(count, q_width).astype(BF)
    hidden = x_tok + row_scatter(nt(mixed, w_out_t).astype(BF)).astype(F32)
    inv_two = lax.rsqrt(jnp.mean(hidden * hidden, axis=1, keepdims=True) + NORM_EPSILON)
    hidden_hat = hidden * inv_two
    normed_two = (hidden_hat * gains[1]).astype(BF)

    rows_a = col_gather(normed_two)
    rows_b = swap(rows_a, "dp", 1)
    dy_a = lax.all_gather(cotangent, "col", axis=1, tiled=True)
    dy_b = swap(dy_a, "dp", 1)
    routes_a = lax.dynamic_slice_in_dim(routes, ri * rows, rows)
    routes_b = swap(routes_a, "dp", 1)
    first_expert = (half * nc + ci) * local

    def my_gates(tokens, chosen):
        return lax.dynamic_slice_in_dim(dense_gates(tokens, router, chosen), first_expert, local, 1)

    lanes = 128

    def both_ways(tokens, pulls, chosen):
        out, d_in, d_gate, kept = expert_pass(
            tokens, pulls, my_gates(tokens, chosen), gate_blocks, up_blocks, down_blocks
        )
        extra = lax.dynamic_update_slice_in_dim(
            jnp.zeros((rows, lanes), F32), d_gate, first_expert, 1
        )
        d_sum = col_scatter(jnp.concatenate([d_in, extra], axis=1).astype(BF))
        return out, d_sum, kept

    out_a, d_sum_a, kept_a = both_ways(rows_a, dy_a, routes_a)
    out_b, d_sum_b, kept_b = both_ways(rows_b, dy_b, routes_b)
    d_sum = d_sum_a.astype(F32) + swap(d_sum_b, "dp", 1).astype(F32)
    routed = col_scatter(
        (out_a + swap(out_b.astype(BF), "dp", 1).astype(F32)).astype(BF)
    ).astype(F32)
    output_tok = (hidden + routed).astype(BF)
    block_output = lax.all_to_all(output_tok, "col", 1, 0, tiled=True)

    def sent_back(pieces):
        mine = spread_weights(pieces, ci, nc)
        if ndp > halves:
            groups = [list(range(h, ndp, halves)) for h in range(halves)]
            mine = lax.psum(mine, "dp", axis_index_groups=groups)
        other = swap(mine, "dp", 1)
        first = jnp.where(half == 0, mine, other)
        second = jnp.where(half == 0, other, mine)
        return jnp.stack([first, second])

    def grad_blocks(index):
        made = []
        for blk in range(nr):
            made.append(
                (
                    tn(rows_a, kept_a[blk][index]) + tn(rows_b, kept_b[blk][index])
                ).astype(BF)
            )
        return row_sum(made)

    down_made = []
    for blk in range(nr):
        down_made.append((tn(kept_a[blk][0], dy_a) + tn(kept_b[blk][0], dy_b)).astype(BF))
    down_sum = row_sum(down_made).reshape(local * hid, nc, feat).transpose(1, 0, 2)
    d_w_down = sent_back(down_sum).reshape(experts, hid, feat).astype(F32)

    def up_grad(index):
        back = sent_back(grad_blocks(index).reshape(nc, feat, local * hid))
        return (
            back.reshape(halves * nc, feat, local, hid)
            .transpose(0, 2, 1, 3)
            .reshape(experts, feat, hid)
            .astype(F32)
        )

    d_w_gate = up_grad(1)
    d_w_up = up_grad(2)

    own_routes = lax.dynamic_slice_in_dim(routes_a, ci * share, share)
    gates = dense_gates(normed_two, router, own_routes)
    d_gates = d_sum[:, width : width + experts]
    d_logits = (gates * (d_gates - jnp.sum(gates * d_gates, axis=1, keepdims=True))).astype(BF)
    d_router = tn(normed_two, d_logits)
    d_normed_two = d_sum[:, :width] + nt(d_logits, router)
    dy_tok = lax.dynamic_slice_in_dim(dy_a, ci * share, share).astype(F32)
    d_hat_two = d_normed_two * gains[1]
    d_gain_two = jnp.sum(d_normed_two * hidden_hat, axis=0)
    inner_two = jnp.mean(d_hat_two * hidden_hat, axis=1, keepdims=True)
    d_hidden = dy_tok + inv_two * (d_hat_two - hidden_hat * inner_two)

    d_branch = row_gather(d_hidden.astype(BF))
    d_mixed = nn(d_branch, w_out_t).astype(BF).reshape(count, q_heads, HEAD_SIZE)
    d_w_out_t = col_scatter(tn(d_branch, mixed).astype(BF))
    d_query, d_key, d_value = attend_back(
        queries, d_mixed, lse, keys_all, values_all, visible, score_scale
    )
    kv_grads = col_scatter(
        jnp.concatenate(
            [d_key.reshape(group, kv_width), d_value.reshape(group, kv_width)], axis=1
        ).astype(BF)
    ).astype(F32)
    d_query = apply_rotation(d_query, cosine_table, -sine_table)
    d_key = apply_rotation(
        kv_grads[:, :kv_width].reshape(count, kv_heads, HEAD_SIZE), cosine_table, -sine_table
    )
    d_qkv = jnp.concatenate(
        [d_query.reshape(count, q_width), d_key.reshape(count, kv_width), kv_grads[:, kv_width:]],
        axis=1,
    ).astype(BF)
    d_normed = row_scatter(nt(d_qkv, w_qkv).astype(BF)).astype(F32)
    d_w_qkv = col_scatter(tn(normed, d_qkv).astype(BF))
    d_hat = d_normed * gains[0]
    d_gain_one = jnp.sum(d_normed * x_hat, axis=0)
    inner_one = jnp.mean(d_hat * x_hat, axis=1, keepdims=True)
    d_input_tok = d_hidden + inv_one * (d_hat - x_hat * inner_one)
    d_input = lax.all_to_all(d_input_tok.astype(BF), "col", 1, 0, tiled=True).astype(F32)

    d_attn = lax.psum(jnp.concatenate([d_w_qkv, d_w_out_t], axis=1), "dp").astype(F32)
    d_w_qkv, d_w_out_t = d_attn[:, : q_width + 2 * kv_width], d_attn[:, q_width + 2 * kv_width :]
    small = jnp.concatenate([d_router, d_gain_two[:, None], d_gain_one[:, None]], axis=1)
    small = lax.psum(col_scatter(small), ("dp", "row"))
    return (
        block_output,
        d_input,
        small[:, experts + 1],
        d_w_qkv[:, :q_width],
        d_w_qkv[:, q_width : q_width + kv_width],
        d_w_qkv[:, q_width + kv_width :],
        d_w_out_t.T,
        small[:, experts],
        small[:, :experts],
        d_w_gate,
        d_w_up,
        d_w_down,
    )


def solution(mesh):
    residual = P(("dp", "row"), "col")
    return jax.shard_map(
        body,
        mesh=mesh,
        in_specs=(
            residual,
            P("dp", None),
            P("dp", None),
            P("dp", None),
            P("col"),
            P("col", "row"),
            P("col", "row"),
            P("col", "row"),
            P("row", "col"),
            P("col"),
            P("col", None),
            P(None, "col", "row"),
            P(None, "col", "row"),
            P(None, "row", "col"),
            residual,
        ),
        out_specs=(
            residual,
            residual,
            P("col"),
            P("col", "row"),
            P("col", "row"),
            P("col", "row"),
            P("row", "col"),
            P("col"),
            P("col", None),
            P(None, "col", "row"),
            P(None, "col", "row"),
            P(None, "row", "col"),
        ),
        check_vma=False,
    )
```

```python
import functools
import math

import jax
import jax.numpy as jnp
from jax import lax
from jax.experimental import pallas as pl
from jax.experimental.pallas import tpu as pltpu
from jax.sharding import PartitionSpec as P

HEAD_SIZE = 64
TOPK = 8
NORM_EPSILON = 1e-06
THETA = 10000.0
FILLER = -1e30
BF = jnp.bfloat16
F32 = jnp.float32


def dot(a, b, dims):
    return lax.dot_general(a, b, (dims, ((), ())), preferred_element_type=F32)


def nn(a, b):
    return dot(a, b, ((1,), (0,)))


def nt(a, b):
    return dot(a, b, ((1,), (1,)))


def tn(a, b):
    return dot(a, b, ((0,), (0,)))


def rope_tables(positions):
    half_head = HEAD_SIZE // 2
    frequency = THETA ** (-(2.0 / HEAD_SIZE) * jnp.arange(half_head).astype(F32))
    angles = positions.astype(F32)[:, None] * frequency[None, :]
    return (jnp.cos(angles), jnp.sin(angles))


def apply_rotation(vector, cosine_table, sine_table):
    half_head = vector.shape[-1] // 2
    first = vector[..., :half_head]
    second = vector[..., half_head:]
    cos_b = cosine_table[:, None, :]
    sin_b = sine_table[:, None, :]
    return jnp.concatenate(
        [first * cos_b - second * sin_b, second * cos_b + first * sin_b], axis=-1
    )


def places(orders, lengths):
    ends = jnp.cumsum(lengths)
    starts = ends - lengths
    inside = ((orders[:, None] >= starts[None, :]) & (orders[:, None] < ends[None, :])).astype(
        jnp.int32
    )
    seq_ids = jnp.sum(inside * jnp.arange(lengths.shape[0], dtype=jnp.int32)[None, :], axis=1)
    positions = orders - jnp.sum(inside * starts[None, :], axis=1)
    return (seq_ids, positions)


def visible_mask(o_rows, s_rows, orders, seq_ids):
    return (s_rows[:, None] == seq_ids[None, :]) & (orders[None, :] <= o_rows[:, None])


def head_scores(q_part, keys_head, visible, score_scale):
    scores = (
        jnp.einsum("bgd,nd->gbn", q_part, keys_head, preferred_element_type=F32) * score_scale
    )
    return jnp.where(visible[None], scores, FILLER)


def attend(q_rows, keys_all, values_all, visible, score_scale):
    kv_heads = keys_all.shape[1]
    per_kv = q_rows.shape[1] // kv_heads
    outputs = []
    lse_parts = []
    for kv_head in range(kv_heads):
        q_part = q_rows[:, kv_head * per_kv : (kv_head + 1) * per_kv, :]
        scores = head_scores(q_part, keys_all[:, kv_head, :], visible, score_scale)
        highest = jnp.max(scores, axis=2, keepdims=True)
        weights = jnp.exp(scores - highest)
        totals = jnp.sum(weights, axis=2, keepdims=True)
        chances = (weights / totals).astype(BF)
        outputs.append(
            jnp.einsum(
                "gbn,nd->bgd", chances, values_all[:, kv_head, :], preferred_element_type=F32
            )
        )
        lse_parts.append((highest + jnp.log(totals))[:, :, 0])
    return (jnp.concatenate(outputs, axis=1), jnp.concatenate(lse_parts, axis=0))


def attend_back(q_rows, d_rows, lse_rows, keys_all, values_all, visible, score_scale):
    kv_heads = keys_all.shape[1]
    per_kv = q_rows.shape[1] // kv_heads
    d_queries = []
    d_keys = []
    d_values = []
    for kv_head in range(kv_heads):
        q_part = q_rows[:, kv_head * per_kv : (kv_head + 1) * per_kv, :]
        d_part = d_rows[:, kv_head * per_kv : (kv_head + 1) * per_kv, :]
        scores = head_scores(q_part, keys_all[:, kv_head, :], visible, score_scale)
        probs_full = jnp.exp(scores - lse_rows[kv_head * per_kv : (kv_head + 1) * per_kv, :, None])
        chances = probs_full.astype(BF)
        d_values.append(
            jnp.einsum("gbn,bgd->nd", chances, d_part, preferred_element_type=F32)
        )
        d_chances = jnp.einsum(
            "bgd,nd->gbn", d_part, values_all[:, kv_head, :], preferred_element_type=F32
        )
        d_scores = (
            probs_full * (d_chances - jnp.sum(probs_full * d_chances, axis=2, keepdims=True))
        ).astype(BF)
        d_queries.append(
            jnp.einsum(
                "gbn,nd->bgd", d_scores, keys_all[:, kv_head, :], preferred_element_type=F32
            )
            * score_scale
        )
        d_keys.append(
            jnp.einsum("gbn,bgd->nd", d_scores, q_part, preferred_element_type=F32) * score_scale
        )
    return (
        jnp.concatenate(d_queries, axis=1),
        jnp.stack(d_keys, axis=1),
        jnp.stack(d_values, axis=1),
    )


def swap(operand, axis, bit):
    n = lax.axis_size(axis)
    return lax.ppermute(operand, axis, [(i, i ^ bit) for i in range(n)])


def col_gather(operand):
    return lax.all_gather(operand, "col", axis=0, tiled=True)


def col_scatter(operand):
    return lax.psum_scatter(operand, "col", scatter_dimension=0, tiled=True)


def row_gather(operand):
    return lax.all_gather(operand, "row", axis=0, tiled=True)


def row_scatter(operand):
    return lax.psum_scatter(operand, "row", scatter_dimension=0, tiled=True)


def pick(stack, index):
    return lax.dynamic_index_in_dim(stack, index, 0, keepdims=False)


def spread_weights(pieces, ci, nc):
    out = jnp.zeros_like(pieces)
    out = lax.dynamic_update_index_in_dim(out, pick(pieces, ci), ci, 0)
    for k in range(1, nc):
        got = swap(pick(pieces, ci ^ k), "col", k)
        out = lax.dynamic_update_index_in_dim(out, got, ci ^ k, 0)
    return out


def row_blocks(block):
    second = swap(block, "row", 2)
    return [block, swap(block, "row", 1), second, swap(second, "row", 1)]


def add_low(first, second):
    return (first.astype(F32) + second.astype(F32)).astype(BF)


def row_sum(blocks):
    send = add_low(blocks[2], swap(blocks[3], "row", 1))
    keep = add_low(blocks[0], swap(blocks[1], "row", 1))
    return add_low(keep, swap(send, "row", 2))


def dp_sum(operand):
    if lax.axis_size("dp") == 2:
        return operand.astype(F32) + swap(operand, "dp", 1).astype(F32)
    return lax.psum(operand, "dp").astype(F32)


def dense_gates(normed, router, routes):
    experts = router.shape[1]
    logits = nn(normed, router)
    chosen = jnp.any(
        routes[:, :, None] == jnp.arange(experts, dtype=jnp.int32)[None, None, :], axis=1
    )
    top = jnp.max(jnp.where(chosen, logits, FILLER), axis=1, keepdims=True)
    weights = jnp.where(chosen, jnp.exp(jnp.where(chosen, logits - top, 0.0)), 0.0)
    return weights / jnp.sum(weights, axis=1, keepdims=True)


def expert_kernel(nb, tile, xa_ref, xb_ref, dya_ref, dyb_ref, gate_ref, mark_ref, *refs):
    wg, wu, wd = refs[:nb], refs[nb : 2 * nb], refs[2 * nb : 3 * nb]
    outs, dxs = refs[3 * nb : 3 * nb + 2], refs[3 * nb + 2 : 3 * nb + 4]
    made_refs = refs[3 * nb + 4 : 6 * nb + 4]
    dwg, dwu, dwd = made_refs[:nb], made_refs[nb : 2 * nb], made_refs[2 * nb :]
    w_in, w_out, xt, acc_out, acc_dx, act_s, dgu_s = refs[6 * nb + 4 :]
    nc, _, feat, hid = wg[0].shape
    wide = nb * hid
    width = nc * feat
    e = pl.program_id(0)
    rows = xa_ref.shape[0]
    for j in range(nb):
        for c in range(nc):
            w_in[c * feat : (c + 1) * feat, j * hid : (j + 1) * hid] = wg[j][c, 0]
            w_in[c * feat : (c + 1) * feat, wide + j * hid : wide + (j + 1) * hid] = wu[j][c, 0]
            w_out[j * hid : (j + 1) * hid, c * feat : (c + 1) * feat] = wd[j][c, 0]

    @pl.when(e == 0)
    def _():
        acc_out[...] = jnp.zeros_like(acc_out)
        acc_dx[...] = jnp.zeros_like(acc_dx)
        for h, ref in enumerate((xa_ref, xb_ref)):
            for c in range(nc):
                xt[c * feat : (c + 1) * feat, h * rows : (h + 1) * rows] = ref[
                    :, c * feat : (c + 1) * feat
                ].T

    mark = mark_ref[pl.ds(e, 1), :]
    for h, (x_ref, dy_ref) in enumerate(((xa_ref, dya_ref), (xb_ref, dyb_ref))):

        @pl.loop(0, rows // tile)
        def _(t):
            at = pl.ds(pl.multiple_of(t * tile, tile), tile)
            here = pl.ds(pl.multiple_of(h * rows + t * tile, tile), tile)
            gu = nn(x_ref[at, :], w_in[...])
            d_act = nt(dy_ref[at, :], w_out[...])
            gate = jnp.sum(gate_ref[here, :] * mark, axis=1, keepdims=True)
            spread = jnp.broadcast_to(gate, (tile, hid))
            total = None
            for j in range(nb):
                lo = j * hid
                g = gu[:, lo : lo + hid]
                u = gu[:, wide + lo : wide + lo + hid]
                da = d_act[:, lo : lo + hid]
                sig = 1.0 / (1.0 + jnp.exp(-g))
                swish = g * sig
                su = swish * u
                act_s[here, lo : lo + hid] = (su * spread).astype(BF)
                part = da * su
                total = part if total is None else total + part
                mid = da * spread
                dgu_s[here, lo : lo + hid] = (mid * u * (sig * (1.0 + g * (1.0 - sig)))).astype(BF)
                dgu_s[here, wide + lo : wide + lo + hid] = (mid * swish).astype(BF)
            acc_dx[here, width:] += jnp.sum(total, axis=1, keepdims=True) * mark
            acc_out[here, :] += nn(act_s[here, :], w_out[...])
            acc_dx[here, :width] += nt(dgu_s[here, :], w_in[...])

    @pl.loop(0, nc)
    def _(c):
        at = pl.ds(pl.multiple_of(c * feat, feat), feat)
        made = nn(xt[at, :], dgu_s[...])
        for j in range(nb):
            dwg[j][0, at, :] = made[:, j * hid : (j + 1) * hid].astype(BF)
            dwu[j][0, at, :] = made[:, wide + j * hid : wide + (j + 1) * hid].astype(BF)

    for j in range(nb):
        cut = slice(j * hid, (j + 1) * hid)
        dwd[j][0] = (tn(act_s[:rows, cut], dya_ref[...]) + tn(act_s[rows:, cut], dyb_ref[...])).astype(BF)

    @pl.when(e == pl.num_programs(0) - 1)
    def _():
        for h in range(2):
            outs[h][...] = acc_out[h * rows : (h + 1) * rows, :].astype(BF)
            dxs[h][...] = acc_dx[h * rows : (h + 1) * rows, :].astype(BF)


def expert_pass(x_a, x_b, dy_a, dy_b, gates, marks, wg, wu, wd):
    rows, width = x_a.shape
    nb = len(wg)
    nc, local, feat, hid = wg[0].shape
    wide = nb * hid
    lanes = marks.shape[1]

    def whole(shape):
        return pl.BlockSpec(shape, lambda e: (0,) * len(shape), pipeline_mode=pl.Buffered(1))

    up_spec = pl.BlockSpec((nc, 1, feat, hid), lambda e: (0, e, 0, 0))
    down_spec = pl.BlockSpec((nc, 1, hid, feat), lambda e: (0, e, 0, 0))
    made = pl.pallas_call(
        functools.partial(expert_kernel, nb, min(256, rows)),
        grid=(local,),
        in_specs=[whole(x_a.shape)] * 4
        + [whole(gates.shape), whole(marks.shape)]
        + [up_spec] * (2 * nb)
        + [down_spec] * nb,
        out_specs=[whole((rows, width))] * 2
        + [whole((rows, width + lanes))] * 2
        + [pl.BlockSpec((1, width, hid), lambda e: (e, 0, 0))] * (2 * nb)
        + [pl.BlockSpec((1, hid, width), lambda e: (e, 0, 0))] * nb,
        out_shape=[jax.ShapeDtypeStruct((rows, width), BF)] * 2
        + [jax.ShapeDtypeStruct((rows, width + lanes), BF)] * 2
        + [jax.ShapeDtypeStruct((local, width, hid), BF)] * (2 * nb)
        + [jax.ShapeDtypeStruct((local, hid, width), BF)] * nb,
        scratch_shapes=[
            pltpu.VMEM((width, 2 * wide), BF),
            pltpu.VMEM((wide, width), BF),
            pltpu.VMEM((width, 2 * rows), BF),
            pltpu.VMEM((2 * rows, width), F32),
            pltpu.VMEM((2 * rows, width + lanes), F32),
            pltpu.VMEM((2 * rows, wide), BF),
            pltpu.VMEM((2 * rows, 2 * wide), BF),
        ],
        compiler_params=pltpu.CompilerParams(vmem_limit_bytes=60 * 2**20),
        cost_estimate=pl.CostEstimate(
            flops=36 * rows * width * wide * local,
            bytes_accessed=12 * nb * local * width * hid,
            transcendentals=2 * rows * wide * local,
        ),
    )(x_a, x_b, dy_a, dy_b, gates, marks, *wg, *wu, *wd)
    made = list(made)
    return made[0:2], made[2:4], made[4 : 4 + nb], made[4 + nb : 4 + 2 * nb], made[4 + 2 * nb :]


def body(
    block_input,
    deal_order,
    lengths,
    routes,
    first_gain,
    w_query,
    key_weight,
    value_weight,
    w_out,
    gain_two,
    w_router,
    w_gate,
    w_up,
    w_down,
    cotangent,
):
    nc, nr, ndp = lax.axis_size("col"), lax.axis_size("row"), lax.axis_size("dp")
    ci, ri, di = lax.axis_index("col"), lax.axis_index("row"), lax.axis_index("dp")
    rows, feat = block_input.shape
    width = feat * nc
    share = rows // nc
    group = rows * nr
    experts, _, hid = w_gate.shape
    halves = 2
    half = di % halves
    local = experts // (nc * halves)
    q_width = w_query.shape[1]
    kv_width = key_weight.shape[1]
    q_heads = q_width // HEAD_SIZE
    kv_heads = kv_width // HEAD_SIZE
    score_scale = 1.0 / math.sqrt(HEAD_SIZE)

    seq_ids, positions = places(deal_order[0], lengths[0])

    def dealt(a):
        return a.reshape(nr, nc, share).transpose(1, 0, 2).reshape(nc, nr * share)

    orders_all, seq_all = dealt(deal_order[0]), dealt(seq_ids)
    cosine_table, sine_table = rope_tables(pick(dealt(positions), ci))
    visible = visible_mask(
        pick(orders_all, ci), pick(seq_all, ci), orders_all.reshape(-1), seq_all.reshape(-1)
    )

    ride = 16
    gain_rows = jnp.concatenate(
        [jnp.stack([first_gain, gain_two]), jnp.zeros((ride - 2, feat), BF)], axis=0
    )
    sent = jnp.concatenate(
        [
            block_input.reshape(nc, share, feat),
            jnp.broadcast_to(gain_rows[None], (nc, ride, feat)),
        ],
        axis=1,
    ).reshape(nc * (share + ride), feat)
    got = lax.all_to_all(sent, "col", 0, 1, tiled=True).astype(F32)
    x_tok, gains = got[:share], got[share : share + 2]
    inv_one = lax.rsqrt(jnp.mean(x_tok * x_tok, axis=1, keepdims=True) + NORM_EPSILON)
    x_hat = x_tok * inv_one
    normed = row_gather((x_hat * gains[0]).astype(BF))
    w_qkv = col_gather(jnp.concatenate([w_query, key_weight, value_weight], axis=1))
    w_qkv, w_gate_later = lax.optimization_barrier((w_qkv, w_gate))

    def spread(w):
        pieces = pick(w.reshape((halves, nc, local) + w.shape[1:]), half)
        return row_blocks(spread_weights(pieces, ci, nc))

    gate_blocks = spread(w_gate_later)
    w_tail = col_gather(jnp.concatenate([w_out.T, w_router], axis=1))
    w_out_t = w_tail[:, : w_out.shape[0]]
    router = w_tail[:, w_out.shape[0] :]

    qkv = nn(normed, w_qkv)
    count = nr * share
    queries = apply_rotation(
        qkv[:, :q_width].reshape(count, q_heads, HEAD_SIZE), cosine_table, sine_table
    ).astype(BF)
    keys = apply_rotation(
        qkv[:, q_width : q_width + kv_width].reshape(count, kv_heads, HEAD_SIZE),
        cosine_table,
        sine_table,
    ).astype(BF)
    pairs = col_gather(
        jnp.concatenate(
            [keys.reshape(count, kv_width), qkv[:, q_width + kv_width :].astype(BF)], axis=1
        )
    )
    pairs, w_up_later, w_down_later = lax.optimization_barrier((pairs, w_up, w_down))
    up_blocks = spread(w_up_later)
    down_blocks = spread(w_down_later)
    keys_all = pairs[:, :kv_width].reshape(group, kv_heads, HEAD_SIZE)
    values_all = pairs[:, kv_width:].reshape(group, kv_heads, HEAD_SIZE)
    attn, lse = attend(queries, keys_all, values_all, visible, score_scale)
    mixed = attn.reshape(count, q_width).astype(BF)
    hidden = x_tok + row_scatter(nt(mixed, w_out_t).astype(BF)).astype(F32)
    inv_two = lax.rsqrt(jnp.mean(hidden * hidden, axis=1, keepdims=True) + NORM_EPSILON)
    hidden_hat = hidden * inv_two
    normed_two = (hidden_hat * gains[1]).astype(BF)

    rows_a = col_gather(normed_two)
    rows_b = swap(rows_a, "dp", 1)
    dy_a = lax.all_gather(cotangent, "col", axis=1, tiled=True)
    dy_b = swap(dy_a, "dp", 1)
    routes_a = lax.dynamic_slice_in_dim(routes, ri * rows, rows)
    routes_b = swap(routes_a, "dp", 1)
    first_expert = (half * nc + ci) * local

    lanes = 128

    def padded_gates(tokens, chosen):
        return jnp.pad(dense_gates(tokens, router, chosen), ((0, 0), (0, lanes - experts)))

    gate_rows = jnp.concatenate([padded_gates(rows_a, routes_a), padded_gates(rows_b, routes_b)])
    marks = (
        jnp.arange(lanes, dtype=jnp.int32)[None, :]
        == first_expert + jnp.arange(local, dtype=jnp.int32)[:, None]
    ).astype(F32)
    outs, d_ins, d_gate_w, d_up_w, d_down_w = expert_pass(
        rows_a, rows_b, dy_a, dy_b, gate_rows, marks, gate_blocks, up_blocks, down_blocks
    )
    d_sum = col_scatter(add_low(d_ins[0], swap(d_ins[1], "dp", 1))).astype(F32)
    routed = col_scatter(add_low(outs[0], swap(outs[1], "dp", 1))).astype(F32)
    output_tok = (hidden + routed).astype(BF)
    block_output = lax.all_to_all(output_tok, "col", 1, 0, tiled=True)

    def sent_back(pieces):
        mine = spread_weights(pieces, ci, nc)
        if ndp > halves:
            groups = [list(range(h, ndp, halves)) for h in range(halves)]
            mine = lax.psum(mine, "dp", axis_index_groups=groups)
        other = swap(mine, "dp", 1)
        first = jnp.where(half == 0, mine, other)
        second = jnp.where(half == 0, other, mine)
        return jnp.stack([first, second]).astype(F32)

    def up_grad(blocks):
        total = row_sum(blocks).reshape(local, nc, feat, hid).transpose(1, 0, 2, 3)
        return sent_back(total).reshape(experts, feat, hid)

    d_w_down = sent_back(
        row_sum(d_down_w).reshape(local, hid, nc, feat).transpose(2, 0, 1, 3)
    ).reshape(experts, hid, feat)
    d_w_gate = up_grad(d_gate_w)
    d_w_up = up_grad(d_up_w)

    own_routes = lax.dynamic_slice_in_dim(routes_a, ci * share, share)
    gates = dense_gates(normed_two, router, own_routes)
    d_gates = d_sum[:, width : width + experts]
    d_logits = (gates * (d_gates - jnp.sum(gates * d_gates, axis=1, keepdims=True))).astype(BF)
    d_router = tn(normed_two, d_logits)
    d_normed_two = d_sum[:, :width] + nt(d_logits, router)
    dy_tok = lax.dynamic_slice_in_dim(dy_a, ci * share, share).astype(F32)
    d_hat_two = d_normed_two * gains[1]
    d_gain_two = jnp.sum(d_normed_two * hidden_hat, axis=0)
    inner_two = jnp.mean(d_hat_two * hidden_hat, axis=1, keepdims=True)
    d_hidden = dy_tok + inv_two * (d_hat_two - hidden_hat * inner_two)

    d_branch = row_gather(d_hidden.astype(BF))
    d_mixed = nn(d_branch, w_out_t).astype(BF).reshape(count, q_heads, HEAD_SIZE)
    d_w_out_t = col_scatter(tn(d_branch, mixed).astype(BF))
    d_query, d_key, d_value = attend_back(
        queries, d_mixed, lse, keys_all, values_all, visible, score_scale
    )
    kv_grads = col_scatter(
        jnp.concatenate(
            [d_key.reshape(group, kv_width), d_value.reshape(group, kv_width)], axis=1
        ).astype(BF)
    ).astype(F32)
    d_query = apply_rotation(d_query, cosine_table, -sine_table)
    d_key = apply_rotation(
        kv_grads[:, :kv_width].reshape(count, kv_heads, HEAD_SIZE), cosine_table, -sine_table
    )
    d_qkv = jnp.concatenate(
        [d_query.reshape(count, q_width), d_key.reshape(count, kv_width), kv_grads[:, kv_width:]],
        axis=1,
    ).astype(BF)
    d_normed = row_scatter(nt(d_qkv, w_qkv).astype(BF)).astype(F32)
    d_w_qkv = col_scatter(tn(normed, d_qkv).astype(BF))
    d_hat = d_normed * gains[0]
    d_gain_one = jnp.sum(d_normed * x_hat, axis=0)
    inner_one = jnp.mean(d_hat * x_hat, axis=1, keepdims=True)
    d_input_tok = d_hidden + inv_one * (d_hat - x_hat * inner_one)
    d_input = lax.all_to_all(d_input_tok.astype(BF), "col", 1, 0, tiled=True).astype(F32)

    d_w_qkv = dp_sum(d_w_qkv)
    d_w_out = dp_sum(d_w_out_t).T
    small = jnp.concatenate([d_router, d_gain_two[:, None]], axis=1)
    small = lax.psum(col_scatter(small), ("dp", "row"))
    d_gain_one = lax.psum(col_scatter(d_gain_one), ("dp", "row"))
    return (
        block_output,
        d_input,
        d_gain_one,
        d_w_qkv[:, :q_width],
        d_w_qkv[:, q_width : q_width + kv_width],
        d_w_qkv[:, q_width + kv_width :],
        d_w_out,
        small[:, experts],
        small[:, :experts],
        d_w_gate,
        d_w_up,
        d_w_down,
    )


def solution(mesh):
    residual = P(("dp", "row"), "col")
    return jax.shard_map(
        body,
        mesh=mesh,
        in_specs=(
            residual,
            P("dp", None),
            P("dp", None),
            P("dp", None),
            P("col"),
            P("col", "row"),
            P("col", "row"),
            P("col", "row"),
            P("row", "col"),
            P("col"),
            P("col", None),
            P(None, "col", "row"),
            P(None, "col", "row"),
            P(None, "row", "col"),
            residual,
        ),
        out_specs=(
            residual,
            residual,
            P("col"),
            P("col", "row"),
            P("col", "row"),
            P("col", "row"),
            P("row", "col"),
            P("col"),
            P("col", None),
            P(None, "col", "row"),
            P(None, "col", "row"),
            P(None, "row", "col"),
        ),
        check_vma=False,
    )
```

```python
import functools
import math

import jax
import jax.numpy as jnp
from jax import lax
from jax.experimental import pallas as pl
from jax.experimental.pallas import tpu as pltpu
from jax.sharding import PartitionSpec as P

HEAD_SIZE = 64
TOPK = 8
NORM_EPSILON = 1e-06
THETA = 10000.0
FILLER = -1e30
BF = jnp.bfloat16
F32 = jnp.float32


def dot(a, b, dims):
    return lax.dot_general(a, b, (dims, ((), ())), preferred_element_type=F32)


def nn(a, b):
    return dot(a, b, ((1,), (0,)))


def nt(a, b):
    return dot(a, b, ((1,), (1,)))


def tn(a, b):
    return dot(a, b, ((0,), (0,)))


def rope_tables(positions):
    half_head = HEAD_SIZE // 2
    frequency = THETA ** (-(2.0 / HEAD_SIZE) * jnp.arange(half_head).astype(F32))
    angles = positions.astype(F32)[None, :] * frequency[:, None]
    return (jnp.cos(angles), jnp.sin(angles))


def rotate(vector, cosine_table, sine_table):
    half_head = HEAD_SIZE // 2
    parts = vector.reshape(-1, HEAD_SIZE, vector.shape[1])
    first, second = parts[:, :half_head], parts[:, half_head:]
    return jnp.concatenate(
        [
            first * cosine_table - second * sine_table,
            second * cosine_table + first * sine_table,
        ],
        axis=1,
    ).reshape(vector.shape)


def places(orders, lengths):
    ends = jnp.cumsum(lengths)
    starts = ends - lengths
    inside = ((orders[:, None] >= starts[None, :]) & (orders[:, None] < ends[None, :])).astype(
        jnp.int32
    )
    seq_ids = jnp.sum(inside * jnp.arange(lengths.shape[0], dtype=jnp.int32)[None, :], axis=1)
    positions = orders - jnp.sum(inside * starts[None, :], axis=1)
    return (seq_ids, positions)


def bias_into(bias, key_ref, row_ref, start_ref, chunk):
    @pl.loop(0, bias.shape[0] // chunk)
    def _(c):
        at = pl.ds(pl.multiple_of(c * chunk, chunk), chunk)
        keys = key_ref[at, :]
        seen = (keys <= row_ref[...]) & (keys >= start_ref[...])
        bias[at, :] = jnp.where(seen, 0.0, FILLER)


def attend_kernel(tile, kv_heads, q_ref, kv_ref, key_ref, row_ref, start_ref, o_ref, lse_ref, bias, k_s):
    size = HEAD_SIZE
    heads = q_ref.shape[0] // size
    per = heads // kv_heads
    rows = q_ref.shape[1]
    bias_into(bias, key_ref, row_ref, start_ref, 256)
    for g in range(kv_heads):
        k_s[g] = kv_ref[g * size : (g + 1) * size, :].T

    @pl.loop(0, heads)
    def _(h):
        g = h // per
        at = pl.ds(pl.multiple_of(h * size, size), size)
        v_at = pl.ds(pl.multiple_of((kv_heads + g) * size, size), size)
        for t in range(rows // tile):
            cut = slice(t * tile, (t + 1) * tile)
            scores = nn(k_s[g], q_ref[at, cut]) + bias[:, cut]
            top = jnp.max(scores, axis=0, keepdims=True)
            weights = jnp.exp(scores - top)
            total = jnp.sum(weights, axis=0, keepdims=True)
            chances = (weights * (1.0 / total)).astype(BF)
            o_ref[at, cut] = nn(kv_ref[v_at, :], chances).astype(BF)
            lse_ref[h, :, cut] = top + jnp.log(total)


def attend(q, kv, keys, rows_at, starts, kv_heads):
    heads, count = q.shape[0] // HEAD_SIZE, q.shape[1]
    group = kv.shape[1]
    return pl.pallas_call(
        functools.partial(attend_kernel, min(256, count), kv_heads),
        out_shape=[
            jax.ShapeDtypeStruct(q.shape, BF),
            jax.ShapeDtypeStruct((heads, 1, count), F32),
        ],
        scratch_shapes=[
            pltpu.VMEM((group, count), F32),
            pltpu.VMEM((kv_heads, group, HEAD_SIZE), BF),
        ],
        compiler_params=pltpu.CompilerParams(vmem_limit_bytes=48 * 2**20),
        cost_estimate=pl.CostEstimate(flops=1024, bytes_accessed=1024, transcendentals=0),
    )(q, kv, keys, rows_at, starts)


def attend_back_kernel(
    tile, kv_heads, q_ref, do_ref, lse_ref, kv_ref, key_ref, row_ref, start_ref, dq_ref, dkv_ref,
    bias, k_s, v_s, dk_s, dv_s,
):
    size = HEAD_SIZE
    heads = q_ref.shape[0] // size
    per = heads // kv_heads
    rows = q_ref.shape[1]
    bias_into(bias, key_ref, row_ref, start_ref, 256)
    for g in range(kv_heads):
        k_s[g] = kv_ref[g * size : (g + 1) * size, :].T
        v_s[g] = kv_ref[(kv_heads + g) * size : (kv_heads + g + 1) * size, :].T
    dk_s[...] = jnp.zeros_like(dk_s)
    dv_s[...] = jnp.zeros_like(dv_s)

    @pl.loop(0, heads)
    def _(h):
        g = h // per
        at = pl.ds(pl.multiple_of(h * size, size), size)
        k_at = pl.ds(pl.multiple_of(g * size, size), size)
        for t in range(rows // tile):
            cut = slice(t * tile, (t + 1) * tile)
            q_part, do_part = q_ref[at, cut], do_ref[at, cut]
            scores = nn(k_s[g], q_part) + bias[:, cut]
            probs = jnp.exp(scores - lse_ref[h, :, cut])
            d_chances = nn(v_s[g], do_part)
            dv_s[g] += nt(probs.astype(BF), do_part)
            both = probs * d_chances
            d_scores = (both - probs * jnp.sum(both, axis=0, keepdims=True)).astype(BF)
            dk_s[g] += nt(d_scores, q_part)
            dq_ref[at, cut] = nn(kv_ref[k_at, :], d_scores)

    for g in range(kv_heads):
        dkv_ref[g * size : (g + 1) * size, :] = dk_s[g].T.astype(BF)
        dkv_ref[(kv_heads + g) * size : (kv_heads + g + 1) * size, :] = dv_s[g].T.astype(BF)


def attend_back(q, do, lse, kv, keys, rows_at, starts, kv_heads):
    count = q.shape[1]
    group = kv.shape[1]
    return pl.pallas_call(
        functools.partial(attend_back_kernel, min(256, count), kv_heads),
        out_shape=[jax.ShapeDtypeStruct(q.shape, F32), jax.ShapeDtypeStruct(kv.shape, BF)],
        scratch_shapes=[
            pltpu.VMEM((group, count), F32),
            pltpu.VMEM((kv_heads, group, HEAD_SIZE), BF),
            pltpu.VMEM((kv_heads, group, HEAD_SIZE), BF),
            pltpu.VMEM((kv_heads, group, HEAD_SIZE), F32),
            pltpu.VMEM((kv_heads, group, HEAD_SIZE), F32),
        ],
        compiler_params=pltpu.CompilerParams(vmem_limit_bytes=56 * 2**20),
        cost_estimate=pl.CostEstimate(flops=1024, bytes_accessed=1024, transcendentals=0),
    )(q, do, lse, kv, keys, rows_at, starts)


def swap(operand, axis, bit):
    n = lax.axis_size(axis)
    return lax.ppermute(operand, axis, [(i, i ^ bit) for i in range(n)])


MESH_ID = pl.DeviceIdType.MESH


def cut(ref, how, index, size):
    if how == "all":
        return ref
    if how == "major":
        return ref.at[index]
    return ref.at[:, pl.ds(pl.multiple_of(index * size, 128), size)]


def greet(peers):
    barrier = pltpu.get_barrier_semaphore()
    for peer in peers:
        pl.semaphore_signal(barrier, inc=1, device_id=peer, device_id_type=MESH_ID)
    pl.semaphore_wait(barrier, len(peers))


WORLD = ("dp", "row", "col")


def size_of(axis):
    return lax.axis_size(WORLD) if axis == "world" else lax.axis_size(axis)


def place_of(axis):
    return lax.axis_index(WORLD) if axis == "world" else lax.axis_index(axis)


def at_place(axis, index):
    if axis != "world":
        return {axis: index}
    nr, nc = lax.axis_size("row"), lax.axis_size("col")
    return {"dp": index // (nr * nc), "row": index // nc % nr, "col": index % nc}


def exchange_kernel(plans, sizes, *refs):
    count = len(plans)
    ins, outs = refs[:count], refs[count : 2 * count]
    send_sem, recv_sem, near_sem = refs[2 * count :]
    me = {axis: place_of(axis) for axis in sizes}
    axes = ["world"] if "world" in sizes else list(sizes)
    greet([at_place(axis, me[axis] ^ k) for axis in axes for k in range(1, sizes[axis])])
    near, far, later, passed, seen = [], [], [], [], []
    slot = 0
    for which, (axis, src, dst) in enumerate(plans):
        x, out, n, i = ins[which], outs[which], sizes[axis], me[axis]
        in_size = x.shape[-1] // n
        out_size = out.shape[-1] // n
        two_step = axis == "row" and src == "all" and n == 4
        own = i
        copy = pltpu.make_async_copy(
            cut(x, src, own, in_size), cut(out, dst, own, out_size), near_sem.at[which]
        )
        copy.start()
        near.append(copy)
        for k in range(1, n):
            if two_step and k == 3:
                seen.append(far.pop())
                later.append((out, i, slot, seen[-1]))
                slot += 1
                continue
            copy = pltpu.make_async_remote_copy(
                src_ref=cut(x, src, i ^ k, in_size),
                dst_ref=cut(out, dst, i, out_size),
                send_sem=send_sem.at[slot],
                recv_sem=recv_sem.at[slot],
                device_id=at_place(axis, i ^ k),
                device_id_type=MESH_ID,
            )
            copy.start()
            slot += 1
            far.append(copy)
    for out, i, at, second in later:
        second.wait_recv()
        copy = pltpu.make_async_remote_copy(
            src_ref=out.at[i ^ 2],
            dst_ref=out.at[i ^ 2],
            send_sem=send_sem.at[at],
            recv_sem=recv_sem.at[at],
            device_id={"row": i ^ 1},
            device_id_type=MESH_ID,
        )
        copy.start()
        passed.append(copy)
    for copy in near + far + passed:
        copy.wait()
    for copy in seen:
        copy.wait_send()


def exchange(number, *moves):
    plans, shapes, sizes = [], [], {}
    for operand, axis, src, dst in moves:
        n = size_of(axis)
        sizes[axis] = n
        shape = operand.shape
        if src == "major":
            shape = shape[1:]
        elif src == "lane":
            shape = shape[:-1] + (shape[-1] // n,)
        if dst == "major":
            shape = (n,) + shape
        else:
            shape = shape[:-1] + (shape[-1] * n,)
        plans.append((axis, src, dst))
        shapes.append(jax.ShapeDtypeStruct(shape, operand.dtype))
    slots = sum(sizes[axis] - 1 for axis, _, _ in plans)
    return pl.pallas_call(
        functools.partial(exchange_kernel, plans, sizes),
        out_shape=shapes,
        in_specs=[pl.BlockSpec(memory_space=pl.ANY)] * len(plans),
        out_specs=[pl.BlockSpec(memory_space=pl.ANY)] * len(plans),
        scratch_shapes=[
            pltpu.SemaphoreType.DMA((slots,)),
            pltpu.SemaphoreType.DMA((slots,)),
            pltpu.SemaphoreType.DMA((len(plans),)),
        ],
        compiler_params=pltpu.CompilerParams(collective_id=number, has_side_effects=True),
        cost_estimate=pl.CostEstimate(flops=1024, bytes_accessed=1024, transcendentals=0),
    )(*[move[0] for move in moves])


def gather_pass_kernel(nc, x_ref, a_ref, b_ref, send_sem, recv_sem, pass_send, pass_recv, near_sem):
    ci, di = lax.axis_index("col"), lax.axis_index("dp")
    greet([{"col": ci ^ k} for k in range(1, nc)] + [{"dp": di ^ 1}])
    near = pltpu.make_async_copy(x_ref, a_ref.at[ci], near_sem)
    near.start()
    far = []
    for k in range(1, nc):
        copy = pltpu.make_async_remote_copy(
            src_ref=x_ref,
            dst_ref=a_ref.at[ci],
            send_sem=send_sem.at[k],
            recv_sem=recv_sem.at[k],
            device_id={"col": ci ^ k},
            device_id_type=MESH_ID,
        )
        copy.start()
        far.append(copy)
    passed = []
    for k in range(nc):
        if k > 0:
            far[k - 1].wait_recv()
        copy = pltpu.make_async_remote_copy(
            src_ref=x_ref if k == 0 else a_ref.at[ci ^ k],
            dst_ref=b_ref.at[ci ^ k],
            send_sem=pass_send.at[k],
            recv_sem=pass_recv.at[k],
            device_id={"dp": di ^ 1},
            device_id_type=MESH_ID,
        )
        copy.start()
        passed.append(copy)
    near.wait()
    for copy in far:
        copy.wait_send()
    for copy in passed:
        copy.wait()


def gather_pass(number, x):
    nc = lax.axis_size("col")
    made = jax.ShapeDtypeStruct((nc,) + x.shape, x.dtype)
    a, b = pl.pallas_call(
        functools.partial(gather_pass_kernel, nc),
        out_shape=[made, made],
        in_specs=[pl.BlockSpec(memory_space=pl.ANY)],
        out_specs=[pl.BlockSpec(memory_space=pl.ANY)] * 2,
        scratch_shapes=[pltpu.SemaphoreType.DMA((nc,))] * 4 + [pltpu.SemaphoreType.DMA],
        compiler_params=pltpu.CompilerParams(collective_id=number, has_side_effects=True),
        cost_estimate=pl.CostEstimate(flops=1024, bytes_accessed=1024, transcendentals=0),
    )(x)
    rows = nc * x.shape[0]
    return a.reshape(rows, x.shape[1]), b.reshape(rows, x.shape[1])


def scatter_pass_kernel(nc, a_ref, b_ref, out_ref, came, total, send_sem, recv_sem, pass_send, pass_recv):
    ci, di = lax.axis_index("col"), lax.axis_index("dp")
    greet([{"col": ci ^ k} for k in range(1, nc)] + [{"dp": di ^ 1}])
    order = list(range(1, nc)) + [0]
    passed = {}
    for k in order:
        passed[k] = pltpu.make_async_remote_copy(
            src_ref=b_ref.at[ci ^ k],
            dst_ref=came.at[ci ^ k],
            send_sem=pass_send.at[k],
            recv_sem=pass_recv.at[k],
            device_id={"dp": di ^ 1},
            device_id_type=MESH_ID,
        )
        passed[k].start()
    far = []
    for k in order:
        passed[k].wait_recv()
        at = ci ^ k
        total[at] = (a_ref[at].astype(F32) + came[at].astype(F32)).astype(BF)
        if k > 0:
            copy = pltpu.make_async_remote_copy(
                src_ref=total.at[at],
                dst_ref=out_ref.at[ci],
                send_sem=send_sem.at[k],
                recv_sem=recv_sem.at[k],
                device_id={"col": at},
                device_id_type=MESH_ID,
            )
            copy.start()
            far.append(copy)
    out_ref[ci] = total[ci]
    for copy in far:
        copy.wait()
    for k in order:
        passed[k].wait_send()


def scatter_pass(number, a, b):
    nc = lax.axis_size("col")
    shape = (nc, a.shape[0] // nc, a.shape[1])
    return pl.pallas_call(
        functools.partial(scatter_pass_kernel, nc),
        out_shape=jax.ShapeDtypeStruct(shape, BF),
        in_specs=[pl.BlockSpec(memory_space=pltpu.VMEM), pl.BlockSpec(memory_space=pl.ANY)],
        out_specs=pl.BlockSpec(memory_space=pltpu.VMEM),
        scratch_shapes=[pltpu.VMEM(shape, BF)] * 2 + [pltpu.SemaphoreType.DMA((nc,))] * 4,
        compiler_params=pltpu.CompilerParams(
            collective_id=number, has_side_effects=True, vmem_limit_bytes=24 * 2**20
        ),
        cost_estimate=pl.CostEstimate(flops=1024, bytes_accessed=1024, transcendentals=0),
    )(a.reshape(shape), b.reshape(shape))


def block_sum(stack):
    return jnp.sum(stack.astype(F32), axis=0)


def col_gather(operand):
    return lax.all_gather(operand, "col", axis=0, tiled=True)


def col_scatter(operand):
    return lax.psum_scatter(operand, "col", scatter_dimension=0, tiled=True)


def pick(stack, index):
    return lax.dynamic_index_in_dim(stack, index, 0, keepdims=False)


def spread_weights(pieces, ci, nc):
    out = jnp.zeros_like(pieces)
    out = lax.dynamic_update_index_in_dim(out, pick(pieces, ci), ci, 0)
    for k in range(1, nc):
        got = swap(pick(pieces, ci ^ k), "col", k)
        out = lax.dynamic_update_index_in_dim(out, got, ci ^ k, 0)
    return out


def row_blocks(block):
    second = swap(block, "row", 2)
    return [block, swap(block, "row", 1), second, swap(second, "row", 1)]


def add_low(first, second):
    return (first.astype(F32) + second.astype(F32)).astype(BF)


def dp_sum(operand):
    if lax.axis_size("dp") == 2:
        return operand.astype(F32) + swap(operand, "dp", 1).astype(F32)
    return lax.psum(operand, "dp").astype(F32)


def dense_gates(normed, router, routes):
    experts = router.shape[1]
    logits = nn(normed, router)
    chosen = jnp.any(
        routes[:, :, None] == jnp.arange(experts, dtype=jnp.int32)[None, None, :], axis=1
    )
    top = jnp.max(jnp.where(chosen, logits, FILLER), axis=1, keepdims=True)
    weights = jnp.where(chosen, jnp.exp(jnp.where(chosen, logits - top, 0.0)), 0.0)
    return weights / jnp.sum(weights, axis=1, keepdims=True)


def expert_kernel(nb, tile, xa_ref, xb_ref, dya_ref, dyb_ref, gate_ref, mark_ref, *refs):
    wg, wu, wd = refs[:nb], refs[nb : 2 * nb], refs[2 * nb : 3 * nb]
    outs, dxs = refs[3 * nb : 3 * nb + 2], refs[3 * nb + 2 : 3 * nb + 4]
    made_refs = refs[3 * nb + 4 : 6 * nb + 4]
    dwg, dwu, dwd = made_refs[:nb], made_refs[nb : 2 * nb], made_refs[2 * nb :]
    w_in, w_out, xt, acc_out, acc_dx, act_s, dgu_s = refs[6 * nb + 4 :]
    nc, _, feat, hid = wg[0].shape
    wide = nb * hid
    width = nc * feat
    e = pl.program_id(0)
    rows = xa_ref.shape[0]
    for j in range(nb):
        for c in range(nc):
            w_in[c * feat : (c + 1) * feat, j * hid : (j + 1) * hid] = wg[j][c, 0]
            w_in[c * feat : (c + 1) * feat, wide + j * hid : wide + (j + 1) * hid] = wu[j][c, 0]
            w_out[j * hid : (j + 1) * hid, c * feat : (c + 1) * feat] = wd[j][c, 0]

    @pl.when(e == 0)
    def _():
        acc_out[...] = jnp.zeros_like(acc_out)
        acc_dx[...] = jnp.zeros_like(acc_dx)
        for h, ref in enumerate((xa_ref, xb_ref)):
            for c in range(nc):
                xt[c * feat : (c + 1) * feat, h * rows : (h + 1) * rows] = ref[
                    :, c * feat : (c + 1) * feat
                ].T

    mark = mark_ref[pl.ds(e, 1), :]
    for h, (x_ref, dy_ref) in enumerate(((xa_ref, dya_ref), (xb_ref, dyb_ref))):

        @pl.loop(0, rows // tile)
        def _(t):
            at = pl.ds(pl.multiple_of(t * tile, tile), tile)
            here = pl.ds(pl.multiple_of(h * rows + t * tile, tile), tile)
            gu = nn(x_ref[at, :], w_in[...])
            d_act = nt(dy_ref[at, :], w_out[...])
            gate = jnp.sum(gate_ref[here, :] * mark, axis=1, keepdims=True)
            spread = jnp.broadcast_to(gate, (tile, hid))
            total = None
            for j in range(nb):
                lo = j * hid
                g = gu[:, lo : lo + hid]
                u = gu[:, wide + lo : wide + lo + hid]
                da = d_act[:, lo : lo + hid]
                sig = 1.0 / (1.0 + jnp.exp(-g))
                swish = g * sig
                su = swish * u
                act_s[here, lo : lo + hid] = (su * spread).astype(BF)
                part = da * su
                total = part if total is None else total + part
                mid = da * spread
                dgu_s[here, lo : lo + hid] = (mid * u * (sig * (1.0 + g * (1.0 - sig)))).astype(BF)
                dgu_s[here, wide + lo : wide + lo + hid] = (mid * swish).astype(BF)
            acc_dx[here, width:] += jnp.sum(total, axis=1, keepdims=True) * mark
            acc_out[here, :] += nn(act_s[here, :], w_out[...])
            acc_dx[here, :width] += nt(dgu_s[here, :], w_in[...])

    @pl.loop(0, nc)
    def _(c):
        at = pl.ds(pl.multiple_of(c * feat, feat), feat)
        made = nn(xt[at, :], dgu_s[...])
        for j in range(nb):
            dwg[j][0, at, :] = made[:, j * hid : (j + 1) * hid].astype(BF)
            dwu[j][0, at, :] = made[:, wide + j * hid : wide + (j + 1) * hid].astype(BF)

    for j in range(nb):
        cut = slice(j * hid, (j + 1) * hid)
        dwd[j][0] = (tn(act_s[:rows, cut], dya_ref[...]) + tn(act_s[rows:, cut], dyb_ref[...])).astype(BF)

    @pl.when(e == pl.num_programs(0) - 1)
    def _():
        for h in range(2):
            outs[h][...] = acc_out[h * rows : (h + 1) * rows, :].astype(BF)
            dxs[h][...] = acc_dx[h * rows : (h + 1) * rows, :].astype(BF)


def expert_pass(x_a, x_b, dy_a, dy_b, gates, marks, wg, wu, wd):
    rows, width = x_a.shape
    nb = len(wg)
    nc, local, feat, hid = wg[0].shape
    wide = nb * hid
    lanes = marks.shape[1]

    def whole(shape):
        return pl.BlockSpec(shape, lambda e: (0,) * len(shape), pipeline_mode=pl.Buffered(1))

    up_spec = pl.BlockSpec((nc, 1, feat, hid), lambda e: (0, e, 0, 0))
    down_spec = pl.BlockSpec((nc, 1, hid, feat), lambda e: (0, e, 0, 0))
    made = pl.pallas_call(
        functools.partial(expert_kernel, nb, min(256, rows)),
        grid=(local,),
        in_specs=[whole(x_a.shape)] * 4
        + [whole(gates.shape), whole(marks.shape)]
        + [up_spec] * (2 * nb)
        + [down_spec] * nb,
        out_specs=[whole((rows, width))] * 2
        + [whole((rows, width + lanes))] * 2
        + [pl.BlockSpec((1, width, hid), lambda e: (e, 0, 0))] * (2 * nb)
        + [pl.BlockSpec((1, hid, width), lambda e: (e, 0, 0))] * nb,
        out_shape=[jax.ShapeDtypeStruct((rows, width), BF)] * 2
        + [jax.ShapeDtypeStruct((rows, width + lanes), BF)] * 2
        + [jax.ShapeDtypeStruct((local, width, hid), BF)] * (2 * nb)
        + [jax.ShapeDtypeStruct((local, hid, width), BF)] * nb,
        scratch_shapes=[
            pltpu.VMEM((width, 2 * wide), BF),
            pltpu.VMEM((wide, width), BF),
            pltpu.VMEM((width, 2 * rows), BF),
            pltpu.VMEM((2 * rows, width), F32),
            pltpu.VMEM((2 * rows, width + lanes), F32),
            pltpu.VMEM((2 * rows, wide), BF),
            pltpu.VMEM((2 * rows, 2 * wide), BF),
        ],
        compiler_params=pltpu.CompilerParams(vmem_limit_bytes=60 * 2**20),
        cost_estimate=pl.CostEstimate(flops=1024, bytes_accessed=1024, transcendentals=0),
    )(x_a, x_b, dy_a, dy_b, gates, marks, *wg, *wu, *wd)
    made = list(made)
    return made[0:2], made[2:4], made[4 : 4 + nb], made[4 + nb : 4 + 2 * nb], made[4 + 2 * nb :]


def body(
    block_input,
    deal_order,
    lengths,
    routes,
    first_gain,
    w_query,
    key_weight,
    value_weight,
    w_out,
    gain_two,
    w_router,
    w_gate,
    w_up,
    w_down,
    cotangent,
):
    nc, nr, ndp = lax.axis_size("col"), lax.axis_size("row"), lax.axis_size("dp")
    ci, ri, di = lax.axis_index("col"), lax.axis_index("row"), lax.axis_index("dp")
    rows, feat = block_input.shape
    width = feat * nc
    share = rows // nc
    group = rows * nr
    experts, _, hid = w_gate.shape
    halves = 2
    half = di % halves
    local = experts // (nc * halves)
    q_width = w_query.shape[1]
    kv_width = key_weight.shape[1]
    q_heads = q_width // HEAD_SIZE
    kv_heads = kv_width // HEAD_SIZE
    score_scale = 1.0 / math.sqrt(HEAD_SIZE)

    orders = deal_order[0]
    _, positions = places(orders, lengths[0])

    def dealt(a):
        return a.reshape(nr, nc, share).transpose(1, 0, 2).reshape(nc, nr * share)

    orders_all, positions_all = dealt(orders), dealt(positions)
    key_orders = orders_all.reshape(group, 1)
    row_orders = pick(orders_all, ci)[None, :]
    row_positions = pick(positions_all, ci)
    row_starts = row_orders - row_positions[None, :]
    cosine_table, sine_table = rope_tables(row_positions)

    ride = 16
    gain_rows = jnp.concatenate(
        [jnp.stack([first_gain, gain_two]), jnp.zeros((ride - 2, feat), BF)], axis=0
    )
    sent = jnp.concatenate(
        [
            block_input.reshape(nc, share, feat),
            jnp.broadcast_to(gain_rows[None], (nc, ride, feat)),
        ],
        axis=1,
    )
    (got,) = exchange(1, (sent, "col", "major", "lane"))
    got, w_gate_later = lax.optimization_barrier((got, w_gate))
    got = got.astype(F32)
    x_tok, gains = got[:share], got[share : share + 2]
    inv_one = lax.rsqrt(jnp.mean(x_tok * x_tok, axis=1, keepdims=True) + NORM_EPSILON)
    x_hat = x_tok * inv_one
    w_mine = jnp.concatenate([w_query, key_weight, value_weight], axis=1)
    normed, w_qkv = exchange(
        2, ((x_hat * gains[0]).astype(BF), "row", "all", "major"), (w_mine, "col", "all", "major")
    )
    normed = normed.reshape(nr * share, width)
    w_qkv = w_qkv.reshape(width, w_mine.shape[1])

    def spread(w):
        pieces = pick(w.reshape((halves, nc, local) + w.shape[1:]), half)
        return spread_weights(pieces, ci, nc)

    gate_stack = spread(w_gate_later)
    normed, w_out_later, router_later, cotangent = lax.optimization_barrier(
        (normed, w_out, w_router, cotangent)
    )
    w_tail = col_gather(jnp.concatenate([w_out_later.T, router_later], axis=1))
    w_out_t = w_tail[:, : w_out.shape[0]]
    router = w_tail[:, w_out.shape[0] :]
    dy_a = lax.all_gather(cotangent, "col", axis=1, tiled=True)
    dy_b = swap(dy_a, "dp", 1)

    qkv = dot(w_qkv, normed, ((0,), (1,)))
    count = nr * share
    queries = (rotate(qkv[:q_width], cosine_table, sine_table) * score_scale).astype(BF)
    keys = rotate(qkv[q_width : q_width + kv_width], cosine_table, sine_table).astype(BF)
    values = qkv[q_width + kv_width :].astype(BF)
    (pairs,) = exchange(3, (jnp.concatenate([keys, values], axis=0), "col", "all", "lane"))
    pairs, gate_stack, w_up_later = lax.optimization_barrier((pairs, gate_stack, w_up))
    up_stack = spread(w_up_later)
    gate_blocks = row_blocks(gate_stack)
    mixed, lse = attend(queries, pairs, key_orders, row_orders, row_starts, kv_heads)
    mixed, up_stack, w_down_later = lax.optimization_barrier((mixed, up_stack, w_down))
    down_stack = spread(w_down_later)
    up_blocks = row_blocks(up_stack)
    (branch,) = exchange(
        4,
        (
            dot(mixed, w_out_t, ((0,), (1,))).astype(BF).reshape(nr, share, width),
            "row",
            "major",
            "major",
        ),
    )
    hidden = x_tok + block_sum(branch)
    inv_two = lax.rsqrt(jnp.mean(hidden * hidden, axis=1, keepdims=True) + NORM_EPSILON)
    hidden_hat = hidden * inv_two
    normed_two = (hidden_hat * gains[1]).astype(BF)

    normed_two, down_stack = lax.optimization_barrier((normed_two, down_stack))
    down_blocks = row_blocks(down_stack)
    rows_a, rows_b = gather_pass(5, normed_two)
    routes_a = lax.dynamic_slice_in_dim(routes, ri * rows, rows)
    routes_b = swap(routes_a, "dp", 1)
    first_expert = (half * nc + ci) * local

    lanes = 128

    def padded_gates(tokens, chosen):
        return jnp.pad(dense_gates(tokens, router, chosen), ((0, 0), (0, lanes - experts)))

    gate_rows = jnp.concatenate([padded_gates(rows_a, routes_a), padded_gates(rows_b, routes_b)])
    marks = (
        jnp.arange(lanes, dtype=jnp.int32)[None, :]
        == first_expert + jnp.arange(local, dtype=jnp.int32)[:, None]
    ).astype(F32)
    outs, d_ins, d_gate_w, d_up_w, d_down_w = expert_pass(
        rows_a, rows_b, dy_a, dy_b, gate_rows, marks, gate_blocks, up_blocks, down_blocks
    )
    d_sum = scatter_pass(6, d_ins[0], d_ins[1])

    def swapped(blocks):
        return (swap(blocks[1], "row", 1), swap(blocks[3], "row", 1))

    def kept(blocks, got):
        return add_low(blocks[0], got[0]), add_low(blocks[2], got[1])

    def up_pieces(total):
        return total.reshape(local, nc, feat, hid).transpose(1, 0, 2, 3)

    def down_pieces(total):
        return total.reshape(local, hid, nc, feat).transpose(2, 0, 1, 3)

    def sent_back(pieces):
        mine = spread_weights(pieces, ci, nc)
        if ndp > halves:
            groups = [list(range(h, ndp, halves)) for h in range(halves)]
            mine = lax.psum(mine, "dp", axis_index_groups=groups)
        return mine

    def both_halves(mine, other):
        first = jnp.where(half == 0, mine, other)
        second = jnp.where(half == 0, other, mine)
        whole = jnp.stack([first, second]).astype(F32)
        return whole.reshape((experts,) + whole.shape[3:])

    got_down, got_gate, got_up = swapped(d_down_w), swapped(d_gate_w), swapped(d_up_w)
    d_sum, got_down, got_gate, got_up = lax.optimization_barrier(
        (d_sum, got_down, got_gate, got_up)
    )
    keep_down, send_down = kept(d_down_w, got_down)
    row_down = swap(send_down, "row", 2)
    keep_gate, send_gate = kept(d_gate_w, got_gate)
    keep_up, send_up = kept(d_up_w, got_up)
    d_sum = block_sum(d_sum)

    own_routes = lax.dynamic_slice_in_dim(routes_a, ci * share, share)
    gates = dense_gates(normed_two, router, own_routes)
    d_gates = d_sum[:, width : width + experts]
    d_logits = (gates * (d_gates - jnp.sum(gates * d_gates, axis=1, keepdims=True))).astype(BF)
    d_router = tn(jnp.pad(d_logits, ((0, 0), (0, 48 - experts))), normed_two).astype(BF)
    d_normed_two = d_sum[:, :width] + nt(d_logits, router)
    dy_tok = lax.dynamic_slice_in_dim(dy_a, ci * share, share).astype(F32)
    d_hat_two = d_normed_two * gains[1]
    d_gain_two = jnp.sum(d_normed_two * hidden_hat, axis=0)
    inner_two = jnp.mean(d_hat_two * hidden_hat, axis=1, keepdims=True)
    d_hidden = dy_tok + inv_two * (d_hat_two - hidden_hat * inner_two)

    (d_branch,) = exchange(7, (d_hidden.astype(BF), "row", "all", "major"))
    d_branch = d_branch.reshape(count, width)
    d_mixed = dot(w_out_t, d_branch, ((0,), (1,))).astype(BF)
    d_mixed, row_down, send_gate, out_b = lax.optimization_barrier(
        (d_mixed, row_down, send_gate, outs[1])
    )
    row_gate = swap(send_gate, "row", 2)
    down_back = sent_back(down_pieces(add_low(keep_down, row_down)))
    routed = col_scatter(add_low(outs[0], swap(out_b, "dp", 1))).astype(F32)
    output_tok = (hidden + routed).astype(BF)
    d_query, d_pairs = attend_back(
        queries, d_mixed, lse, pairs, key_orders, row_orders, row_starts, kv_heads
    )
    d_pairs, row_gate, send_up = lax.optimization_barrier((d_pairs, row_gate, send_up))
    row_up = swap(send_up, "row", 2)
    gate_back = sent_back(up_pieces(add_low(keep_gate, row_gate)))
    d_w_out_t = col_scatter(dot(d_branch, mixed, ((0,), (1,))).astype(BF))
    kv_parts, router_parts = exchange(
        8, (d_pairs, "col", "lane", "major"), (d_router, "col", "lane", "major")
    )
    kv_parts, down_back = lax.optimization_barrier((kv_parts, down_back))
    down_other = swap(down_back, "dp", 1)
    kv_grads = block_sum(kv_parts)
    d_query = rotate(d_query * score_scale, cosine_table, -sine_table).astype(BF)
    d_key = rotate(kv_grads[:kv_width], cosine_table, -sine_table).astype(BF)
    d_qkv = jnp.concatenate([d_query, d_key, kv_grads[kv_width:].astype(BF)], axis=0)
    d_parts, router_parts = exchange(
        9,
        (
            dot(d_qkv, w_qkv, ((0,), (1,))).astype(BF).reshape(nr, share, width),
            "row",
            "major",
            "major",
        ),
        (block_sum(router_parts).astype(BF), "row", "all", "major"),
    )
    d_parts, gate_back, row_up = lax.optimization_barrier((d_parts, gate_back, row_up))
    gate_other = swap(gate_back, "dp", 1)
    up_back = sent_back(up_pieces(add_low(keep_up, row_up)))
    d_w_qkv = col_scatter(dot(normed, d_qkv, ((0,), (1,))).astype(BF))
    d_normed = block_sum(d_parts)
    d_hat = d_normed * gains[0]
    d_gain_one = jnp.sum(d_normed * x_hat, axis=0)
    inner_one = jnp.mean(d_hat * x_hat, axis=1, keepdims=True)
    d_input_tok = d_hidden + inv_one * (d_hat - x_hat * inner_one)
    gain_parts = jnp.stack([d_gain_one, d_gain_two]).reshape(2, nc, feat).transpose(1, 0, 2)
    gain_parts = jnp.broadcast_to(gain_parts[None], (ndp * nr, nc, 2, feat)).reshape(-1, 2, feat)
    d_input, block_output, gain_parts, router_parts = exchange(
        10,
        (d_input_tok.astype(BF), "col", "lane", "major"),
        (output_tok, "col", "lane", "major"),
        (gain_parts, "world", "major", "major"),
        (block_sum(router_parts).astype(BF), "dp", "all", "major"),
    )
    d_input = d_input.reshape(rows, feat).astype(F32)
    block_output = block_output.reshape(rows, feat)
    d_gains = block_sum(gain_parts)
    d_router = block_sum(router_parts)[:experts].T

    d_w_qkv = dp_sum(d_w_qkv)
    d_w_out = dp_sum(d_w_out_t).T
    up_other = swap(up_back, "dp", 1)
    d_w_down = both_halves(down_back, down_other)
    d_w_gate = both_halves(gate_back, gate_other)
    d_w_up = both_halves(up_back, up_other)
    return (
        block_output,
        d_input,
        d_gains[0],
        d_w_qkv[:, :q_width],
        d_w_qkv[:, q_width : q_width + kv_width],
        d_w_qkv[:, q_width + kv_width :],
        d_w_out,
        d_gains[1],
        d_router,
        d_w_gate,
        d_w_up,
        d_w_down,
    )


def solution(mesh):
    residual = P(("dp", "row"), "col")
    return jax.shard_map(
        body,
        mesh=mesh,
        in_specs=(
            residual,
            P("dp", None),
            P("dp", None),
            P("dp", None),
            P("col"),
            P("col", "row"),
            P("col", "row"),
            P("col", "row"),
            P("row", "col"),
            P("col"),
            P("col", None),
            P(None, "col", "row"),
            P(None, "col", "row"),
            P(None, "row", "col"),
            residual,
        ),
        out_specs=(
            residual,
            residual,
            P("col"),
            P("col", "row"),
            P("col", "row"),
            P("col", "row"),
            P("row", "col"),
            P("col"),
            P("col", None),
            P(None, "col", "row"),
            P(None, "col", "row"),
            P(None, "row", "col"),
        ),
        check_vma=False,
    )
```

```python
import functools
import math

import jax
import jax.numpy as jnp
from jax import lax
from jax.experimental import pallas as pl
from jax.experimental.pallas import tpu as pltpu
from jax.sharding import PartitionSpec as P

HEAD_SIZE = 64
TOPK = 8
NORM_EPSILON = 1e-06
THETA = 10000.0
FILLER = -1e30
BF = jnp.bfloat16
F32 = jnp.float32


def dot(a, b, dims):
    return lax.dot_general(a, b, (dims, ((), ())), preferred_element_type=F32)


def nn(a, b):
    return dot(a, b, ((1,), (0,)))


def nt(a, b):
    return dot(a, b, ((1,), (1,)))


def tn(a, b):
    return dot(a, b, ((0,), (0,)))


def rope_tables(positions):
    half_head = HEAD_SIZE // 2
    frequency = THETA ** (-(2.0 / HEAD_SIZE) * jnp.arange(half_head).astype(F32))
    angles = positions.astype(F32)[None, :] * frequency[:, None]
    return (jnp.cos(angles), jnp.sin(angles))


def rotate(vector, cosine_table, sine_table):
    half_head = HEAD_SIZE // 2
    parts = vector.reshape(-1, HEAD_SIZE, vector.shape[1])
    first, second = parts[:, :half_head], parts[:, half_head:]
    return jnp.concatenate(
        [
            first * cosine_table - second * sine_table,
            second * cosine_table + first * sine_table,
        ],
        axis=1,
    ).reshape(vector.shape)


def places(orders, lengths):
    ends = jnp.cumsum(lengths)
    starts = ends - lengths
    inside = ((orders[:, None] >= starts[None, :]) & (orders[:, None] < ends[None, :])).astype(
        jnp.int32
    )
    seq_ids = jnp.sum(inside * jnp.arange(lengths.shape[0], dtype=jnp.int32)[None, :], axis=1)
    positions = orders - jnp.sum(inside * starts[None, :], axis=1)
    return (seq_ids, positions)


def swap(operand, axis, bit):
    n = lax.axis_size(axis)
    return lax.ppermute(operand, axis, [(i, i ^ bit) for i in range(n)])


MESH_ID = pl.DeviceIdType.MESH


def cut(ref, how, index, size):
    if how == "all":
        return ref
    if how == "major":
        return ref.at[index]
    return ref.at[:, pl.ds(pl.multiple_of(index * size, 128), size)]


WORLD = ("dp", "row", "col")
HBM = pl.BlockSpec(memory_space=pl.ANY)
FREE = pl.CostEstimate(flops=1024, bytes_accessed=1024, transcendentals=0)


def size_of(axis):
    return lax.axis_size(WORLD) if axis == "world" else lax.axis_size(axis)


def place_of(axis):
    return lax.axis_index(WORLD) if axis == "world" else lax.axis_index(axis)


def at_place(axis, index):
    if axis != "world":
        return {axis: index}
    nr, nc = lax.axis_size("row"), lax.axis_size("col")
    return {"dp": index // (nr * nc), "row": index // nc % nr, "col": index % nc}


def two_step(plan):
    axis, src, _, n = plan
    return axis == "row" and src == "all" and n == 4


def partners(plans):
    found = []
    for plan in plans:
        axis, src, _, n = plan
        if src[0] == "swap":
            ways = [(axis, src[1])]
        else:
            ways = [(axis, k) for k in range(1, 3 if two_step(plan) else n)]
        if src == "shared":
            ways.append(("dp", 1))
        found += [way for way in ways if way not in found]
    if any(axis == "world" for axis, _ in found):
        found = [way for way in found if way[0] == "world"]
    return found


def greet(ways):
    barrier = pltpu.get_barrier_semaphore()
    for axis, k in ways:
        peer = at_place(axis, place_of(axis) ^ k)
        pl.semaphore_signal(barrier, inc=1, device_id=peer, device_id_type=MESH_ID)
    pl.semaphore_wait(barrier, len(ways))


def remote(src, dst, sems, at, device):
    return pltpu.make_async_remote_copy(
        src_ref=src,
        dst_ref=dst,
        send_sem=sems[0].at[at],
        recv_sem=sems[1].at[at],
        device_id=device,
        device_id_type=MESH_ID,
    )


def slots_of(plan):
    _, src, _, n = plan
    if src[0] == "swap":
        return 1
    return 2 * (n - 1) if src == "shared" else n - 1


class Move:
    def __init__(self, plan, x, out, sems, base, which):
        axis, src, dst, n = plan
        i, di = place_of(axis), place_of("dp")
        self.near, self.far, self.relays = [], [], []

        def near(source, target):
            self.near.append(pltpu.make_async_copy(source, target, sems[2].at[which]))

        def far(source, target, device):
            at = base + len(self.far) + len(self.relays)
            return remote(source, target, sems, at, device)

        if src[0] == "swap":
            self.far.append(far(x, out, at_place(axis, i ^ src[1])))
        elif src == "shared":
            part = x.shape[0] // 2
            half = pl.ds(pl.multiple_of(di % 2 * part, part), part)
            near(x, out.at[i])
            for k in range(1, n):
                self.far.append(far(x.at[half], out.at[i, half], at_place(axis, i ^ k)))
            for k in range(1, n):
                block = out.at[i ^ k, half]
                self.relays.append((self.far[k - 1], far(block, block, {"dp": di ^ 1})))
        elif src[0] == "spread":
            first, local, count = src[1:]

            def block(c):
                return x.at[pl.ds((di % 2 * n + c) * local + first, count)]

            near(block(i), out.at[i])
            for k in range(1, n):
                self.far.append(far(block(i ^ k), out.at[i], at_place(axis, i ^ k)))
        elif src == "second":
            size = x.shape[1] // n

            def cols(c):
                return x.at[:, pl.ds(pl.multiple_of(c * size, size), size)]

            near(cols(i), out.at[i])
            for k in range(1, n):
                self.far.append(far(cols(i ^ k), out.at[i], at_place(axis, i ^ k)))
        else:
            in_size, out_size = x.shape[-1] // n, out.shape[-1] // n
            near(cut(x, src, i, in_size), cut(out, dst, i, out_size))
            for k in range(1, 3 if two_step(plan) else n):
                self.far.append(
                    far(
                        cut(x, src, i ^ k, in_size),
                        cut(out, dst, i, out_size),
                        at_place(axis, i ^ k),
                    )
                )
            if two_step(plan):
                block = out.at[i ^ 2]
                self.relays.append((self.far[1], far(block, block, {"row": i ^ 1})))

    def start(self):
        for copy in self.near + self.far:
            copy.start()

    def relay(self):
        for came, onward in self.relays:
            came.wait_recv()
            onward.start()

    def finish(self):
        passed = [came for came, _ in self.relays]
        for copy in self.near:
            copy.wait()
        for copy in self.far:
            if any(copy is came for came in passed):
                copy.wait_send()
            else:
                copy.wait()
        for _, onward in self.relays:
            onward.wait()


def moves_in(plans, ins, outs, sems):
    made, base = [], 0
    for which, plan in enumerate(plans):
        made.append(Move(plan, ins[which], outs[which], sems, base, which))
        base += slots_of(plan)
    return made


def finish_all(moves):
    for move in moves:
        move.relay()
    for move in moves:
        move.finish()


def planned(moves):
    plans, shapes = [], []
    for operand, axis, src, dst in moves:
        n = size_of(axis)
        shape = operand.shape
        if src[0] == "swap":
            plans.append((axis, src, dst, n))
            shapes.append(jax.ShapeDtypeStruct(shape, operand.dtype))
            continue
        if src[0] == "spread":
            shape = (src[3],) + shape[1:]
        elif src == "second":
            shape = shape[:1] + (shape[1] // n,) + shape[2:]
        elif src == "major":
            shape = shape[1:]
        elif src == "lane":
            shape = shape[:-1] + (shape[-1] // n,)
        if dst == "major":
            shape = (n,) + shape
        else:
            shape = shape[:-1] + (shape[-1] * n,)
        plans.append((axis, src, dst, n))
        shapes.append(jax.ShapeDtypeStruct(shape, operand.dtype))
    return plans, shapes


def move_sems(plans):
    count = sum(slots_of(plan) for plan in plans)
    return [
        pltpu.SemaphoreType.DMA((count,)),
        pltpu.SemaphoreType.DMA((count,)),
        pltpu.SemaphoreType.DMA((len(plans),)),
    ]


def exchange_kernel(plans, *refs):
    count = len(plans)
    greet(partners(plans))
    moves = moves_in(plans, refs[:count], refs[count : 2 * count], refs[2 * count :])
    for move in moves:
        move.start()
    finish_all(moves)


def exchange(number, *moves):
    plans, shapes = planned(moves)
    return pl.pallas_call(
        functools.partial(exchange_kernel, plans),
        out_shape=shapes,
        in_specs=[HBM] * len(plans),
        out_specs=[HBM] * len(plans),
        scratch_shapes=move_sems(plans),
        compiler_params=pltpu.CompilerParams(collective_id=number, has_side_effects=True),
        cost_estimate=FREE,
    )(*[move[0] for move in moves])


def gather_pass_kernel(nc, plans, *refs):
    count = len(plans)
    x_ref, ins, refs = refs[0], refs[1 : 1 + count], refs[1 + count :]
    own, core, pair, both = refs[:4]
    outs, refs = refs[4 : 4 + count], refs[4 + count :]
    sems, near_sem, move_sem = refs[:2], refs[2], refs[3:]
    ci, ri, di = lax.axis_index("col"), lax.axis_index("row"), lax.axis_index("dp")
    to_core, to_pair = {"row": ri ^ 1}, {"dp": di ^ 1}
    ways = [("col", k) for k in range(1, nc)] + [("row", 1), ("dp", 1)]
    greet(ways + [way for way in partners(plans) if way not in ways])

    def send(way, k, src, dst, device):
        copy = remote(src, dst, (sems[0].at[way], sems[1].at[way]), k, device)
        copy.start()
        return copy

    near = pltpu.make_async_copy(x_ref, own.at[ci], near_sem)
    near.start()
    far = [send(0, k, x_ref, own.at[ci], {"col": ci ^ k}) for k in range(1, nc)]
    moves = moves_in(plans, ins, outs, move_sem)
    for move in moves:
        move.start()
    paired, cored, waits = [], [], []
    for k in range(nc):
        if k > 0:
            far[k - 1].wait_recv()
            waits.append(far[k - 1].wait_send)
        block = x_ref if k == 0 else own.at[ci ^ k]
        paired.append(send(1, k, block, pair.at[ci ^ k], to_pair))
        cored.append(send(2, k, block, core.at[ci ^ k], to_core))
    for k in range(nc):
        paired[k].wait_recv()
        waits.append(paired[k].wait_send)
        waits.append(cored[k].wait)
        waits.append(send(3, k, pair.at[ci ^ k], both.at[ci ^ k], to_core).wait)
    waits.append(near.wait)
    for wait in waits:
        wait()
    finish_all(moves)


def gather_pass(number, x, *moves):
    nc = lax.axis_size("col")
    plans, shapes = planned(moves)
    made = jax.ShapeDtypeStruct((nc,) + x.shape, x.dtype)
    got = pl.pallas_call(
        functools.partial(gather_pass_kernel, nc, plans),
        out_shape=[made] * 4 + shapes,
        in_specs=[HBM] * (1 + len(plans)),
        out_specs=[HBM] * (4 + len(plans)),
        scratch_shapes=[pltpu.SemaphoreType.DMA((4, nc))] * 2
        + [pltpu.SemaphoreType.DMA]
        + move_sems(plans),
        compiler_params=pltpu.CompilerParams(collective_id=number, has_side_effects=True),
        cost_estimate=FREE,
    )(x, *[move[0] for move in moves])
    got = list(got)
    return [block.reshape(nc * x.shape[0], x.shape[1]) for block in got[:4]], got[4:]


def scatter_pass_kernel(nc, parts, plans, *refs):
    count = len(plans)
    ins, refs = refs[: 4 * parts], refs[4 * parts :]
    move_ins, out_ref, move_outs = refs[:count], refs[count], refs[count + 1 : 2 * count + 1]
    made, came, total, send_sem, recv_sem = refs[2 * count + 1 : 2 * count + 6]
    move_sem = refs[2 * count + 6 :]
    ci, ri, di = lax.axis_index("col"), lax.axis_index("row"), lax.axis_index("dp")
    to_core, to_pair = {"row": ri ^ 1}, {"dp": di ^ 1}
    ways = [("col", k) for k in range(1, nc)] + [("row", 1), ("dp", 1)]
    greet(ways + [way for way in partners(plans) if way not in ways])
    moves = moves_in(plans, move_ins, move_outs, move_sem)
    for move in moves:
        move.start()
    order = list(range(1, nc)) + [0]

    def send(way, k, src, dst, device):
        copy = remote(src, dst, (send_sem.at[way], recv_sem.at[way]), k, device)
        copy.start()
        return copy

    def added(which, at, *more):
        value = ins[which][at].astype(F32)
        for p in range(1, parts):
            value = value + ins[4 * p + which][at].astype(F32)
        for other in more:
            value = value + came[other, at].astype(F32)
        return value.astype(BF)

    sent = {}
    for k in order:
        at = ci ^ k
        for way, which in ((0, 3), (1, 1)):
            made[way, at] = added(which, at)
            sent[way, k] = send(way, k, made.at[way, at], came.at[way, at], to_core)
    for k in order:
        at = ci ^ k
        sent[0, k].wait_recv()
        made[2, at] = added(2, at, 0)
        sent[2, k] = send(2, k, made.at[2, at], came.at[2, at], to_pair)
    for k in order:
        at = ci ^ k
        sent[1, k].wait_recv()
        sent[2, k].wait_recv()
        total[at] = added(0, at, 1, 2)
        if k > 0:
            sent[3, k] = send(3, k, total.at[at], out_ref.at[ci], {"col": at})
    out_ref[ci] = total[ci]
    for way in range(3):
        for k in order:
            sent[way, k].wait_send()
    for k in range(1, nc):
        sent[3, k].wait()
    finish_all(moves)


def scatter_pass(number, parts, *moves):
    nc = lax.axis_size("col")
    plans, shapes = planned(moves)
    rows, width = parts[0][0].shape
    shape = (nc, rows // nc, width)
    vmem = pl.BlockSpec(memory_space=pltpu.VMEM)
    got = pl.pallas_call(
        functools.partial(scatter_pass_kernel, nc, len(parts), plans),
        out_shape=[jax.ShapeDtypeStruct(shape, BF)] + shapes,
        in_specs=[vmem] * (4 * len(parts)) + [HBM] * len(plans),
        out_specs=[vmem] + [HBM] * len(plans),
        scratch_shapes=[
            pltpu.VMEM((3,) + shape, BF),
            pltpu.VMEM((3,) + shape, BF),
            pltpu.VMEM(shape, BF),
            pltpu.SemaphoreType.DMA((4, nc)),
            pltpu.SemaphoreType.DMA((4, nc)),
        ]
        + move_sems(plans),
        compiler_params=pltpu.CompilerParams(
            collective_id=number, has_side_effects=True, vmem_limit_bytes=48 * 2**20
        ),
        cost_estimate=FREE,
    )(*[block.reshape(shape) for part in parts for block in part], *[move[0] for move in moves])
    return got[0], list(got[1:])


def block_sum(stack):
    return jnp.sum(stack.astype(F32), axis=0)


def col_gather(operand):
    return lax.all_gather(operand, "col", axis=0, tiled=True)


def col_scatter(operand):
    return lax.psum_scatter(operand, "col", scatter_dimension=0, tiled=True)


def pick(stack, index):
    return lax.dynamic_index_in_dim(stack, index, 0, keepdims=False)


def add_low(first, second):
    return (first.astype(F32) + second.astype(F32)).astype(BF)


def pair_sums(operand):
    ndp = lax.axis_size("dp")
    if ndp == 2:
        return operand
    return lax.psum(operand, "dp", axis_index_groups=[list(range(h, ndp, 2)) for h in range(2)])


def weight_sum(operand, half):
    nc = lax.axis_size("col")
    parts = operand.reshape(nc, 2, -1, operand.shape[1]).transpose(1, 0, 2, 3)
    mine = add_low(pick(parts, half), swap(pick(parts, 1 - half), "dp", 1))
    mine = pair_sums(col_scatter(mine.reshape(-1, operand.shape[1])))
    other = swap(mine, "dp", 1)
    first = jnp.where(half == 0, mine, other)
    second = jnp.where(half == 0, other, mine)
    return jnp.concatenate([first, second]).astype(F32)


def dense_gates(normed, router, routes):
    experts = router.shape[1]
    logits = nn(normed, router)
    chosen = jnp.any(
        routes[:, :, None] == jnp.arange(experts, dtype=jnp.int32)[None, None, :], axis=1
    )
    top = jnp.max(jnp.where(chosen, logits, FILLER), axis=1, keepdims=True)
    weights = jnp.where(chosen, jnp.exp(jnp.where(chosen, logits - top, 0.0)), 0.0)
    return weights / jnp.sum(weights, axis=1, keepdims=True)


def bias_into(bias, key_ref, row_ref, start_ref, chunk):
    @pl.loop(0, bias.shape[0] // chunk)
    def _(c):
        at = pl.ds(pl.multiple_of(c * chunk, chunk), chunk)
        keys = key_ref[at, :]
        seen = (keys <= row_ref[...]) & (keys >= start_ref[...])
        bias[at, :] = jnp.where(seen, 0.0, FILLER)


def attend_kernel(tile, kv_heads, plans, *refs):
    count = len(plans)
    q_ref, kv_ref, key_ref, row_ref, start_ref = refs[:5]
    ins, refs = refs[5 : 5 + count], refs[5 + count :]
    o_ref, lse_ref = refs[:2]
    outs, refs = refs[2 : 2 + count], refs[2 + count :]
    bias, k_s, sems = refs[0], refs[1], refs[2:]
    greet(partners(plans))
    moves = moves_in(plans, ins, outs, sems)
    for move in moves:
        move.start()
    size = HEAD_SIZE
    heads = q_ref.shape[0] // size
    per = heads // kv_heads
    rows = q_ref.shape[1]
    bias_into(bias, key_ref, row_ref, start_ref, 256)
    for g in range(kv_heads):
        k_s[g] = kv_ref[g * size : (g + 1) * size, :].T

    @pl.loop(0, heads)
    def _(h):
        g = h // per
        at = pl.ds(pl.multiple_of(h * size, size), size)
        v_at = pl.ds(pl.multiple_of((kv_heads + g) * size, size), size)
        for t in range(rows // tile):
            cut = slice(t * tile, (t + 1) * tile)
            scores = nn(k_s[g], q_ref[at, cut]) + bias[:, cut]
            top = jnp.max(scores, axis=0, keepdims=True)
            weights = jnp.exp(scores - top)
            total = jnp.sum(weights, axis=0, keepdims=True)
            chances = (weights * (1.0 / total)).astype(BF)
            o_ref[at, cut] = nn(kv_ref[v_at, :], chances).astype(BF)
            lse_ref[h, :, cut] = top + jnp.log(total)

    finish_all(moves)


def attend(number, q, kv, keys, rows_at, starts, kv_heads, *moves):
    plans, shapes = planned(moves)
    heads, count = q.shape[0] // HEAD_SIZE, q.shape[1]
    group = kv.shape[1]
    vmem = pl.BlockSpec(memory_space=pltpu.VMEM)
    got = pl.pallas_call(
        functools.partial(attend_kernel, min(256, count), kv_heads, plans),
        out_shape=[
            jax.ShapeDtypeStruct(q.shape, BF),
            jax.ShapeDtypeStruct((heads, 1, count), F32),
        ]
        + shapes,
        in_specs=[vmem] * 5 + [HBM] * len(plans),
        out_specs=[vmem] * 2 + [HBM] * len(plans),
        scratch_shapes=[
            pltpu.VMEM((group, count), F32),
            pltpu.VMEM((kv_heads, group, HEAD_SIZE), BF),
        ]
        + move_sems(plans),
        compiler_params=pltpu.CompilerParams(
            collective_id=number, has_side_effects=True, vmem_limit_bytes=48 * 2**20
        ),
        cost_estimate=FREE,
    )(q, kv, keys, rows_at, starts, *[move[0] for move in moves])
    return got[0], got[1], list(got[2:])


def attend_back_kernel(tile, kv_heads, plans, *refs):
    count = len(plans)
    q_ref, do_ref, lse_ref, kv_ref, key_ref, row_ref, start_ref = refs[:7]
    ins, refs = refs[7 : 7 + count], refs[7 + count :]
    dq_ref, dkv_ref = refs[:2]
    outs, refs = refs[2 : 2 + count], refs[2 + count :]
    bias, k_s, v_s, dk_s, dv_s = refs[:5]
    greet(partners(plans))
    moves = moves_in(plans, ins, outs, refs[5:])
    for move in moves:
        move.start()
    size = HEAD_SIZE
    heads = q_ref.shape[0] // size
    per = heads // kv_heads
    rows = q_ref.shape[1]
    bias_into(bias, key_ref, row_ref, start_ref, 256)
    for g in range(kv_heads):
        k_s[g] = kv_ref[g * size : (g + 1) * size, :].T
        v_s[g] = kv_ref[(kv_heads + g) * size : (kv_heads + g + 1) * size, :].T
    dk_s[...] = jnp.zeros_like(dk_s)
    dv_s[...] = jnp.zeros_like(dv_s)

    @pl.loop(0, heads)
    def _(h):
        g = h // per
        at = pl.ds(pl.multiple_of(h * size, size), size)
        k_at = pl.ds(pl.multiple_of(g * size, size), size)
        for t in range(rows // tile):
            cut = slice(t * tile, (t + 1) * tile)
            q_part, do_part = q_ref[at, cut], do_ref[at, cut]
            scores = nn(k_s[g], q_part) + bias[:, cut]
            probs = jnp.exp(scores - lse_ref[h, :, cut])
            d_chances = nn(v_s[g], do_part)
            dv_s[g] += nt(probs.astype(BF), do_part)
            both = probs * d_chances
            d_scores = (both - probs * jnp.sum(both, axis=0, keepdims=True)).astype(BF)
            dk_s[g] += nt(d_scores, q_part)
            dq_ref[at, cut] = nn(kv_ref[k_at, :], d_scores)

    for g in range(kv_heads):
        dkv_ref[g * size : (g + 1) * size, :] = dk_s[g].T.astype(BF)
        dkv_ref[(kv_heads + g) * size : (kv_heads + g + 1) * size, :] = dv_s[g].T.astype(BF)
    finish_all(moves)


def attend_back(number, q, do, lse, kv, keys, rows_at, starts, kv_heads, *moves):
    plans, shapes = planned(moves)
    count = q.shape[1]
    group = kv.shape[1]
    vmem = pl.BlockSpec(memory_space=pltpu.VMEM)
    got = pl.pallas_call(
        functools.partial(attend_back_kernel, min(256, count), kv_heads, plans),
        out_shape=[jax.ShapeDtypeStruct(q.shape, F32), jax.ShapeDtypeStruct(kv.shape, BF)]
        + shapes,
        in_specs=[vmem] * 7 + [HBM] * len(plans),
        out_specs=[vmem] * 2 + [HBM] * len(plans),
        scratch_shapes=[
            pltpu.VMEM((group, count), F32),
            pltpu.VMEM((kv_heads, group, HEAD_SIZE), BF),
            pltpu.VMEM((kv_heads, group, HEAD_SIZE), BF),
            pltpu.VMEM((kv_heads, group, HEAD_SIZE), F32),
            pltpu.VMEM((kv_heads, group, HEAD_SIZE), F32),
        ]
        + move_sems(plans),
        compiler_params=pltpu.CompilerParams(
            collective_id=number, has_side_effects=True, vmem_limit_bytes=56 * 2**20
        ),
        cost_estimate=FREE,
    )(q, do, lse, kv, keys, rows_at, starts, *[move[0] for move in moves])
    return got[0], got[1], list(got[2:])


def expert_kernel(sets, nb, tile, plans, onward, *refs):
    x_refs, dy_refs = refs[:sets], refs[sets : 2 * sets]
    gate_ref, mark_ref = refs[2 * sets : 2 * sets + 2]
    refs = refs[2 * sets + 2 :]
    wg, wu, wd = refs[:nb], refs[nb : 2 * nb], refs[2 * nb : 3 * nb]
    refs = refs[3 * nb :]
    count = len(plans) - len(onward)
    move_ins, refs = list(refs[:count]), refs[count:]
    outs, dxs = refs[:sets], refs[sets : 2 * sets]
    refs = refs[2 * sets :]
    dwg, dwu, dwd = refs[:nb], refs[nb : 2 * nb], refs[2 * nb : 3 * nb]
    refs = refs[3 * nb :]
    move_outs, refs = refs[: len(plans)], refs[len(plans) :]
    w_in, w_out, xt, act_s, dgu_s = refs[:5]
    move_ins += [move_outs[which] for which, _ in onward]
    moves = moves_in(plans, move_ins, move_outs, refs[5:])
    done = [which for which, _ in onward]
    nc, _, feat, hid = wg[0].shape
    wide = nb * hid
    width = nc * feat
    e = pl.program_id(0)
    rows = x_refs[0].shape[0]

    @pl.when(e == 0)
    def _():
        greet(partners(plans))
        for move in moves[:count]:
            move.start()

    for later, (which, step) in enumerate(onward):

        @pl.when(e == step)
        def _():
            moves[which].finish()
            moves[count + later].start()

    for j in range(nb):
        for c in range(nc):
            w_in[c * feat : (c + 1) * feat, j * hid : (j + 1) * hid] = wg[j][c, 0]
            w_in[c * feat : (c + 1) * feat, wide + j * hid : wide + (j + 1) * hid] = wu[j][c, 0]
            w_out[j * hid : (j + 1) * hid, c * feat : (c + 1) * feat] = wd[j][c, 0]

    @pl.when(e == 0)
    def _():
        for h in range(sets):
            outs[h][...] = jnp.zeros_like(outs[h])
            dxs[h][...] = jnp.zeros_like(dxs[h])
            for c in range(nc):
                cut_at = slice(c * feat, (c + 1) * feat)
                xt[cut_at, h * rows : (h + 1) * rows] = x_refs[h][:, cut_at].T

    mark = mark_ref[pl.ds(e, 1), :]
    for h in range(sets):
        x_ref, dy_ref, out_ref, dx_ref = x_refs[h], dy_refs[h], outs[h], dxs[h]

        @pl.loop(0, rows // tile)
        def _(t):
            at = pl.ds(pl.multiple_of(t * tile, tile), tile)
            here = pl.ds(pl.multiple_of(h * rows + t * tile, tile), tile)
            gu = nn(x_ref[at, :], w_in[...])
            d_act = nt(dy_ref[at, :], w_out[...])
            gate = jnp.sum(gate_ref[here, :] * mark, axis=1, keepdims=True)
            spread = jnp.broadcast_to(gate, (tile, hid))
            total = None
            for j in range(nb):
                lo = j * hid
                g = gu[:, lo : lo + hid]
                u = gu[:, wide + lo : wide + lo + hid]
                da = d_act[:, lo : lo + hid]
                sig = 1.0 / (1.0 + jnp.exp(-g))
                swish = g * sig
                su = swish * u
                act_s[here, lo : lo + hid] = (su * spread).astype(BF)
                part = da * su
                total = part if total is None else total + part
                mid = da * spread
                dgu_s[here, lo : lo + hid] = (mid * u * (sig * (1.0 + g * (1.0 - sig)))).astype(BF)
                dgu_s[here, wide + lo : wide + lo + hid] = (mid * swish).astype(BF)
            d_gate = jnp.sum(total, axis=1, keepdims=True) * mark
            dx_ref[at, width:] = (dx_ref[at, width:].astype(F32) + d_gate).astype(BF)
            out_ref[at, :] = (out_ref[at, :].astype(F32) + nn(act_s[here, :], w_out[...])).astype(BF)
            dx_ref[at, :width] = (
                dx_ref[at, :width].astype(F32) + nt(dgu_s[here, :], w_in[...])
            ).astype(BF)

    @pl.loop(0, nc)
    def _(c):
        at = pl.ds(pl.multiple_of(c * feat, feat), feat)
        made = nn(xt[at, :], dgu_s[...])
        for j in range(nb):
            dwg[j][0, at, :] = made[:, j * hid : (j + 1) * hid].astype(BF)
            dwu[j][0, at, :] = made[:, wide + j * hid : wide + (j + 1) * hid].astype(BF)

    made = None
    for h in range(sets):
        part = tn(act_s[h * rows : (h + 1) * rows, :], dy_refs[h][...])
        made = part if made is None else made + part
    for j in range(nb):
        for c in range(nc):
            dwd[j][c, 0] = made[j * hid : (j + 1) * hid, c * feat : (c + 1) * feat].astype(BF)

    @pl.when(e == pl.num_programs(0) - 1)
    def _():
        finish_all([move for which, move in enumerate(moves) if which not in done])


def expert_pass(number, xs, dys, gates, marks, wg, wu, wd, moves, onward=(), tile=512):
    plans, shapes = planned(moves)
    for which, _ in onward:
        plans.append(("row", ("swap", 2), None, size_of("row")))
        shapes.append(shapes[which])
    rows, width = xs[0].shape
    sets, nb = len(xs), len(wg)
    nc, local, feat, hid = wg[0].shape
    wide = nb * hid
    lanes = marks.shape[1]
    tile = min(tile, rows)

    def whole(shape):
        return pl.BlockSpec(shape, lambda e: (0,) * len(shape), pipeline_mode=pl.Buffered(1))

    up_spec = pl.BlockSpec((nc, 1, feat, hid), lambda e: (0, e, 0, 0))
    down_spec = pl.BlockSpec((nc, 1, hid, feat), lambda e: (0, e, 0, 0))
    made = pl.pallas_call(
        functools.partial(expert_kernel, sets, nb, tile, plans, onward),
        grid=(local,),
        in_specs=[whole((rows, width))] * (2 * sets)
        + [whole(gates.shape), whole(marks.shape)]
        + [up_spec] * (2 * nb)
        + [down_spec] * nb
        + [HBM] * len(moves),
        out_specs=[whole((rows, width))] * sets
        + [whole((rows, width + lanes))] * sets
        + [pl.BlockSpec((1, width, hid), lambda e: (e, 0, 0))] * (2 * nb)
        + [down_spec] * nb
        + [HBM] * len(plans),
        out_shape=[jax.ShapeDtypeStruct((rows, width), BF)] * sets
        + [jax.ShapeDtypeStruct((rows, width + lanes), BF)] * sets
        + [jax.ShapeDtypeStruct((local, width, hid), BF)] * (2 * nb)
        + [jax.ShapeDtypeStruct((nc, local, hid, feat), BF)] * nb
        + shapes,
        scratch_shapes=[
            pltpu.VMEM((width, 2 * wide), BF),
            pltpu.VMEM((wide, width), BF),
            pltpu.VMEM((width, sets * rows), BF),
            pltpu.VMEM((sets * rows, wide), BF),
            pltpu.VMEM((sets * rows, 2 * wide), BF),
        ]
        + move_sems(plans),
        compiler_params=pltpu.CompilerParams(
            collective_id=number, has_side_effects=True, vmem_limit_bytes=60 * 2**20
        ),
        cost_estimate=FREE,
    )(*xs, *dys, gates, marks, *wg, *wu, *wd, *[move[0] for move in moves])
    made = list(made)
    outs, dxs, made = made[:sets], made[sets : 2 * sets], made[2 * sets :]
    return outs, dxs, [made[:nb], made[nb : 2 * nb], made[2 * nb : 3 * nb]], made[3 * nb :]


def body(
    block_input,
    deal_order,
    lengths,
    routes,
    first_gain,
    w_query,
    key_weight,
    value_weight,
    w_out,
    gain_two,
    w_router,
    w_gate,
    w_up,
    w_down,
    cotangent,
):
    nc, nr, ndp = lax.axis_size("col"), lax.axis_size("row"), lax.axis_size("dp")
    ci, ri, di = lax.axis_index("col"), lax.axis_index("row"), lax.axis_index("dp")
    rows, feat = block_input.shape
    width = feat * nc
    share = rows // nc
    group = rows * nr
    experts, _, hid = w_gate.shape
    halves = 2
    half = di % halves
    local = experts // (nc * halves)
    q_width = w_query.shape[1]
    kv_width = key_weight.shape[1]
    q_heads = q_width // HEAD_SIZE
    kv_heads = kv_width // HEAD_SIZE
    score_scale = 1.0 / math.sqrt(HEAD_SIZE)

    orders = deal_order[0]
    _, positions = places(orders, lengths[0])

    def dealt(a):
        return a.reshape(nr, nc, share).transpose(1, 0, 2).reshape(nc, nr * share)

    orders_all, positions_all = dealt(orders), dealt(positions)
    key_orders = orders_all.reshape(group, 1)
    row_orders = pick(orders_all, ci)[None, :]
    row_positions = pick(positions_all, ci)
    row_starts = row_orders - row_positions[None, :]
    cosine_table, sine_table = rope_tables(row_positions)

    ride = 16
    gain_rows = jnp.concatenate(
        [jnp.stack([first_gain, gain_two]), jnp.zeros((ride - 2, feat), BF)], axis=0
    )
    sent = jnp.concatenate(
        [
            block_input.reshape(nc, share, feat),
            jnp.broadcast_to(gain_rows[None], (nc, ride, feat)),
        ],
        axis=1,
    )
    (got,) = exchange(1, (sent, "col", "major", "lane"))
    got = got.astype(F32)
    x_tok, gains = got[:share], got[share : share + 2]
    inv_one = lax.rsqrt(jnp.mean(x_tok * x_tok, axis=1, keepdims=True) + NORM_EPSILON)
    x_hat = x_tok * inv_one
    w_mine = jnp.concatenate([w_query, key_weight, value_weight], axis=1)
    first_part = max(1, 3 * local // 5)
    bounds = ((0, first_part), (first_part, local))

    def spread(w, part):
        low, high = bounds[part]
        return (w, "col", ("spread", low, local, high - low), "major")

    def to_row(block):
        return (block, "row", ("swap", 2), None)

    def to_core(block):
        return (block, "row", ("swap", 1), None)

    def to_pair(block):
        return (block, "dp", ("swap", 1), None)

    normed, w_qkv, dy_own = exchange(
        2,
        ((x_hat * gains[0]).astype(BF), "row", "all", "major"),
        (w_mine, "col", "shared", "major"),
        (cotangent, "col", "all", "lane"),
    )
    normed = normed.reshape(nr * share, width)
    w_qkv = w_qkv.reshape(width, w_mine.shape[1])

    qkv = dot(w_qkv, normed, ((0,), (1,)))
    count = nr * share
    queries = (rotate(qkv[:q_width], cosine_table, sine_table) * score_scale).astype(BF)
    keys = rotate(qkv[q_width : q_width + kv_width], cosine_table, sine_table).astype(BF)
    values = qkv[q_width + kv_width :].astype(BF)
    tail = jnp.pad(w_router, ((0, 0), (0, 128 - experts)))
    pairs, w_tail, gate_own, dy_pair = exchange(
        3,
        (jnp.concatenate([keys, values], axis=0), "col", "all", "lane"),
        (jnp.concatenate([w_out.T, tail], axis=1), "col", "shared", "major"),
        spread(w_gate, 0),
        to_pair(dy_own),
    )
    w_tail = w_tail.reshape(width, -1)
    w_out_t = w_tail[:, : w_out.shape[0]]
    router = w_tail[:, w_out.shape[0] : w_out.shape[0] + experts]
    mixed, lse, (down_own, gate_row, dy_core, dy_both) = attend(
        4,
        queries,
        pairs,
        key_orders,
        row_orders,
        row_starts,
        kv_heads,
        spread(w_down, 0),
        to_row(gate_own),
        to_core(dy_own),
        to_core(dy_pair),
    )
    dys = [dy_own, dy_core, dy_pair, dy_both]
    branch, up_own = exchange(
        5,
        (
            dot(mixed, w_out_t, ((0,), (1,))).astype(BF).reshape(nr, share, width),
            "row",
            "major",
            "major",
        ),
        spread(w_up, 0),
    )
    hidden = x_tok + block_sum(branch)
    inv_two = lax.rsqrt(jnp.mean(hidden * hidden, axis=1, keepdims=True) + NORM_EPSILON)
    hidden_hat = hidden * inv_two
    normed_two = (hidden_hat * gains[1]).astype(BF)

    own_routes = [
        lax.dynamic_slice_in_dim(routes, ri * rows, rows),
        lax.dynamic_slice_in_dim(routes, (ri ^ 1) * rows, rows),
    ]
    rows_of, (down_row, up_row, down_own_b) = gather_pass(
        6, normed_two, to_row(down_own), to_row(up_own), spread(w_down, 1)
    )
    pair_routes = swap(jnp.stack(own_routes), "dp", 1)
    first_expert = (half * nc + ci) * local
    lanes = 128

    def padded_gates(tokens, chosen):
        return jnp.pad(dense_gates(tokens, router, chosen), ((0, 0), (0, lanes - experts)))

    gate_rows = jnp.concatenate(
        [
            padded_gates(tokens, chosen)
            for tokens, chosen in zip(rows_of, own_routes + [pair_routes[0], pair_routes[1]])
        ]
    )
    marks = (
        jnp.arange(lanes, dtype=jnp.int32)[None, :]
        == first_expert + jnp.arange(local, dtype=jnp.int32)[:, None]
    ).astype(F32)

    def experts_of(number, part, blocks, *more):
        cut_at = slice(bounds[part][0], bounds[part][1])
        return expert_pass(number, rows_of, dys, gate_rows, marks[cut_at], *blocks, *more)

    last = first_part - 1
    outs_a, d_ins_a, made_a, (gate_own_b, up_own_b, down_row_b, gate_row_b, up_row_b) = experts_of(
        7,
        0,
        ([gate_own, gate_row], [up_own, up_row], [down_own, down_row]),
        [spread(w_gate, 1), spread(w_up, 1), to_row(down_own_b)],
        ((0, min(1, last)), (1, min(2, last))),
    )
    outs_b, d_ins_b, made_b, (down_came, gate_came) = experts_of(
        8,
        1,
        ([gate_own_b, gate_row_b], [up_own_b, up_row_b], [down_own_b, down_row_b]),
        [to_row(made_a[2][1]), to_row(made_a[0][1])],
    )

    def over_col(block, came, tensor):
        return (add_low(block, came), "col", "major" if tensor == 2 else "second", "major")

    def both_halves(*pairs_of):
        first = [jnp.where(half == 0, mine, other) for mine, other in pairs_of]
        second = [jnp.where(half == 0, other, mine) for mine, other in pairs_of]
        whole = jnp.stack([jnp.concatenate(first, 1), jnp.concatenate(second, 1)]).astype(F32)
        return whole.reshape((experts,) + whole.shape[3:])

    d_sum, (down_a, up_came, down_came_b) = scatter_pass(
        9,
        (d_ins_a, d_ins_b),
        over_col(made_a[2][0], down_came, 2),
        to_row(made_a[1][1]),
        to_row(made_b[2][1]),
    )
    down_a = pair_sums(down_a)
    d_sum = block_sum(d_sum)

    chosen = lax.dynamic_slice_in_dim(own_routes[0], ci * share, share)
    gates = dense_gates(normed_two, router, chosen)
    d_gates = d_sum[:, width : width + experts]
    d_logits = (gates * (d_gates - jnp.sum(gates * d_gates, axis=1, keepdims=True))).astype(BF)
    d_router = tn(jnp.pad(d_logits, ((0, 0), (0, 48 - experts))), normed_two).astype(BF)
    d_normed_two = d_sum[:, :width] + nt(d_logits, router)
    dy_tok = lax.dynamic_slice_in_dim(dy_own, ci * share, share).astype(F32)
    d_hat_two = d_normed_two * gains[1]
    d_gain_two = jnp.sum(d_normed_two * hidden_hat, axis=0)
    inner_two = jnp.mean(d_hat_two * hidden_hat, axis=1, keepdims=True)
    d_hidden = dy_tok + inv_two * (d_hat_two - hidden_hat * inner_two)

    d_branch, gate_a, down_a2, gate_came_b = exchange(
        10,
        (d_hidden.astype(BF), "row", "all", "major"),
        over_col(made_a[0][0], gate_came, 0),
        to_pair(down_a),
        to_row(made_b[0][1]),
    )
    gate_a = pair_sums(gate_a)
    d_branch = d_branch.reshape(count, width)
    d_mixed = dot(w_out_t, d_branch, ((0,), (1,))).astype(BF)
    d_query, d_pairs, (up_a, gate_a2, up_came_b) = attend_back(
        11,
        queries,
        d_mixed,
        lse,
        pairs,
        key_orders,
        row_orders,
        row_starts,
        kv_heads,
        over_col(made_a[1][0], up_came, 1),
        to_pair(gate_a),
        to_row(made_b[1][1]),
    )
    up_a = pair_sums(up_a)
    kv_parts, router_parts, down_b, up_a2 = exchange(
        12,
        (d_pairs, "col", "lane", "major"),
        (d_router, "col", "lane", "major"),
        over_col(made_b[2][0], down_came_b, 2),
        to_pair(up_a),
    )
    down_b = pair_sums(down_b)

    def wide(a):
        return a.astype(F32)

    core_outs = [swap(add_low(outs_a[i], outs_b[i]), "row", 1) for i in (1, 3)]
    pair_out = swap((wide(outs_a[2]) + wide(outs_b[2]) + wide(core_outs[1])).astype(BF), "dp", 1)
    kv_grads = block_sum(kv_parts)
    d_query = rotate(d_query * score_scale, cosine_table, -sine_table).astype(BF)
    d_key = rotate(kv_grads[:kv_width], cosine_table, -sine_table).astype(BF)
    d_qkv = jnp.concatenate([d_query, d_key, kv_grads[kv_width:].astype(BF)], axis=0)
    d_parts, router_parts, gate_b, down_b2 = exchange(
        13,
        (
            dot(d_qkv, w_qkv, ((0,), (1,))).astype(BF).reshape(nr, share, width),
            "row",
            "major",
            "major",
        ),
        (block_sum(router_parts).astype(BF), "row", "all", "major"),
        over_col(made_b[0][0], gate_came_b, 0),
        to_pair(down_b),
    )
    gate_b = pair_sums(gate_b)
    d_w_qkv = weight_sum(dot(normed, d_qkv, ((0,), (1,))).astype(BF), half)
    d_w_out = weight_sum(dot(d_branch, mixed, ((0,), (1,))).astype(BF), half).T
    d_normed = block_sum(d_parts)
    d_hat = d_normed * gains[0]
    d_gain_one = jnp.sum(d_normed * x_hat, axis=0)
    inner_one = jnp.mean(d_hat * x_hat, axis=1, keepdims=True)
    d_input_tok = d_hidden + inv_one * (d_hat - x_hat * inner_one)
    gain_parts = jnp.stack([d_gain_one, d_gain_two]).reshape(2, nc, feat).transpose(1, 0, 2)
    gain_parts = jnp.broadcast_to(gain_parts[None], (ndp * nr, nc, 2, feat)).reshape(-1, 2, feat)
    d_input, gain_parts, router_parts, up_b, gate_b2 = exchange(
        14,
        (d_input_tok.astype(BF), "col", "lane", "major"),
        (gain_parts, "world", "major", "major"),
        (block_sum(router_parts).astype(BF), "dp", "all", "major"),
        over_col(made_b[1][0], up_came_b, 1),
        to_pair(gate_b),
    )
    up_b = pair_sums(up_b)
    d_input = d_input.reshape(rows, feat).astype(F32)
    d_gains = block_sum(gain_parts)
    d_router = block_sum(router_parts)[:experts].T

    own = (jnp.arange(nc) == ci)[:, None, None]
    out_part = (
        wide(outs_a[0]) + wide(outs_b[0]) + wide(core_outs[0]) + wide(pair_out)
    ).reshape(nc, share, width) + jnp.where(own, hidden[None], 0.0)
    out_part = out_part.astype(BF).reshape(rows, nc, feat).transpose(1, 0, 2)
    block_output = col_scatter(out_part.reshape(nc * rows, feat))

    up_b2 = swap(up_b, "dp", 1)
    d_w_down = both_halves((down_a, down_a2), (down_b, down_b2))
    d_w_gate = both_halves((gate_a, gate_a2), (gate_b, gate_b2))
    d_w_up = both_halves((up_a, up_a2), (up_b, up_b2))
    return (
        block_output,
        d_input,
        d_gains[0],
        d_w_qkv[:, :q_width],
        d_w_qkv[:, q_width : q_width + kv_width],
        d_w_qkv[:, q_width + kv_width :],
        d_w_out,
        d_gains[1],
        d_router,
        d_w_gate,
        d_w_up,
        d_w_down,
    )


def solution(mesh):
    residual = P(("dp", "row"), "col")
    return jax.shard_map(
        body,
        mesh=mesh,
        in_specs=(
            residual,
            P("dp", None),
            P("dp", None),
            P("dp", None),
            P("col"),
            P("col", "row"),
            P("col", "row"),
            P("col", "row"),
            P("row", "col"),
            P("col"),
            P("col", None),
            P(None, "col", "row"),
            P(None, "col", "row"),
            P(None, "row", "col"),
            residual,
        ),
        out_specs=(
            residual,
            residual,
            P("col"),
            P("col", "row"),
            P("col", "row"),
            P("col", "row"),
            P("row", "col"),
            P("col"),
            P("col", None),
            P(None, "col", "row"),
            P(None, "col", "row"),
            P(None, "row", "col"),
        ),
        check_vma=False,
    )
```

```python
import functools
import math

import jax
import jax.numpy as jnp
from jax import lax
from jax.experimental import pallas as pl
from jax.experimental.pallas import tpu as pltpu
from jax.sharding import PartitionSpec as P

HEAD_SIZE = 64
TOPK = 8
NORM_EPSILON = 1e-06
THETA = 10000.0
FILLER = -1e30
BF = jnp.bfloat16
F32 = jnp.float32


def dot(a, b, dims):
    return lax.dot_general(a, b, (dims, ((), ())), preferred_element_type=F32)


def nn(a, b):
    return dot(a, b, ((1,), (0,)))


def nt(a, b):
    return dot(a, b, ((1,), (1,)))


def tn(a, b):
    return dot(a, b, ((0,), (0,)))


def rope_tables(positions):
    half_head = HEAD_SIZE // 2
    frequency = THETA ** (-(2.0 / HEAD_SIZE) * jnp.arange(half_head).astype(F32))
    angles = positions.astype(F32)[None, :] * frequency[:, None]
    return (jnp.cos(angles), jnp.sin(angles))


def rotate(vector, cosine_table, sine_table):
    half_head = HEAD_SIZE // 2
    parts = vector.reshape(-1, HEAD_SIZE, vector.shape[1])
    first, second = parts[:, :half_head], parts[:, half_head:]
    return jnp.concatenate(
        [
            first * cosine_table - second * sine_table,
            second * cosine_table + first * sine_table,
        ],
        axis=1,
    ).reshape(vector.shape)


def places(orders, lengths):
    ends = jnp.cumsum(lengths)
    starts = ends - lengths
    inside = ((orders[:, None] >= starts[None, :]) & (orders[:, None] < ends[None, :])).astype(
        jnp.int32
    )
    seq_ids = jnp.sum(inside * jnp.arange(lengths.shape[0], dtype=jnp.int32)[None, :], axis=1)
    positions = orders - jnp.sum(inside * starts[None, :], axis=1)
    return (seq_ids, positions)


def swap(operand, axis, bit):
    n = lax.axis_size(axis)
    return lax.ppermute(operand, axis, [(i, i ^ bit) for i in range(n)])


MESH_ID = pl.DeviceIdType.MESH


def cut(ref, how, index, size):
    if how == "all":
        return ref
    if how == "major":
        return ref.at[index]
    return ref.at[:, pl.ds(pl.multiple_of(index * size, 128), size)]


WORLD = ("dp", "row", "col")
HBM = pl.BlockSpec(memory_space=pl.ANY)
FREE = pl.CostEstimate(flops=1024, bytes_accessed=1024, transcendentals=0)


def size_of(axis):
    return lax.axis_size(WORLD) if axis == "world" else lax.axis_size(axis)


def place_of(axis):
    return lax.axis_index(WORLD) if axis == "world" else lax.axis_index(axis)


def at_place(axis, index):
    if axis != "world":
        return {axis: index}
    nr, nc = lax.axis_size("row"), lax.axis_size("col")
    return {"dp": index // (nr * nc), "row": index // nc % nr, "col": index % nc}


def two_step(plan):
    axis, src, _, n, _ = plan
    return axis == "row" and src == "all" and n == 4


def partners(plans):
    found = []
    for plan in plans:
        axis, src, _, n, _ = plan
        if src[0] == "swap":
            ways = [(axis, src[1])]
        elif src == "pair":
            ways = [("dp", 1)]
        else:
            ways = [(axis, k) for k in range(1, 3 if two_step(plan) else n)]
        if src == "shared":
            ways.append(("dp", 1))
        found += [way for way in ways if way not in found]
    if any(axis == "world" for axis, _ in found):
        found = [way for way in found if way[0] == "world"]
    return found


def greet(ways):
    barrier = pltpu.get_barrier_semaphore()
    for axis, k in ways:
        peer = at_place(axis, place_of(axis) ^ k)
        pl.semaphore_signal(barrier, inc=1, device_id=peer, device_id_type=MESH_ID)
    pl.semaphore_wait(barrier, len(ways))


def remote(src, dst, sems, at, device):
    return pltpu.make_async_remote_copy(
        src_ref=src,
        dst_ref=dst,
        send_sem=sems[0].at[at],
        recv_sem=sems[1].at[at],
        device_id=device,
        device_id_type=MESH_ID,
    )


def slots_of(plan):
    _, src, _, n, _ = plan
    if src[0] == "swap" or src == "pair":
        return 1
    return 2 * (n - 1) if src == "shared" else n - 1


class Move:
    def __init__(self, plan, x, out, sems, base, which, buffer):
        axis, src, dst, n, _ = plan
        i, di = place_of(axis), place_of("dp")
        self.near, self.back, self.far, self.relays = [], [], [], []

        def near(source, target):
            self.near.append(pltpu.make_async_copy(source, buffer, sems[2].at[which]))
            self.back.append(pltpu.make_async_copy(buffer, target, sems[2].at[which]))

        def far(source, target, device):
            at = base + len(self.far) + len(self.relays)
            return remote(source, target, sems, at, device)

        if src[0] == "swap":
            self.far.append(far(x, out, at_place(axis, i ^ src[1])))
        elif src == "pair":
            near(x, out.at[di % 2])
            self.far.append(far(x, out.at[di % 2], {"dp": di ^ 1}))
        elif src == "shared":
            part = x.shape[0] // 2
            half = pl.ds(pl.multiple_of(di % 2 * part, part), part)
            near(x, out.at[i])
            for k in range(1, n):
                self.far.append(far(x.at[half], out.at[i, half], at_place(axis, i ^ k)))
            for k in range(1, n):
                block = out.at[i ^ k, half]
                self.relays.append((self.far[k - 1], far(block, block, {"dp": di ^ 1})))
        elif src[0] == "spread":
            first, local, count = src[1:]

            def block(c):
                return x.at[pl.ds((di % 2 * n + c) * local + first, count)]

            near(block(i), out.at[i])
            for k in range(1, n):
                self.far.append(far(block(i ^ k), out.at[i], at_place(axis, i ^ k)))
        elif src == "second":
            size = x.shape[1] // n

            def cols(c):
                return x.at[:, pl.ds(pl.multiple_of(c * size, size), size)]

            near(cols(i), out.at[i])
            for k in range(1, n):
                self.far.append(far(cols(i ^ k), out.at[i], at_place(axis, i ^ k)))
        else:
            in_size, out_size = x.shape[-1] // n, out.shape[-1] // n
            near(cut(x, src, i, in_size), cut(out, dst, i, out_size))
            for k in range(1, 3 if two_step(plan) else n):
                self.far.append(
                    far(
                        cut(x, src, i ^ k, in_size),
                        cut(out, dst, i, out_size),
                        at_place(axis, i ^ k),
                    )
                )
            if two_step(plan):
                block = out.at[i ^ 2]
                self.relays.append((self.far[1], far(block, block, {"row": i ^ 1})))

    def start(self):
        for copy in self.far + self.near:
            copy.start()

    def relay(self):
        for copy, back in zip(self.near, self.back):
            copy.wait()
            back.start()
        for came, onward in self.relays:
            came.wait_recv()
            onward.start()

    def finish(self):
        passed = [came for came, _ in self.relays]
        for copy in self.back:
            copy.wait()
        for copy in self.far:
            if any(copy is came for came in passed):
                copy.wait_send()
            else:
                copy.wait()
        for _, onward in self.relays:
            onward.wait()


def moves_in(plans, ins, outs, sems):
    made, base, buffers = [], 0, list(sems[3:])
    for which, plan in enumerate(plans):
        buffer = None if plan[4] is None else buffers.pop(0)
        made.append(Move(plan, ins[which], outs[which], sems, base, which, buffer))
        base += slots_of(plan)
    return made


def finish_all(moves):
    for move in moves:
        move.relay()
    for move in moves:
        move.finish()


def planned(moves):
    plans, shapes = [], []
    for operand, axis, src, dst in moves:
        n = 2 if src == "pair" else size_of(axis)
        shape = operand.shape
        if src[0] == "swap":
            plans.append((axis, src, dst, n, None))
            shapes.append(jax.ShapeDtypeStruct(shape, operand.dtype))
            continue
        if src[0] == "spread":
            shape = (src[3],) + shape[1:]
        elif src == "second":
            shape = shape[:1] + (shape[1] // n,) + shape[2:]
        elif src == "major":
            shape = shape[1:]
        elif src == "lane":
            shape = shape[:-1] + (shape[-1] // n,)
        plans.append((axis, src, dst, n, (shape, operand.dtype)))
        if dst == "major":
            shape = (n,) + shape
        else:
            shape = shape[:-1] + (shape[-1] * n,)
        shapes.append(jax.ShapeDtypeStruct(shape, operand.dtype))
    return plans, shapes


def move_sems(plans):
    count = sum(slots_of(plan) for plan in plans)
    return [
        pltpu.SemaphoreType.DMA((count,)),
        pltpu.SemaphoreType.DMA((count,)),
        pltpu.SemaphoreType.DMA((len(plans),)),
    ] + [pltpu.VMEM(*plan[4]) for plan in plans if plan[4] is not None]


def exchange_kernel(plans, *refs):
    count = len(plans)
    greet(partners(plans))
    moves = moves_in(plans, refs[:count], refs[count : 2 * count], refs[2 * count :])
    for move in moves:
        move.start()
    finish_all(moves)


def exchange(number, *moves):
    plans, shapes = planned(moves)
    return pl.pallas_call(
        functools.partial(exchange_kernel, plans),
        out_shape=shapes,
        in_specs=[HBM] * len(plans),
        out_specs=[HBM] * len(plans),
        scratch_shapes=move_sems(plans),
        compiler_params=pltpu.CompilerParams(collective_id=number, has_side_effects=True),
        cost_estimate=FREE,
    )(*[move[0] for move in moves])


def gather_pass_kernel(nc, plans, *refs):
    count = len(plans)
    x_ref, ins, refs = refs[0], refs[1 : 1 + count], refs[1 + count :]
    own, core, pair, both = refs[:4]
    outs, refs = refs[4 : 4 + count], refs[4 + count :]
    sems, near_sem, move_sem = refs[:2], refs[2], refs[3:]
    ci, ri, di = lax.axis_index("col"), lax.axis_index("row"), lax.axis_index("dp")
    to_core, to_pair = {"row": ri ^ 1}, {"dp": di ^ 1}
    ways = [("col", k) for k in range(1, nc)] + [("row", 1), ("dp", 1)]
    greet(ways + [way for way in partners(plans) if way not in ways])

    def send(way, k, src, dst, device):
        copy = remote(src, dst, (sems[0].at[way], sems[1].at[way]), k, device)
        copy.start()
        return copy

    near = pltpu.make_async_copy(x_ref, own.at[ci], near_sem)
    near.start()
    far = [send(0, k, x_ref, own.at[ci], {"col": ci ^ k}) for k in range(1, nc)]
    moves = moves_in(plans, ins, outs, move_sem)
    for move in moves:
        move.start()
    paired, cored, waits = [], [], []
    for k in range(nc):
        if k > 0:
            far[k - 1].wait_recv()
            waits.append(far[k - 1].wait_send)
        block = x_ref if k == 0 else own.at[ci ^ k]
        paired.append(send(1, k, block, pair.at[ci ^ k], to_pair))
        cored.append(send(2, k, block, core.at[ci ^ k], to_core))
    for k in range(nc):
        paired[k].wait_recv()
        waits.append(paired[k].wait_send)
        waits.append(cored[k].wait)
        waits.append(send(3, k, pair.at[ci ^ k], both.at[ci ^ k], to_core).wait)
    waits.append(near.wait)
    for wait in waits:
        wait()
    finish_all(moves)


def gather_pass(number, x, *moves):
    nc = lax.axis_size("col")
    plans, shapes = planned(moves)
    made = jax.ShapeDtypeStruct((nc,) + x.shape, x.dtype)
    got = pl.pallas_call(
        functools.partial(gather_pass_kernel, nc, plans),
        out_shape=[made] * 4 + shapes,
        in_specs=[pl.BlockSpec(memory_space=pltpu.VMEM)] + [HBM] * len(plans),
        out_specs=[HBM] * (4 + len(plans)),
        scratch_shapes=[pltpu.SemaphoreType.DMA((4, nc))] * 2
        + [pltpu.SemaphoreType.DMA]
        + move_sems(plans),
        compiler_params=pltpu.CompilerParams(collective_id=number, has_side_effects=True),
        cost_estimate=FREE,
    )(x, *[move[0] for move in moves])
    got = list(got)
    return [block.reshape(nc * x.shape[0], x.shape[1]) for block in got[:4]], got[4:]


def scatter_pass_kernel(nc, parts, plans, *refs):
    count = len(plans)
    ins, refs = refs[: 4 * parts], refs[4 * parts :]
    move_ins, out_ref, move_outs = refs[:count], refs[count], refs[count + 1 : 2 * count + 1]
    made, came, total, send_sem, recv_sem = refs[2 * count + 1 : 2 * count + 6]
    move_sem = refs[2 * count + 6 :]
    ci, ri, di = lax.axis_index("col"), lax.axis_index("row"), lax.axis_index("dp")
    to_core, to_pair = {"row": ri ^ 1}, {"dp": di ^ 1}
    ways = [("col", k) for k in range(1, nc)] + [("row", 1), ("dp", 1)]
    greet(ways + [way for way in partners(plans) if way not in ways])
    moves = moves_in(plans, move_ins, move_outs, move_sem)
    for move in moves:
        move.start()
    order = list(range(1, nc)) + [0]

    def send(way, k, src, dst, device):
        copy = remote(src, dst, (send_sem.at[way], recv_sem.at[way]), k, device)
        copy.start()
        return copy

    def added(which, at, *more):
        value = ins[which][at].astype(F32)
        for p in range(1, parts):
            value = value + ins[4 * p + which][at].astype(F32)
        for other in more:
            value = value + came[other, at].astype(F32)
        return value.astype(BF)

    sent = {}
    for k in order:
        at = ci ^ k
        for way, which in ((0, 3), (1, 1)):
            made[way, at] = added(which, at)
            sent[way, k] = send(way, k, made.at[way, at], came.at[way, at], to_core)
    for k in order:
        at = ci ^ k
        sent[0, k].wait_recv()
        made[2, at] = added(2, at, 0)
        sent[2, k] = send(2, k, made.at[2, at], came.at[2, at], to_pair)
    for k in order:
        at = ci ^ k
        sent[1, k].wait_recv()
        sent[2, k].wait_recv()
        total[at] = added(0, at, 1, 2)
        if k > 0:
            sent[3, k] = send(3, k, total.at[at], out_ref.at[ci], {"col": at})
    out_ref[ci] = total[ci]
    for way in range(3):
        for k in order:
            sent[way, k].wait_send()
    for k in range(1, nc):
        sent[3, k].wait()
    finish_all(moves)


def scatter_pass(number, parts, *moves):
    nc = lax.axis_size("col")
    plans, shapes = planned(moves)
    rows, width = parts[0][0].shape
    shape = (nc, rows // nc, width)
    vmem = pl.BlockSpec(memory_space=pltpu.VMEM)
    got = pl.pallas_call(
        functools.partial(scatter_pass_kernel, nc, len(parts), plans),
        out_shape=[jax.ShapeDtypeStruct(shape, BF)] + shapes,
        in_specs=[vmem] * (4 * len(parts)) + [HBM] * len(plans),
        out_specs=[vmem] + [HBM] * len(plans),
        scratch_shapes=[
            pltpu.VMEM((3,) + shape, BF),
            pltpu.VMEM((3,) + shape, BF),
            pltpu.VMEM(shape, BF),
            pltpu.SemaphoreType.DMA((4, nc)),
            pltpu.SemaphoreType.DMA((4, nc)),
        ]
        + move_sems(plans),
        compiler_params=pltpu.CompilerParams(
            collective_id=number, has_side_effects=True, vmem_limit_bytes=48 * 2**20
        ),
        cost_estimate=FREE,
    )(*[block.reshape(shape) for part in parts for block in part], *[move[0] for move in moves])
    return got[0], list(got[1:])


def block_sum(stack):
    return jnp.sum(stack.astype(F32), axis=0)


def col_gather(operand):
    return lax.all_gather(operand, "col", axis=0, tiled=True)


def col_scatter(operand):
    return lax.psum_scatter(operand, "col", scatter_dimension=0, tiled=True)


def pick(stack, index):
    return lax.dynamic_index_in_dim(stack, index, 0, keepdims=False)


def add_low(first, second):
    return (first.astype(F32) + second.astype(F32)).astype(BF)


def pair_sums(operand):
    ndp = lax.axis_size("dp")
    if ndp == 2:
        return operand
    return lax.psum(operand, "dp", axis_index_groups=[list(range(h, ndp, 2)) for h in range(2)])


def weight_sum(operand, half):
    nc = lax.axis_size("col")
    parts = operand.reshape(nc, 2, -1, operand.shape[1]).transpose(1, 0, 2, 3)
    mine = add_low(pick(parts, half), swap(pick(parts, 1 - half), "dp", 1))
    mine = pair_sums(col_scatter(mine.reshape(-1, operand.shape[1])))
    other = swap(mine, "dp", 1)
    first = jnp.where(half == 0, mine, other)
    second = jnp.where(half == 0, other, mine)
    return jnp.concatenate([first, second]).astype(F32)


def widen_kernel(parts, *refs):
    low = 0
    for ref in refs[:parts]:
        refs[parts][0, low : low + ref.shape[1]] = ref[0].astype(F32)
        low += ref.shape[1]


def widen(*stacks):
    blocks = [stack.reshape((-1,) + stack.shape[2:]) for stack in stacks]
    count = sum(block.shape[1] for block in blocks)
    shape = (blocks[0].shape[0], count) + blocks[0].shape[2:]

    def spec(block):
        return pl.BlockSpec((1,) + block[1:], lambda i: (i, 0, 0, 0))

    out = pl.pallas_call(
        functools.partial(widen_kernel, len(blocks)),
        grid=(shape[0],),
        out_shape=jax.ShapeDtypeStruct(shape, F32),
        in_specs=[spec(block.shape) for block in blocks],
        out_specs=spec(shape),
        compiler_params=pltpu.CompilerParams(vmem_limit_bytes=16 * 2**20),
    )(*blocks)
    return out.reshape((-1,) + shape[2:])


def dense_gates(normed, router, routes):
    experts = router.shape[1]
    logits = nn(normed, router)
    chosen = jnp.any(
        routes[:, :, None] == jnp.arange(experts, dtype=jnp.int32)[None, None, :], axis=1
    )
    top = jnp.max(jnp.where(chosen, logits, FILLER), axis=1, keepdims=True)
    weights = jnp.where(chosen, jnp.exp(jnp.where(chosen, logits - top, 0.0)), 0.0)
    return weights / jnp.sum(weights, axis=1, keepdims=True)


def bias_into(bias, key_ref, row_ref, start_ref, chunk):
    @pl.loop(0, bias.shape[0] // chunk)
    def _(c):
        at = pl.ds(pl.multiple_of(c * chunk, chunk), chunk)
        keys = key_ref[at, :]
        seen = (keys <= row_ref[...]) & (keys >= start_ref[...])
        bias[at, :] = jnp.where(seen, 0.0, FILLER)


def attend_kernel(tile, kv_heads, plans, *refs):
    count = len(plans)
    q_ref, kv_ref, key_ref, row_ref, start_ref = refs[:5]
    ins, refs = refs[5 : 5 + count], refs[5 + count :]
    o_ref, lse_ref = refs[:2]
    outs, refs = refs[2 : 2 + count], refs[2 + count :]
    bias, k_s, sems = refs[0], refs[1], refs[2:]
    greet(partners(plans))
    moves = moves_in(plans, ins, outs, sems)
    for move in moves:
        move.start()
    size = HEAD_SIZE
    heads = q_ref.shape[0] // size
    per = heads // kv_heads
    rows = q_ref.shape[1]
    bias_into(bias, key_ref, row_ref, start_ref, 256)
    for g in range(kv_heads):
        k_s[g] = kv_ref[g * size : (g + 1) * size, :].T

    @pl.loop(0, heads)
    def _(h):
        g = h // per
        at = pl.ds(pl.multiple_of(h * size, size), size)
        v_at = pl.ds(pl.multiple_of((kv_heads + g) * size, size), size)
        for t in range(rows // tile):
            cut = slice(t * tile, (t + 1) * tile)
            scores = nn(k_s[g], q_ref[at, cut]) + bias[:, cut]
            top = jnp.max(scores, axis=0, keepdims=True)
            weights = jnp.exp(scores - top)
            total = jnp.sum(weights, axis=0, keepdims=True)
            chances = (weights * (1.0 / total)).astype(BF)
            o_ref[at, cut] = nn(kv_ref[v_at, :], chances).astype(BF)
            lse_ref[h, :, cut] = top + jnp.log(total)

    finish_all(moves)


def attend(number, q, kv, keys, rows_at, starts, kv_heads, *moves):
    plans, shapes = planned(moves)
    heads, count = q.shape[0] // HEAD_SIZE, q.shape[1]
    group = kv.shape[1]
    vmem = pl.BlockSpec(memory_space=pltpu.VMEM)
    got = pl.pallas_call(
        functools.partial(attend_kernel, min(256, count), kv_heads, plans),
        out_shape=[
            jax.ShapeDtypeStruct(q.shape, BF),
            jax.ShapeDtypeStruct((heads, 1, count), F32),
        ]
        + shapes,
        in_specs=[vmem] * 5 + [HBM] * len(plans),
        out_specs=[vmem] * 2 + [HBM] * len(plans),
        scratch_shapes=[
            pltpu.VMEM((group, count), F32),
            pltpu.VMEM((kv_heads, group, HEAD_SIZE), BF),
        ]
        + move_sems(plans),
        compiler_params=pltpu.CompilerParams(
            collective_id=number, has_side_effects=True, vmem_limit_bytes=48 * 2**20
        ),
        cost_estimate=FREE,
    )(q, kv, keys, rows_at, starts, *[move[0] for move in moves])
    return got[0], got[1], list(got[2:])


def attend_back_kernel(tile, kv_heads, plans, *refs):
    count = len(plans)
    q_ref, do_ref, lse_ref, kv_ref, key_ref, row_ref, start_ref = refs[:7]
    ins, refs = refs[7 : 7 + count], refs[7 + count :]
    dq_ref, dkv_ref = refs[:2]
    outs, refs = refs[2 : 2 + count], refs[2 + count :]
    bias, k_s, v_s, dk_s, dv_s = refs[:5]
    greet(partners(plans))
    moves = moves_in(plans, ins, outs, refs[5:])
    for move in moves:
        move.start()
    size = HEAD_SIZE
    heads = q_ref.shape[0] // size
    per = heads // kv_heads
    rows = q_ref.shape[1]
    bias_into(bias, key_ref, row_ref, start_ref, 256)
    for g in range(kv_heads):
        k_s[g] = kv_ref[g * size : (g + 1) * size, :].T
        v_s[g] = kv_ref[(kv_heads + g) * size : (kv_heads + g + 1) * size, :].T
    dk_s[...] = jnp.zeros_like(dk_s)
    dv_s[...] = jnp.zeros_like(dv_s)

    @pl.loop(0, heads)
    def _(h):
        g = h // per
        at = pl.ds(pl.multiple_of(h * size, size), size)
        k_at = pl.ds(pl.multiple_of(g * size, size), size)
        for t in range(rows // tile):
            cut = slice(t * tile, (t + 1) * tile)
            q_part, do_part = q_ref[at, cut], do_ref[at, cut]
            scores = nn(k_s[g], q_part) + bias[:, cut]
            probs = jnp.exp(scores - lse_ref[h, :, cut])
            d_chances = nn(v_s[g], do_part)
            dv_s[g] += nt(probs.astype(BF), do_part)
            both = probs * d_chances
            d_scores = (both - probs * jnp.sum(both, axis=0, keepdims=True)).astype(BF)
            dk_s[g] += nt(d_scores, q_part)
            dq_ref[at, cut] = nn(kv_ref[k_at, :], d_scores)

    for g in range(kv_heads):
        dkv_ref[g * size : (g + 1) * size, :] = dk_s[g].T.astype(BF)
        dkv_ref[(kv_heads + g) * size : (kv_heads + g + 1) * size, :] = dv_s[g].T.astype(BF)
    finish_all(moves)


def attend_back(number, q, do, lse, kv, keys, rows_at, starts, kv_heads, *moves):
    plans, shapes = planned(moves)
    count = q.shape[1]
    group = kv.shape[1]
    vmem = pl.BlockSpec(memory_space=pltpu.VMEM)
    got = pl.pallas_call(
        functools.partial(attend_back_kernel, min(256, count), kv_heads, plans),
        out_shape=[jax.ShapeDtypeStruct(q.shape, F32), jax.ShapeDtypeStruct(kv.shape, BF)]
        + shapes,
        in_specs=[vmem] * 7 + [HBM] * len(plans),
        out_specs=[vmem] * 2 + [HBM] * len(plans),
        scratch_shapes=[
            pltpu.VMEM((group, count), F32),
            pltpu.VMEM((kv_heads, group, HEAD_SIZE), BF),
            pltpu.VMEM((kv_heads, group, HEAD_SIZE), BF),
            pltpu.VMEM((kv_heads, group, HEAD_SIZE), F32),
            pltpu.VMEM((kv_heads, group, HEAD_SIZE), F32),
        ]
        + move_sems(plans),
        compiler_params=pltpu.CompilerParams(
            collective_id=number, has_side_effects=True, vmem_limit_bytes=56 * 2**20
        ),
        cost_estimate=FREE,
    )(q, do, lse, kv, keys, rows_at, starts, *[move[0] for move in moves])
    return got[0], got[1], list(got[2:])


def expert_kernel(sets, nb, tile, plans, onward, *refs):
    x_refs, dy_refs = refs[:sets], refs[sets : 2 * sets]
    mark_ref, refs = refs[2 * sets], refs[2 * sets + 1 :]
    wg, wu, wd = refs[:nb], refs[nb : 2 * nb], refs[2 * nb : 3 * nb]
    refs = refs[3 * nb :]
    count = len(plans) - len(onward)
    move_ins, refs = list(refs[:count]), refs[count:]
    outs, dxs = refs[:sets], refs[sets : 2 * sets]
    refs = refs[2 * sets :]
    dwg, dwu, dwd = refs[:nb], refs[nb : 2 * nb], refs[2 * nb : 3 * nb]
    refs = refs[3 * nb :]
    move_outs, refs = refs[: len(plans)], refs[len(plans) :]
    w_in, w_out, xt, act_s, dgu_s = refs[:5]
    move_ins += [move_outs[which] for which, _ in onward]
    moves = moves_in(plans, move_ins, move_outs, refs[5:])
    done = [which for which, _ in onward]
    nc, _, feat, hid = wg[0].shape
    wide = nb * hid
    width = nc * feat
    e = pl.program_id(0)
    rows = x_refs[0].shape[0]

    @pl.when(e == 0)
    def _():
        greet(partners(plans))
        for move in moves[:count]:
            move.start()

    for later, (which, step) in enumerate(onward):

        @pl.when(e == step)
        def _():
            finish_all([moves[which]])
            moves[count + later].start()

    for j in range(nb):
        for c in range(nc):
            w_in[c * feat : (c + 1) * feat, j * hid : (j + 1) * hid] = wg[j][c, 0]
            w_in[c * feat : (c + 1) * feat, wide + j * hid : wide + (j + 1) * hid] = wu[j][c, 0]
            w_out[j * hid : (j + 1) * hid, c * feat : (c + 1) * feat] = wd[j][c, 0]

    @pl.when(e == 0)
    def _():
        for h in range(sets):
            outs[h][...] = jnp.zeros_like(outs[h])
            dxs[h][...] = jnp.zeros_like(dxs[h])
            for c in range(nc):
                cut_at = slice(c * feat, (c + 1) * feat)
                xt[cut_at, h * rows : (h + 1) * rows] = x_refs[h][:, cut_at].T

    mark, both_marks = mark_ref[0, pl.ds(e, 1), :], mark_ref[1, pl.ds(e, 1), :]
    for h in range(sets):
        x_ref, dy_ref, out_ref, dx_ref = x_refs[h], dy_refs[h], outs[h], dxs[h]

        @pl.loop(0, rows // tile)
        def _(t):
            at = pl.ds(pl.multiple_of(t * tile, tile), tile)
            here = pl.ds(pl.multiple_of(h * rows + t * tile, tile), tile)
            gu = nn(x_ref[at, :width], w_in[...])
            d_act = nt(dy_ref[at, :], w_out[...])
            gate = jnp.sum(x_ref[at, width:].astype(F32) * both_marks, axis=1, keepdims=True)
            spread = jnp.broadcast_to(gate, (tile, hid))
            total = None
            for j in range(nb):
                lo = j * hid
                g = gu[:, lo : lo + hid]
                u = gu[:, wide + lo : wide + lo + hid]
                da = d_act[:, lo : lo + hid]
                sig = 1.0 / (1.0 + jnp.exp(-g))
                swish = g * sig
                su = swish * u
                act_s[here, lo : lo + hid] = (su * spread).astype(BF)
                part = da * su
                total = part if total is None else total + part
                mid = da * spread
                dgu_s[here, lo : lo + hid] = (mid * u * (sig * (1.0 + g * (1.0 - sig)))).astype(BF)
                dgu_s[here, wide + lo : wide + lo + hid] = (mid * swish).astype(BF)
            d_gate = jnp.sum(total, axis=1, keepdims=True) * mark
            dx_ref[at, width:] = (dx_ref[at, width:].astype(F32) + d_gate).astype(BF)
            out_ref[at, :] = (out_ref[at, :].astype(F32) + nn(act_s[here, :], w_out[...])).astype(BF)
            dx_ref[at, :width] = (
                dx_ref[at, :width].astype(F32) + nt(dgu_s[here, :], w_in[...])
            ).astype(BF)

    @pl.loop(0, nc)
    def _(c):
        at = pl.ds(pl.multiple_of(c * feat, feat), feat)
        made = nn(xt[at, :], dgu_s[...])
        for j in range(nb):
            dwg[j][0, at, :] = made[:, j * hid : (j + 1) * hid].astype(BF)
            dwu[j][0, at, :] = made[:, wide + j * hid : wide + (j + 1) * hid].astype(BF)

    made = None
    for h in range(sets):
        part = tn(act_s[h * rows : (h + 1) * rows, :], dy_refs[h][...])
        made = part if made is None else made + part
    for j in range(nb):
        for c in range(nc):
            dwd[j][c, 0] = made[j * hid : (j + 1) * hid, c * feat : (c + 1) * feat].astype(BF)

    @pl.when(e == pl.num_programs(0) - 1)
    def _():
        finish_all([move for which, move in enumerate(moves) if which not in done])


def expert_pass(number, xs, dys, marks, wg, wu, wd, moves, onward=(), tile=512):
    plans, shapes = planned(moves)
    for which, _ in onward:
        plans.append(("row", ("swap", 2), None, size_of("row"), None))
        shapes.append(shapes[which])
    rows, width = dys[0].shape
    sets, nb = len(xs), len(wg)
    nc, local, feat, hid = wg[0].shape
    wide = nb * hid
    lanes = marks.shape[2]
    tile = min(tile, rows)

    def whole(shape):
        return pl.BlockSpec(shape, lambda e: (0,) * len(shape), pipeline_mode=pl.Buffered(1))

    up_spec = pl.BlockSpec((nc, 1, feat, hid), lambda e: (0, e, 0, 0))
    down_spec = pl.BlockSpec((nc, 1, hid, feat), lambda e: (0, e, 0, 0))
    made = pl.pallas_call(
        functools.partial(expert_kernel, sets, nb, tile, plans, onward),
        grid=(local,),
        in_specs=[whole((rows, width + lanes))] * sets
        + [whole((rows, width))] * sets
        + [whole(marks.shape)]
        + [up_spec] * (2 * nb)
        + [down_spec] * nb
        + [HBM] * len(moves),
        out_specs=[whole((rows, width))] * sets
        + [whole((rows, width + lanes))] * sets
        + [pl.BlockSpec((1, width, hid), lambda e: (e, 0, 0))] * (2 * nb)
        + [down_spec] * nb
        + [HBM] * len(plans),
        out_shape=[jax.ShapeDtypeStruct((rows, width), BF)] * sets
        + [jax.ShapeDtypeStruct((rows, width + lanes), BF)] * sets
        + [jax.ShapeDtypeStruct((local, width, hid), BF)] * (2 * nb)
        + [jax.ShapeDtypeStruct((nc, local, hid, feat), BF)] * nb
        + shapes,
        scratch_shapes=[
            pltpu.VMEM((width, 2 * wide), BF),
            pltpu.VMEM((wide, width), BF),
            pltpu.VMEM((width, sets * rows), BF),
            pltpu.VMEM((sets * rows, wide), BF),
            pltpu.VMEM((sets * rows, 2 * wide), BF),
        ]
        + move_sems(plans),
        compiler_params=pltpu.CompilerParams(
            collective_id=number, has_side_effects=True, vmem_limit_bytes=60 * 2**20
        ),
        cost_estimate=FREE,
    )(*xs, *dys, marks, *wg, *wu, *wd, *[move[0] for move in moves])
    made = list(made)
    outs, dxs, made = made[:sets], made[sets : 2 * sets], made[2 * sets :]
    return outs, dxs, [made[:nb], made[nb : 2 * nb], made[2 * nb : 3 * nb]], made[3 * nb :]


def body(
    block_input,
    deal_order,
    lengths,
    routes,
    first_gain,
    w_query,
    key_weight,
    value_weight,
    w_out,
    gain_two,
    w_router,
    w_gate,
    w_up,
    w_down,
    cotangent,
):
    nc, nr, ndp = lax.axis_size("col"), lax.axis_size("row"), lax.axis_size("dp")
    ci, ri, di = lax.axis_index("col"), lax.axis_index("row"), lax.axis_index("dp")
    rows, feat = block_input.shape
    width = feat * nc
    share = rows // nc
    group = rows * nr
    experts, _, hid = w_gate.shape
    halves = 2
    half = di % halves
    local = experts // (nc * halves)
    q_width = w_query.shape[1]
    kv_width = key_weight.shape[1]
    q_heads = q_width // HEAD_SIZE
    kv_heads = kv_width // HEAD_SIZE
    score_scale = 1.0 / math.sqrt(HEAD_SIZE)

    orders = deal_order[0]
    _, positions = places(orders, lengths[0])

    def dealt(a):
        return a.reshape(nr, nc, share).transpose(1, 0, 2).reshape(nc, nr * share)

    orders_all, positions_all = dealt(orders), dealt(positions)
    key_orders = orders_all.reshape(group, 1)
    row_orders = pick(orders_all, ci)[None, :]
    row_positions = pick(positions_all, ci)
    row_starts = row_orders - row_positions[None, :]
    cosine_table, sine_table = rope_tables(row_positions)

    ride = 16
    gain_rows = jnp.concatenate(
        [jnp.stack([first_gain, gain_two]), jnp.zeros((ride - 2, feat), BF)], axis=0
    )
    sent = jnp.concatenate(
        [
            block_input.reshape(nc, share, feat),
            jnp.broadcast_to(gain_rows[None], (nc, ride, feat)),
        ],
        axis=1,
    )
    (got,) = exchange(1, (sent, "col", "major", "lane"))
    got = got.astype(F32)
    x_tok, gains = got[:share], got[share : share + 2]
    inv_one = lax.rsqrt(jnp.mean(x_tok * x_tok, axis=1, keepdims=True) + NORM_EPSILON)
    x_hat = x_tok * inv_one
    w_mine = jnp.concatenate([w_query, key_weight, value_weight], axis=1)
    first_part = max(1, 3 * local // 5)
    bounds = ((0, first_part), (first_part, local))

    def spread(w, part):
        low, high = bounds[part]
        return (w, "col", ("spread", low, local, high - low), "major")

    def to_row(block):
        return (block, "row", ("swap", 2), None)

    def to_core(block):
        return (block, "row", ("swap", 1), None)

    def to_pair(block):
        return (block, "dp", ("swap", 1), None)

    normed, w_qkv, dy_own = exchange(
        2,
        ((x_hat * gains[0]).astype(BF), "row", "all", "major"),
        (w_mine, "col", "shared", "major"),
        (cotangent, "col", "all", "lane"),
    )
    normed = normed.reshape(nr * share, width)
    w_qkv = w_qkv.reshape(width, w_mine.shape[1])

    qkv = dot(w_qkv, normed, ((0,), (1,)))
    count = nr * share
    queries = (rotate(qkv[:q_width], cosine_table, sine_table) * score_scale).astype(BF)
    keys = rotate(qkv[q_width : q_width + kv_width], cosine_table, sine_table).astype(BF)
    values = qkv[q_width + kv_width :].astype(BF)
    tail = jnp.pad(w_router, ((0, 0), (0, 128 - experts)))
    pairs, w_tail, gate_own, dy_pair = exchange(
        3,
        (jnp.concatenate([keys, values], axis=0), "col", "all", "lane"),
        (jnp.concatenate([w_out.T, tail], axis=1), "col", "shared", "major"),
        spread(w_gate, 0),
        to_pair(dy_own),
    )
    w_tail = w_tail.reshape(width, -1)
    w_out_t = w_tail[:, : w_out.shape[0]]
    router = w_tail[:, w_out.shape[0] : w_out.shape[0] + experts]
    mixed, lse, (down_own, gate_row, dy_core, dy_both) = attend(
        4,
        queries,
        pairs,
        key_orders,
        row_orders,
        row_starts,
        kv_heads,
        spread(w_down, 0),
        to_row(gate_own),
        to_core(dy_own),
        to_core(dy_pair),
    )
    dys = [dy_own, dy_core, dy_pair, dy_both]
    branch, up_own = exchange(
        5,
        (
            dot(mixed, w_out_t, ((0,), (1,))).astype(BF).reshape(nr, share, width),
            "row",
            "major",
            "major",
        ),
        spread(w_up, 0),
    )
    hidden = x_tok + block_sum(branch)
    inv_two = lax.rsqrt(jnp.mean(hidden * hidden, axis=1, keepdims=True) + NORM_EPSILON)
    hidden_hat = hidden * inv_two
    normed_two = (hidden_hat * gains[1]).astype(BF)

    lanes = 128
    own_routes = lax.dynamic_slice_in_dim(routes, ri * rows + ci * share, share)
    gates = dense_gates(normed_two, router, own_routes)
    high = gates.astype(BF)
    low = (gates - high.astype(F32)).astype(BF)
    gap = jnp.zeros((share, lanes // 2 - experts), BF)
    rows_of, (down_row, up_row, down_own_b) = gather_pass(
        6,
        jnp.concatenate([normed_two, high, gap, low, gap], axis=1),
        to_row(down_own),
        to_row(up_own),
        spread(w_down, 1),
    )
    first_expert = (half * nc + ci) * local
    places_of = first_expert + jnp.arange(local, dtype=jnp.int32)[:, None]
    lane = jnp.arange(lanes, dtype=jnp.int32)[None, :]
    marks = jnp.stack(
        [lane == places_of, (lane == places_of) | (lane == places_of + lanes // 2)]
    ).astype(F32)

    def experts_of(number, part, blocks, *more):
        cut_at = slice(bounds[part][0], bounds[part][1])
        return expert_pass(number, rows_of, dys, marks[:, cut_at], *blocks, *more)

    last = first_part - 1
    outs_a, d_ins_a, made_a, (gate_own_b, up_own_b, down_row_b, gate_row_b, up_row_b) = experts_of(
        7,
        0,
        ([gate_own, gate_row], [up_own, up_row], [down_own, down_row]),
        [spread(w_gate, 1), spread(w_up, 1), to_row(down_own_b)],
        ((0, min(1, last)), (1, min(2, last))),
    )
    outs_b, d_ins_b, made_b, (down_came,) = experts_of(
        8,
        1,
        ([gate_own_b, gate_row_b], [up_own_b, up_row_b], [down_own_b, down_row_b]),
        [to_row(made_a[2][1])],
    )

    def over_col(block, came, tensor):
        return (add_low(block, came), "col", "major" if tensor == 2 else "second", "major")

    def both(block):
        return (pair_sums(block), "dp", "pair", "major")

    d_sum, (down_a, gate_came, up_came) = scatter_pass(
        9,
        (d_ins_a, d_ins_b),
        over_col(made_a[2][0], down_came, 2),
        to_row(made_a[0][1]),
        to_row(made_a[1][1]),
    )
    d_sum = block_sum(d_sum)

    d_gates = d_sum[:, width : width + experts]
    d_logits = (gates * (d_gates - jnp.sum(gates * d_gates, axis=1, keepdims=True))).astype(BF)
    d_router = tn(jnp.pad(d_logits, ((0, 0), (0, 48 - experts))), normed_two).astype(BF)
    d_normed_two = d_sum[:, :width] + nt(d_logits, router)
    dy_tok = lax.dynamic_slice_in_dim(dy_own, ci * share, share).astype(F32)
    d_hat_two = d_normed_two * gains[1]
    d_gain_two = jnp.sum(d_normed_two * hidden_hat, axis=0)
    inner_two = jnp.mean(d_hat_two * hidden_hat, axis=1, keepdims=True)
    d_hidden = dy_tok + inv_two * (d_hat_two - hidden_hat * inner_two)

    def wide(a):
        return a.astype(F32)

    d_branch, gate_a, down_a, down_came_b = exchange(
        10,
        (d_hidden.astype(BF), "row", "all", "major"),
        over_col(made_a[0][0], gate_came, 0),
        both(down_a),
        to_row(made_b[2][1]),
    )
    d_branch = d_branch.reshape(count, width)
    d_mixed = dot(w_out_t, d_branch, ((0,), (1,))).astype(BF)
    d_mixed, outs_a, outs_b = lax.optimization_barrier((d_mixed, outs_a, outs_b))
    core_outs = [swap(add_low(outs_a[i], outs_b[i]), "row", 1) for i in (1, 3)]
    d_query, d_pairs, (up_a, gate_a, gate_came_b) = attend_back(
        11,
        queries,
        d_mixed,
        lse,
        pairs,
        key_orders,
        row_orders,
        row_starts,
        kv_heads,
        over_col(made_a[1][0], up_came, 1),
        both(gate_a),
        to_row(made_b[0][1]),
    )
    d_pairs, core_outs = lax.optimization_barrier((d_pairs, core_outs))
    pair_out = swap((wide(outs_a[2]) + wide(outs_b[2]) + wide(core_outs[1])).astype(BF), "dp", 1)
    kv_parts, router_parts, down_b, up_a, up_came_b = exchange(
        12,
        (d_pairs, "col", "lane", "major"),
        (d_router, "col", "lane", "major"),
        over_col(made_b[2][0], down_came_b, 2),
        both(up_a),
        to_row(made_b[1][1]),
    )
    kv_parts, pair_out = lax.optimization_barrier((kv_parts, pair_out))
    own = (jnp.arange(nc) == ci)[:, None, None]
    out_part = (
        wide(outs_a[0]) + wide(outs_b[0]) + wide(core_outs[0]) + wide(pair_out)
    ).reshape(nc, share, width) + jnp.where(own, hidden[None], 0.0)
    out_part = out_part.astype(BF).reshape(rows, nc, feat).transpose(1, 0, 2)
    block_output = col_scatter(out_part.reshape(nc * rows, feat))
    d_w_out = weight_sum(dot(d_branch, mixed, ((0,), (1,))).astype(BF), half).T
    kv_grads = block_sum(kv_parts)
    d_query = rotate(d_query * score_scale, cosine_table, -sine_table).astype(BF)
    d_key = rotate(kv_grads[:kv_width], cosine_table, -sine_table).astype(BF)
    d_qkv = jnp.concatenate([d_query, d_key, kv_grads[kv_width:].astype(BF)], axis=0)
    d_parts, router_parts, gate_b, down_b = exchange(
        13,
        (
            dot(d_qkv, w_qkv, ((0,), (1,))).astype(BF).reshape(nr, share, width),
            "row",
            "major",
            "major",
        ),
        (block_sum(router_parts).astype(BF), "row", "all", "major"),
        over_col(made_b[0][0], gate_came_b, 0),
        both(down_b),
    )
    d_w_qkv = weight_sum(dot(normed, d_qkv, ((0,), (1,))).astype(BF), half)
    d_normed = block_sum(d_parts)
    d_hat = d_normed * gains[0]
    d_gain_one = jnp.sum(d_normed * x_hat, axis=0)
    inner_one = jnp.mean(d_hat * x_hat, axis=1, keepdims=True)
    d_input_tok = d_hidden + inv_one * (d_hat - x_hat * inner_one)
    gain_parts = jnp.stack([d_gain_one, d_gain_two]).reshape(2, nc, feat).transpose(1, 0, 2)
    gain_parts = jnp.broadcast_to(gain_parts[None], (ndp * nr, nc, 2, feat)).reshape(-1, 2, feat)
    d_input, gain_parts, router_parts, up_b, gate_b = exchange(
        14,
        (d_input_tok.astype(BF), "col", "lane", "major"),
        (gain_parts, "world", "major", "major"),
        (block_sum(router_parts).astype(BF), "dp", "all", "major"),
        over_col(made_b[1][0], up_came_b, 1),
        both(gate_b),
    )
    (up_b,) = exchange(15, both(up_b))
    d_input = d_input.reshape(rows, feat).astype(F32)
    d_gains = block_sum(gain_parts)
    d_router = block_sum(router_parts)[:experts].T

    d_w_down = widen(down_a, down_b)
    d_w_gate = widen(gate_a, gate_b)
    d_w_up = widen(up_a, up_b)
    return (
        block_output,
        d_input,
        d_gains[0],
        d_w_qkv[:, :q_width],
        d_w_qkv[:, q_width : q_width + kv_width],
        d_w_qkv[:, q_width + kv_width :],
        d_w_out,
        d_gains[1],
        d_router,
        d_w_gate,
        d_w_up,
        d_w_down,
    )


def solution(mesh):
    residual = P(("dp", "row"), "col")
    return jax.shard_map(
        body,
        mesh=mesh,
        in_specs=(
            residual,
            P("dp", None),
            P("dp", None),
            P("dp", None),
            P("col"),
            P("col", "row"),
            P("col", "row"),
            P("col", "row"),
            P("row", "col"),
            P("col"),
            P("col", None),
            P(None, "col", "row"),
            P(None, "col", "row"),
            P(None, "row", "col"),
            residual,
        ),
        out_specs=(
            residual,
            residual,
            P("col"),
            P("col", "row"),
            P("col", "row"),
            P("col", "row"),
            P("row", "col"),
            P("col"),
            P("col", None),
            P(None, "col", "row"),
            P(None, "col", "row"),
            P(None, "row", "col"),
        ),
        check_vma=False,
    )
```

```python
import functools
import math

import jax
import jax.numpy as jnp
from jax import lax
from jax.experimental import pallas as pl
from jax.experimental.pallas import tpu as pltpu
from jax.sharding import PartitionSpec as P

HEAD_SIZE = 64
TOPK = 8
NORM_EPSILON = 1e-06
THETA = 10000.0
FILLER = -1e30
BF = jnp.bfloat16
F32 = jnp.float32


def dot(a, b, dims):
    return lax.dot_general(a, b, (dims, ((), ())), preferred_element_type=F32)


def nn(a, b):
    return dot(a, b, ((1,), (0,)))


def nt(a, b):
    return dot(a, b, ((1,), (1,)))


def tn(a, b):
    return dot(a, b, ((0,), (0,)))


def rope_tables(positions):
    half_head = HEAD_SIZE // 2
    frequency = THETA ** (-(2.0 / HEAD_SIZE) * jnp.arange(half_head).astype(F32))
    angles = positions.astype(F32)[None, :] * frequency[:, None]
    return (jnp.cos(angles), jnp.sin(angles))


def rotate(vector, cosine_table, sine_table):
    half_head = HEAD_SIZE // 2
    parts = vector.reshape(-1, HEAD_SIZE, vector.shape[1])
    first, second = parts[:, :half_head], parts[:, half_head:]
    return jnp.concatenate(
        [
            first * cosine_table - second * sine_table,
            second * cosine_table + first * sine_table,
        ],
        axis=1,
    ).reshape(vector.shape)


def places(orders, lengths):
    ends = jnp.cumsum(lengths)
    starts = ends - lengths
    inside = ((orders[:, None] >= starts[None, :]) & (orders[:, None] < ends[None, :])).astype(
        jnp.int32
    )
    seq_ids = jnp.sum(inside * jnp.arange(lengths.shape[0], dtype=jnp.int32)[None, :], axis=1)
    positions = orders - jnp.sum(inside * starts[None, :], axis=1)
    return (seq_ids, positions)


def swap(operand, axis, bit):
    n = lax.axis_size(axis)
    return lax.ppermute(operand, axis, [(i, i ^ bit) for i in range(n)])


MESH_ID = pl.DeviceIdType.MESH


def cut(ref, how, index, size):
    if how == "all":
        return ref
    if how == "major":
        return ref.at[index]
    return ref.at[:, pl.ds(pl.multiple_of(index * size, 128), size)]


WORLD = ("dp", "row", "col")
HBM = pl.BlockSpec(memory_space=pl.ANY)
FREE = pl.CostEstimate(flops=1024, bytes_accessed=1024, transcendentals=0)


def size_of(axis):
    return lax.axis_size(WORLD) if axis == "world" else lax.axis_size(axis)


def place_of(axis):
    return lax.axis_index(WORLD) if axis == "world" else lax.axis_index(axis)


def at_place(axis, index):
    if axis != "world":
        return {axis: index}
    nr, nc = lax.axis_size("row"), lax.axis_size("col")
    return {"dp": index // (nr * nc), "row": index // nc % nr, "col": index % nc}


def two_step(plan):
    axis, src, _, n, _ = plan
    return axis == "row" and src == "all" and n == 4


def partners(plans):
    found = []
    for plan in plans:
        axis, src, _, n, _ = plan
        if src[0] == "swap":
            ways = [(axis, src[1])]
        elif src == "pair":
            ways = [("dp", 1)]
        else:
            ways = [(axis, k) for k in range(1, 3 if two_step(plan) else n)]
        if src == "shared":
            ways.append(("dp", 1))
        found += [way for way in ways if way not in found]
    if any(axis == "world" for axis, _ in found):
        found = [way for way in found if way[0] == "world"]
    return found


def greet(ways):
    barrier = pltpu.get_barrier_semaphore()
    for axis, k in ways:
        peer = at_place(axis, place_of(axis) ^ k)
        pl.semaphore_signal(barrier, inc=1, device_id=peer, device_id_type=MESH_ID)
    pl.semaphore_wait(barrier, len(ways))


def remote(src, dst, sems, at, device):
    return pltpu.make_async_remote_copy(
        src_ref=src,
        dst_ref=dst,
        send_sem=sems[0].at[at],
        recv_sem=sems[1].at[at],
        device_id=device,
        device_id_type=MESH_ID,
    )


def slots_of(plan):
    _, src, _, n, _ = plan
    if src[0] == "swap" or src == "pair":
        return 1
    return 2 * (n - 1) if src == "shared" else n - 1


class Move:
    def __init__(self, plan, x, out, sems, base, which, buffer):
        axis, src, dst, n, _ = plan
        i, di = place_of(axis), place_of("dp")
        self.near, self.back, self.far, self.relays = [], [], [], []

        def near(source, target):
            self.near.append(pltpu.make_async_copy(source, buffer, sems[2].at[which]))
            self.back.append(pltpu.make_async_copy(buffer, target, sems[2].at[which]))

        def far(source, target, device):
            at = base + len(self.far) + len(self.relays)
            return remote(source, target, sems, at, device)

        if src[0] == "swap":
            self.far.append(far(x, out, at_place(axis, i ^ src[1])))
        elif src == "pair":
            near(x, out.at[di % 2])
            self.far.append(far(x, out.at[di % 2], {"dp": di ^ 1}))
        elif src == "shared":
            part = x.shape[0] // 2
            half = pl.ds(pl.multiple_of(di % 2 * part, part), part)
            near(x, out.at[i])
            for k in range(1, n):
                self.far.append(far(x.at[half], out.at[i, half], at_place(axis, i ^ k)))
            for k in range(1, n):
                block = out.at[i ^ k, half]
                self.relays.append((self.far[k - 1], far(block, block, {"dp": di ^ 1})))
        elif src[0] == "spread":
            first, local, count = src[1:]

            def block(c):
                return x.at[pl.ds((di % 2 * n + c) * local + first, count)]

            near(block(i), out.at[i])
            for k in range(1, n):
                self.far.append(far(block(i ^ k), out.at[i], at_place(axis, i ^ k)))
        elif src == "second":
            size = x.shape[1] // n

            def cols(c):
                return x.at[:, pl.ds(pl.multiple_of(c * size, size), size)]

            near(cols(i), out.at[i])
            for k in range(1, n):
                self.far.append(far(cols(i ^ k), out.at[i], at_place(axis, i ^ k)))
        else:
            in_size, out_size = x.shape[-1] // n, out.shape[-1] // n
            near(cut(x, src, i, in_size), cut(out, dst, i, out_size))
            for k in range(1, 3 if two_step(plan) else n):
                self.far.append(
                    far(
                        cut(x, src, i ^ k, in_size),
                        cut(out, dst, i, out_size),
                        at_place(axis, i ^ k),
                    )
                )
            if two_step(plan):
                block = out.at[i ^ 2]
                self.relays.append((self.far[1], far(block, block, {"row": i ^ 1})))

    def start(self):
        for copy in self.far + self.near:
            copy.start()

    def relay(self):
        for copy, back in zip(self.near, self.back):
            copy.wait()
            back.start()
        for came, onward in self.relays:
            came.wait_recv()
            onward.start()

    def finish(self):
        passed = [came for came, _ in self.relays]
        for copy in self.back:
            copy.wait()
        for copy in self.far:
            if any(copy is came for came in passed):
                copy.wait_send()
            else:
                copy.wait()
        for _, onward in self.relays:
            onward.wait()


def moves_in(plans, ins, outs, sems):
    made, base, buffers = [], 0, list(sems[3:])
    for which, plan in enumerate(plans):
        buffer = None if plan[4] is None else buffers.pop(0)
        made.append(Move(plan, ins[which], outs[which], sems, base, which, buffer))
        base += slots_of(plan)
    return made


def finish_all(moves):
    for move in moves:
        move.relay()
    for move in moves:
        move.finish()


def planned(moves):
    plans, shapes = [], []
    for operand, axis, src, dst in moves:
        n = 2 if src == "pair" else size_of(axis)
        shape = operand.shape
        if src[0] == "swap":
            plans.append((axis, src, dst, n, None))
            shapes.append(jax.ShapeDtypeStruct(shape, operand.dtype))
            continue
        if src[0] == "spread":
            shape = (src[3],) + shape[1:]
        elif src == "second":
            shape = shape[:1] + (shape[1] // n,) + shape[2:]
        elif src == "major":
            shape = shape[1:]
        elif src == "lane":
            shape = shape[:-1] + (shape[-1] // n,)
        plans.append((axis, src, dst, n, (shape, operand.dtype)))
        if dst == "major":
            shape = (n,) + shape
        else:
            shape = shape[:-1] + (shape[-1] * n,)
        shapes.append(jax.ShapeDtypeStruct(shape, operand.dtype))
    return plans, shapes


def move_sems(plans):
    count = sum(slots_of(plan) for plan in plans)
    return [
        pltpu.SemaphoreType.DMA((count,)),
        pltpu.SemaphoreType.DMA((count,)),
        pltpu.SemaphoreType.DMA((len(plans),)),
    ] + [pltpu.VMEM(*plan[4]) for plan in plans if plan[4] is not None]


def exchange_kernel(plans, *refs):
    count = len(plans)
    greet(partners(plans))
    moves = moves_in(plans, refs[:count], refs[count : 2 * count], refs[2 * count :])
    for move in moves:
        move.start()
    finish_all(moves)


def exchange(number, *moves):
    plans, shapes = planned(moves)
    return pl.pallas_call(
        functools.partial(exchange_kernel, plans),
        out_shape=shapes,
        in_specs=[HBM] * len(plans),
        out_specs=[HBM] * len(plans),
        scratch_shapes=move_sems(plans),
        compiler_params=pltpu.CompilerParams(collective_id=number, has_side_effects=True),
        cost_estimate=FREE,
    )(*[move[0] for move in moves])


def gather_pass_kernel(nc, plans, *refs):
    count = len(plans)
    x_ref, ins, refs = refs[0], refs[1 : 1 + count], refs[1 + count :]
    own, core, pair, both = refs[:4]
    outs, refs = refs[4 : 4 + count], refs[4 + count :]
    sems, near_sem, move_sem = refs[:2], refs[2], refs[3:]
    ci, ri, di = lax.axis_index("col"), lax.axis_index("row"), lax.axis_index("dp")
    to_core, to_pair = {"row": ri ^ 1}, {"dp": di ^ 1}
    ways = [("col", k) for k in range(1, nc)] + [("row", 1), ("dp", 1)]
    greet(ways + [way for way in partners(plans) if way not in ways])

    def send(way, k, src, dst, device):
        copy = remote(src, dst, (sems[0].at[way], sems[1].at[way]), k, device)
        copy.start()
        return copy

    near = pltpu.make_async_copy(x_ref, own.at[ci], near_sem)
    near.start()
    far = [send(0, k, x_ref, own.at[ci], {"col": ci ^ k}) for k in range(1, nc)]
    moves = moves_in(plans, ins, outs, move_sem)
    for move in moves:
        move.start()
    paired, cored, waits = [], [], []
    for k in range(nc):
        if k > 0:
            far[k - 1].wait_recv()
            waits.append(far[k - 1].wait_send)
        block = x_ref if k == 0 else own.at[ci ^ k]
        paired.append(send(1, k, block, pair.at[ci ^ k], to_pair))
        cored.append(send(2, k, block, core.at[ci ^ k], to_core))
    for k in range(nc):
        paired[k].wait_recv()
        waits.append(paired[k].wait_send)
        waits.append(cored[k].wait)
        waits.append(send(3, k, pair.at[ci ^ k], both.at[ci ^ k], to_core).wait)
    waits.append(near.wait)
    for wait in waits:
        wait()
    finish_all(moves)


def gather_pass(number, x, *moves):
    nc = lax.axis_size("col")
    plans, shapes = planned(moves)
    made = jax.ShapeDtypeStruct((nc,) + x.shape, x.dtype)
    got = pl.pallas_call(
        functools.partial(gather_pass_kernel, nc, plans),
        out_shape=[made] * 4 + shapes,
        in_specs=[pl.BlockSpec(memory_space=pltpu.VMEM)] + [HBM] * len(plans),
        out_specs=[HBM] * (4 + len(plans)),
        scratch_shapes=[pltpu.SemaphoreType.DMA((4, nc))] * 2
        + [pltpu.SemaphoreType.DMA]
        + move_sems(plans),
        compiler_params=pltpu.CompilerParams(collective_id=number, has_side_effects=True),
        cost_estimate=FREE,
    )(x, *[move[0] for move in moves])
    got = list(got)
    return [block.reshape(nc * x.shape[0], x.shape[1]) for block in got[:4]], got[4:]


def scatter_pass_kernel(nc, parts, plans, *refs):
    count = len(plans)
    ins, more_ins, refs = refs[: 4 * parts], refs[4 * parts : 8 * parts], refs[8 * parts :]
    move_ins, out_ref, part_ref = refs[:count], refs[count], refs[count + 1]
    refs = refs[count + 2 :]
    move_outs, refs = refs[:count], refs[count:]
    made, came, more_made, more_came, total, send_sem, recv_sem = refs[:7]
    ci, ri, di = lax.axis_index("col"), lax.axis_index("row"), lax.axis_index("dp")
    to_core, to_pair = {"row": ri ^ 1}, {"dp": di ^ 1}
    ways = [("col", k) for k in range(1, nc)] + [("row", 1), ("dp", 1)]
    greet(ways + [way for way in partners(plans) if way not in ways])
    moves = moves_in(plans, move_ins, move_outs, refs[7:])
    for move in moves:
        move.start()
    order = list(range(1, nc)) + [0]

    def send(way, k, src, dst, device):
        copy = remote(src, dst, (send_sem.at[way], recv_sem.at[way]), k, device)
        copy.start()
        return copy

    def added(from_refs, from_came, which, at, *more):
        value = from_refs[which][at].astype(F32)
        for p in range(1, parts):
            value = value + from_refs[4 * p + which][at].astype(F32)
        for other in more:
            value = value + from_came[other, at].astype(F32)
        return value.astype(BF)

    groups = ((ins, made, came, 0), (more_ins, more_made, more_came, 4))
    sent = {}
    for from_refs, to_made, to_came, base in groups:
        for k in order:
            at = ci ^ k
            for way, which in ((0, 3), (1, 1)):
                to_made[way, at] = added(from_refs, to_came, which, at)
                sent[base + way, k] = send(
                    base + way, k, to_made.at[way, at], to_came.at[way, at], to_core
                )
    for from_refs, to_made, to_came, base in groups:
        for k in order:
            at = ci ^ k
            sent[base, k].wait_recv()
            to_made[2, at] = added(from_refs, to_came, 2, at, 0)
            sent[base + 2, k] = send(base + 2, k, to_made.at[2, at], to_came.at[2, at], to_pair)
    for from_refs, to_made, to_came, base in groups:
        for k in order:
            at = ci ^ k
            sent[base + 1, k].wait_recv()
            sent[base + 2, k].wait_recv()
            if base:
                part_ref[at] = added(from_refs, to_came, 0, at, 1, 2)
                continue
            total[at] = added(from_refs, to_came, 0, at, 1, 2)
            if k > 0:
                sent[3, k] = send(3, k, total.at[at], out_ref.at[ci], {"col": at})
    out_ref[ci] = total[ci]
    for _, _, _, base in groups:
        for way in range(3):
            for k in order:
                sent[base + way, k].wait_send()
    for k in range(1, nc):
        sent[3, k].wait()
    finish_all(moves)


def scatter_pass(number, parts, more, *moves):
    nc = lax.axis_size("col")
    plans, shapes = planned(moves)
    rows, width = parts[0][0].shape
    shape = (nc, rows // nc, width)
    more_shape = (nc, rows // nc, more[0][0].shape[1])
    vmem = pl.BlockSpec(memory_space=pltpu.VMEM)
    got = pl.pallas_call(
        functools.partial(scatter_pass_kernel, nc, len(parts), plans),
        out_shape=[jax.ShapeDtypeStruct(shape, BF), jax.ShapeDtypeStruct(more_shape, BF)] + shapes,
        in_specs=[vmem] * (8 * len(parts)) + [HBM] * len(plans),
        out_specs=[vmem] * 2 + [HBM] * len(plans),
        scratch_shapes=[
            pltpu.VMEM((3,) + shape, BF),
            pltpu.VMEM((3,) + shape, BF),
            pltpu.VMEM((3,) + more_shape, BF),
            pltpu.VMEM((3,) + more_shape, BF),
            pltpu.VMEM(shape, BF),
            pltpu.SemaphoreType.DMA((7, nc)),
            pltpu.SemaphoreType.DMA((7, nc)),
        ]
        + move_sems(plans),
        compiler_params=pltpu.CompilerParams(
            collective_id=number, has_side_effects=True, vmem_limit_bytes=61 * 2**20
        ),
        cost_estimate=FREE,
    )(
        *[block.reshape(shape) for part in parts for block in part],
        *[block.reshape(more_shape) for part in more for block in part],
        *[move[0] for move in moves],
    )
    return got[0], got[1], list(got[2:])


def rotated(first, second, cosine, sine):
    return first * cosine - second * sine, second * cosine + first * sine


def back_kernel(names, sizes, *refs):
    r = dict(zip(names, refs))
    nc, nr, ndp, kv_heads, counts = sizes
    ci, ri, di = lax.axis_index("col"), lax.axis_index("row"), lax.axis_index("dp")
    me = place_of("world")
    world = nc * nr * ndp
    half = di % 2
    share, width = r["hidden"].shape
    feat = width // nc
    count = nr * share
    size = HEAD_SIZE
    q_rows = r["q"].shape[0]
    heads = q_rows // size
    per = heads // kv_heads
    kv_rows = kv_heads * size
    used = [0, 0]

    def send(src, dst, device):
        copy = remote(src, dst, (r["send"], r["recv"]), used[0], device)
        used[0] += 1
        copy.start()
        return copy

    def load(src, dst):
        copy = pltpu.make_async_copy(src, dst, r["near"].at[used[1]])
        used[1] += 1
        copy.start()
        return copy

    waits = []

    def lanes_of(c):
        return pl.ds(pl.multiple_of(c * feat, feat), feat)

    def over_col(dst, block):
        return [send(block(ci ^ k), dst.at[ci], {"col": ci ^ k}) for k in range(1, nc)]

    greet([("world", k) for k in range(1, world)])

    pending = {}

    def add_and_send(tensor, part, buffer):
        name = tensor + "_" + part
        own, came = r["own_" + name], r["came_" + name]
        n = counts[part]
        total = r[buffer].at[:, :n] if tensor == "down" else r[buffer].at[:n]
        other = r["add_down" if tensor == "down" else "add_up"]
        other = other.at[:, :n] if tensor == "down" else other.at[:n]
        loads = [load(own, total), load(came, other)]
        for copy in loads:
            copy.wait()
        if tensor == "down":
            for c in range(nc):
                for i in range(n):
                    total[c, i] = (total[c, i].astype(F32) + other[c, i].astype(F32)).astype(BF)
        else:

            @pl.loop(0, nc)
            def _(c):
                for i in range(n):
                    total[i, lanes_of(c)] = (
                        total[i, lanes_of(c)].astype(F32) + other[i, lanes_of(c)].astype(F32)
                    ).astype(BF)

        out = r["out_" + name]
        out = out.at[half] if ndp == 2 else out

        def block(c):
            return total.at[c] if tensor == "down" else total.at[:, lanes_of(c)]

        copies = over_col(out, block)
        near = load(block(ci), out.at[ci])
        pending[name] = (copies, near, out)

    def over_dp(name):
        copies, near, out = pending[name]
        for copy in copies:
            copy.wait()
        near.wait()
        if ndp == 2:
            waits.append(send(out, out, {"dp": di ^ 1}).wait)

    add_and_send("gate", "a", "sum_up_0")
    if ndp == 2:
        own = r["in_down_a"]
        mine = r["out_down_a"].at[half]
        first_load = load(own, r["sum_down"])
        waits.append(send(own, mine, {"dp": di ^ 1}).wait)

    d_sum = r["d_parts"][0].astype(F32)
    for c in range(1, nc):
        d_sum = d_sum + r["d_parts"][c].astype(F32)
    hidden = r["hidden"][...]
    g_one, g_two = r["gains"][0:1, :], r["gains"][1:2, :]
    inv_two = lax.rsqrt(jnp.mean(hidden * hidden, axis=1, keepdims=True) + NORM_EPSILON)
    hat_two = hidden * inv_two
    normed_two = (hat_two * g_two).astype(BF)
    gates = r["gates"][...]
    d_gates = d_sum[:, width:]
    d_logits = (gates * (d_gates - jnp.sum(gates * d_gates, axis=1, keepdims=True))).astype(BF)
    r["rt"][...] = tn(d_logits, normed_two)[: r["rt"].shape[0]].astype(BF)
    d_normed = d_sum[:, :width] + nt(d_logits, r["router"][...])
    gain_two = jnp.sum(d_normed * hat_two, axis=0, keepdims=True)
    r["gain_send"][...] = jnp.zeros_like(r["gain_send"])
    chunks = feat // 128

    def put_gain(gain, low):
        for c in range(nc):
            for j in range(chunks):
                at = c * feat + j * 128
                r["gain_send"][c, low + j : low + j + 1, :] = gain[:, at : at + 128]

    put_gain(gain_two, chunks)
    d_hat = d_normed * g_two
    inner = jnp.mean(d_hat * hat_two, axis=1, keepdims=True)
    d_hidden = r["dy"][...].astype(F32) + inv_two * (d_hat - hat_two * inner)
    r["dh"][...] = d_hidden
    branch = r["branch"]
    branch[ri] = d_hidden.astype(BF)
    mine = branch.at[ri]
    to_core = send(mine, mine, {"row": ri ^ 1})
    to_other = send(mine, mine, {"row": ri ^ 2})
    rowed = {}
    for name in ("down_b", "gate_b", "up_b"):
        rowed[name] = send(r["go_" + name], r["came_" + name], {"row": ri ^ 2})
    add_and_send("up", "a", "sum_up_1")
    if ndp == 2:
        first_load.wait()
        first_store = load(r["sum_down"], r["out_down_a"].at[half])
    to_other.wait_recv()
    block = branch.at[ri ^ 2]
    passed = send(block, block, {"row": ri ^ 1})
    bias, k_s, v_s, dk_s, dv_s = r["bias"], r["k_s"], r["v_s"], r["dk_s"], r["dv_s"]
    bias_into(bias, r["key_orders"], r["row_orders"], r["row_starts"], 256)
    kv = r["kv"]
    for g in range(kv_heads):
        k_s[g] = kv[g * size : (g + 1) * size, :].T
        v_s[g] = kv[kv_rows + g * size : kv_rows + (g + 1) * size, :].T
    dk_s[...] = jnp.zeros_like(dk_s)
    dv_s[...] = jnp.zeros_like(dv_s)
    to_core.wait()
    to_other.wait_send()
    passed.wait()
    for row in range(nr):
        r["do"][:, row * share : (row + 1) * share] = nt(r["w_out"][...], branch[row]).astype(BF)

    tile = min(256, count)

    def heads_part(low, high):
        @pl.loop(low, high)
        def _(h):
            g = h // per
            at = pl.ds(pl.multiple_of(h * size, size), size)
            k_at = pl.ds(pl.multiple_of(g * size, size), size)
            for t in range(count // tile):
                cut_at = slice(t * tile, (t + 1) * tile)
                q_part, do_part = r["q"][at, cut_at], r["do"][at, cut_at]
                scores = nn(k_s[g], q_part) + bias[:, cut_at]
                probs = jnp.exp(scores - r["lse"][h, :, cut_at])
                d_chances = nn(v_s[g], do_part)
                dv_s[g] += nt(probs.astype(BF), do_part)
                both = probs * d_chances
                d_scores = (both - probs * jnp.sum(both, axis=0, keepdims=True)).astype(BF)
                dk_s[g] += nt(d_scores, q_part)
                r["dq"][at, cut_at] = nn(kv[k_at, :], d_scores)

    heads_part(0, heads // 2)
    over_dp("gate_a")
    rowed["down_b"].wait()
    if ndp == 2:
        first_store.wait()
    add_and_send("down", "b", "sum_down")
    heads_part(heads // 2, heads)
    for g in range(kv_heads):
        r["dkv"][g * size : (g + 1) * size, :] = dk_s[g].T.astype(BF)
        r["dkv"][kv_rows + g * size : kv_rows + (g + 1) * size, :] = dv_s[g].T.astype(BF)

    def part_of(c):
        return r["dkv"].at[:, pl.ds(pl.multiple_of(c * count, count), count)]

    kv_copies = over_col(r["kv_came"], part_of)
    kv_near = load(part_of(ci), r["kv_came"].at[ci])
    rt_copies = over_col(r["rt_came"], lambda c: r["rt"].at[:, lanes_of(c)])
    rt_near = load(r["rt"].at[:, lanes_of(ci)], r["rt_came"].at[ci])
    other_half = 1 - half
    branches = branch[...].reshape(count, width)
    q_half = q_rows // 2
    w_half = r["w_keep"].shape[0]

    def halves_of(lhs, rows_half, rhs, came):
        for which, name in ((other_half, "w_go"), (half, "w_keep")):
            at = pl.ds(pl.multiple_of(which * rows_half, rows_half), rows_half)
            r[name][:rows_half] = nn(lhs[at, :], rhs).astype(BF)
        return send(r["w_go"].at[:rows_half], r[came], {"dp": di ^ 1})

    def halves_sum(copy, rows_half, came, out):
        copy.wait()
        total = r["w_keep"].at[:rows_half]
        total[...] = (total[...].astype(F32) + r[came][...].astype(F32)).astype(BF)
        copies = over_col(r[out], lambda c: total.at[:, lanes_of(c)])
        near = load(total.at[:, lanes_of(ci)], r[out].at[ci])
        return copies + [near]

    out_copy = halves_of(r["mixed"], q_half, branches, "came_w_out")
    rowed["gate_b"].wait()
    add_and_send("gate", "b", "sum_up_0")
    over_dp("up_a")
    for copy in kv_copies + [kv_near]:
        copy.wait()
    grads = r["kv_came"][0].astype(F32)
    for c in range(1, nc):
        grads = grads + r["kv_came"][c].astype(F32)
    cosine, sine = r["cosine"][...], -r["sine"][...]
    scale = 1.0 / math.sqrt(size)
    hop = size // 2
    for h in range(heads):
        a = r["dq"][h * size : h * size + hop, :] * scale
        b = r["dq"][h * size + hop : (h + 1) * size, :] * scale
        a, b = rotated(a, b, cosine, sine)
        r["dqkv"][h * size : h * size + hop, :] = a.astype(BF)
        r["dqkv"][h * size + hop : (h + 1) * size, :] = b.astype(BF)
    for g in range(kv_heads):
        a, b = rotated(
            grads[g * size : g * size + hop], grads[g * size + hop : (g + 1) * size], cosine, sine
        )
        low = q_rows + g * size
        r["dqkv"][low : low + hop, :] = a.astype(BF)
        r["dqkv"][low + hop : low + size, :] = b.astype(BF)
    r["dqkv"][q_rows + kv_rows :, :] = grads[kv_rows:].astype(BF)
    r["turned"][...] = r["dqkv"][...].T
    parts, parts_came = r["dn"], r["dn_came"]
    row_copies = []
    for k in (2, 3, 1, 0):
        at = ri ^ k
        rows_at = pl.ds(pl.multiple_of(at * share, share), share)
        parts[at] = nt(r["turned"][rows_at, :], r["w_qkv"][...]).astype(BF)
        if k > 0:
            row_copies.append(send(parts.at[at], parts_came.at[ri], {"row": at}))
    for copy in rt_copies + [rt_near]:
        copy.wait()
    rt_sum = r["rt_came"][0].astype(F32)
    for c in range(1, nc):
        rt_sum = rt_sum + r["rt_came"][c].astype(F32)
    r["rt_row"][ri] = rt_sum.astype(BF)
    block = r["rt_row"].at[ri]
    rt_copies = [send(block, block, {"row": ri ^ k}) for k in range(1, nr)]
    out_copies = halves_sum(out_copy, q_half, "came_w_out", "out_w_out")
    rowed["up_b"].wait()
    add_and_send("up", "b", "sum_up_1")
    total = r["out_sum"]
    total[...] = r["out_part"][...]
    total[ci] = (r["out_part"][ci].astype(F32) + r["hidden"][...]).astype(BF)
    for copy in row_copies:
        copy.wait()
    d_normed = parts[ri].astype(F32)
    for k in range(1, nr):
        d_normed = d_normed + parts_came[ri ^ k].astype(F32)
    x = r["x"][...]
    inv_one = lax.rsqrt(jnp.mean(x * x, axis=1, keepdims=True) + NORM_EPSILON)
    hat_one = x * inv_one
    gain_one = jnp.sum(d_normed * hat_one, axis=0, keepdims=True)
    put_gain(gain_one, 0)
    d_hat = d_normed * g_one
    inner = jnp.mean(d_hat * hat_one, axis=1, keepdims=True)
    r["din"][...] = (r["dh"][...] + inv_one * (d_hat - hat_one * inner)).astype(BF)
    last = over_col(r["d_input"], lambda c: r["din"].at[:, lanes_of(c)])
    last.append(load(r["din"].at[:, lanes_of(ci)], r["d_input"].at[ci]))
    for k in range(1, world):
        at = me ^ k
        last.append(
            send(r["gain_send"].at[at % nc], r["gain_came"].at[me], at_place("world", at))
        )
    last.append(load(r["gain_send"].at[ci], r["gain_came"].at[me]))
    last += over_col(r["output"], lambda c: total.at[:, :, lanes_of(c)])
    last.append(load(total.at[:, :, lanes_of(ci)], r["output"].at[ci]))
    for copy in out_copies:
        copy.wait()
    qkv_copy = halves_of(r["dqkv"], w_half, r["normed"][...], "came_w_qkv")
    over_dp("down_b")
    for copy in rt_copies:
        copy.wait()
    rt_sum = r["rt_row"][0].astype(F32)
    for row in range(1, nr):
        rt_sum = rt_sum + r["rt_row"][row].astype(F32)
    r["rt_dp"][...] = rt_sum.astype(BF)
    last += [send(r["rt_dp"], r["router_grad"].at[di], {"dp": di ^ k}) for k in range(1, ndp)]
    last.append(load(r["rt_dp"], r["router_grad"].at[di]))
    over_dp("gate_b")
    last += halves_sum(qkv_copy, w_half, "came_w_qkv", "out_w_qkv")
    over_dp("up_b")
    for copy in last:
        copy.wait()
    for wait in waits:
        wait()


def back_pass(number, vmem, hbm, q_heads, kv_heads, counts):
    nc, nr, ndp = lax.axis_size("col"), lax.axis_size("row"), lax.axis_size("dp")
    world = nc * nr * ndp
    share, width = vmem["hidden"].shape
    feat, count = width // nc, nr * share
    group = vmem["kv"].shape[1]
    q_rows, kv_rows = q_heads * HEAD_SIZE, 2 * kv_heads * HEAD_SIZE
    all_rows = q_rows + kv_rows
    stack = (2, nc) if ndp == 2 else (nc,)
    hid = hbm["own_gate_a"].shape[2]

    def like(shape, dtype=BF):
        return jax.ShapeDtypeStruct(shape, dtype)

    outs = {
        "d_input": like((nc, share, feat)),
        "output": like((nc, nc, share, feat)),
        "gain_came": like((world, 8, 128), F32),
        "router_grad": like((ndp, 48, feat)),
        "out_w_out": like((nc, q_rows // 2, feat)),
        "out_w_qkv": like((nc, all_rows // 2, feat)),
    }
    for part, n in counts.items():
        outs["out_gate_" + part] = like(stack + (n, feat, hid))
        outs["out_up_" + part] = like(stack + (n, feat, hid))
        if part != "a" or ndp == 2:
            outs["out_down_" + part] = like(stack + (n, hid, feat))
    for name in ("down_b", "gate_b", "up_b"):
        outs["came_" + name] = like(hbm["go_" + name].shape)
    most = max(counts.values())
    scratch = {
        "rt": pltpu.VMEM((48, width), BF),
        "rt_came": pltpu.VMEM((nc, 48, feat), BF),
        "rt_row": pltpu.VMEM((nr, 48, feat), BF),
        "rt_dp": pltpu.VMEM((48, feat), BF),
        "gain_send": pltpu.VMEM((nc, 8, 128), F32),
        "dh": pltpu.VMEM((share, width), F32),
        "branch": pltpu.VMEM((nr, share, width), BF),
        "do": pltpu.VMEM((q_rows, count), BF),
        "bias": pltpu.VMEM((group, count), F32),
        "k_s": pltpu.VMEM((kv_heads, group, HEAD_SIZE), BF),
        "v_s": pltpu.VMEM((kv_heads, group, HEAD_SIZE), BF),
        "dk_s": pltpu.VMEM((kv_heads, group, HEAD_SIZE), F32),
        "dv_s": pltpu.VMEM((kv_heads, group, HEAD_SIZE), F32),
        "dq": pltpu.VMEM((q_rows, count), F32),
        "dkv": pltpu.VMEM((kv_rows, group), BF),
        "kv_came": pltpu.VMEM((nc, kv_rows, count), BF),
        "dqkv": pltpu.VMEM((all_rows, count), BF),
        "turned": pltpu.VMEM((count, all_rows), BF),
        "dn": pltpu.VMEM((nr, share, width), BF),
        "dn_came": pltpu.VMEM((nr, share, width), BF),
        "din": pltpu.VMEM((share, width), BF),
        "out_sum": pltpu.VMEM((nc, share, width), BF),
        "w_go": pltpu.VMEM((all_rows // 2, width), BF),
        "w_keep": pltpu.VMEM((all_rows // 2, width), BF),
        "came_w_out": pltpu.VMEM((q_rows // 2, width), BF),
        "came_w_qkv": pltpu.VMEM((all_rows // 2, width), BF),
        "sum_up_0": pltpu.VMEM((most, width, hid), BF),
        "sum_up_1": pltpu.VMEM((most, width, hid), BF),
        "add_up": pltpu.VMEM((most, width, hid), BF),
        "sum_down": pltpu.VMEM((nc, most, hid, feat), BF),
        "add_down": pltpu.VMEM((nc, most, hid, feat), BF),
        "send": pltpu.SemaphoreType.DMA((96 + world,)),
        "recv": pltpu.SemaphoreType.DMA((96 + world,)),
        "near": pltpu.SemaphoreType.DMA((64,)),
    }
    names = list(vmem) + list(hbm) + list(outs) + list(scratch)
    sizes = (nc, nr, ndp, kv_heads, counts)
    made = pl.pallas_call(
        functools.partial(back_kernel, names, sizes),
        out_shape=list(outs.values()),
        in_specs=[pl.BlockSpec(memory_space=pltpu.VMEM)] * len(vmem) + [HBM] * len(hbm),
        out_specs=[HBM] * len(outs),
        scratch_shapes=list(scratch.values()),
        compiler_params=pltpu.CompilerParams(
            collective_id=number, has_side_effects=True, vmem_limit_bytes=61 * 2**20
        ),
        cost_estimate=FREE,
    )(*vmem.values(), *hbm.values())
    return dict(zip(outs, made))


def block_sum(stack):
    return jnp.sum(stack.astype(F32), axis=0)


def col_gather(operand):
    return lax.all_gather(operand, "col", axis=0, tiled=True)


def col_scatter(operand):
    return lax.psum_scatter(operand, "col", scatter_dimension=0, tiled=True)


def pick(stack, index):
    return lax.dynamic_index_in_dim(stack, index, 0, keepdims=False)


def add_low(first, second):
    return (first.astype(F32) + second.astype(F32)).astype(BF)


def pair_sums(operand):
    ndp = lax.axis_size("dp")
    if ndp == 2:
        return operand
    return lax.psum(operand, "dp", axis_index_groups=[list(range(h, ndp, 2)) for h in range(2)])


def widen_kernel(parts, *refs):
    low = 0
    for ref in refs[:parts]:
        refs[parts][0, low : low + ref.shape[1]] = ref[0].astype(F32)
        low += ref.shape[1]


def widen(*stacks):
    blocks = [stack.reshape((-1,) + stack.shape[2:]) for stack in stacks]
    count = sum(block.shape[1] for block in blocks)
    shape = (blocks[0].shape[0], count) + blocks[0].shape[2:]

    def spec(block):
        return pl.BlockSpec((1,) + block[1:], lambda i: (i, 0, 0, 0))

    out = pl.pallas_call(
        functools.partial(widen_kernel, len(blocks)),
        grid=(shape[0],),
        out_shape=jax.ShapeDtypeStruct(shape, F32),
        in_specs=[spec(block.shape) for block in blocks],
        out_specs=spec(shape),
        compiler_params=pltpu.CompilerParams(vmem_limit_bytes=16 * 2**20),
    )(*blocks)
    return out.reshape((-1,) + shape[2:])


def dense_gates(normed, router, routes):
    experts = router.shape[1]
    logits = nn(normed, router)
    chosen = jnp.any(
        routes[:, :, None] == jnp.arange(experts, dtype=jnp.int32)[None, None, :], axis=1
    )
    top = jnp.max(jnp.where(chosen, logits, FILLER), axis=1, keepdims=True)
    weights = jnp.where(chosen, jnp.exp(jnp.where(chosen, logits - top, 0.0)), 0.0)
    return weights / jnp.sum(weights, axis=1, keepdims=True)


def bias_into(bias, key_ref, row_ref, start_ref, chunk):
    @pl.loop(0, bias.shape[0] // chunk)
    def _(c):
        at = pl.ds(pl.multiple_of(c * chunk, chunk), chunk)
        keys = key_ref[at, :]
        seen = (keys <= row_ref[...]) & (keys >= start_ref[...])
        bias[at, :] = jnp.where(seen, 0.0, FILLER)


def attend_kernel(tile, kv_heads, plans, *refs):
    count = len(plans)
    q_ref, kv_ref, key_ref, row_ref, start_ref = refs[:5]
    ins, refs = refs[5 : 5 + count], refs[5 + count :]
    o_ref, lse_ref = refs[:2]
    outs, refs = refs[2 : 2 + count], refs[2 + count :]
    bias, k_s, sems = refs[0], refs[1], refs[2:]
    greet(partners(plans))
    moves = moves_in(plans, ins, outs, sems)
    for move in moves:
        move.start()
    size = HEAD_SIZE
    heads = q_ref.shape[0] // size
    per = heads // kv_heads
    rows = q_ref.shape[1]
    bias_into(bias, key_ref, row_ref, start_ref, 256)
    for g in range(kv_heads):
        k_s[g] = kv_ref[g * size : (g + 1) * size, :].T

    @pl.loop(0, heads)
    def _(h):
        g = h // per
        at = pl.ds(pl.multiple_of(h * size, size), size)
        v_at = pl.ds(pl.multiple_of((kv_heads + g) * size, size), size)
        for t in range(rows // tile):
            cut = slice(t * tile, (t + 1) * tile)
            scores = nn(k_s[g], q_ref[at, cut]) + bias[:, cut]
            top = jnp.max(scores, axis=0, keepdims=True)
            weights = jnp.exp(scores - top)
            total = jnp.sum(weights, axis=0, keepdims=True)
            chances = (weights * (1.0 / total)).astype(BF)
            o_ref[at, cut] = nn(kv_ref[v_at, :], chances).astype(BF)
            lse_ref[h, :, cut] = top + jnp.log(total)

    finish_all(moves)


def attend(number, q, kv, keys, rows_at, starts, kv_heads, *moves):
    plans, shapes = planned(moves)
    heads, count = q.shape[0] // HEAD_SIZE, q.shape[1]
    group = kv.shape[1]
    vmem = pl.BlockSpec(memory_space=pltpu.VMEM)
    got = pl.pallas_call(
        functools.partial(attend_kernel, min(256, count), kv_heads, plans),
        out_shape=[
            jax.ShapeDtypeStruct(q.shape, BF),
            jax.ShapeDtypeStruct((heads, 1, count), F32),
        ]
        + shapes,
        in_specs=[vmem] * 5 + [HBM] * len(plans),
        out_specs=[vmem] * 2 + [HBM] * len(plans),
        scratch_shapes=[
            pltpu.VMEM((group, count), F32),
            pltpu.VMEM((kv_heads, group, HEAD_SIZE), BF),
        ]
        + move_sems(plans),
        compiler_params=pltpu.CompilerParams(
            collective_id=number, has_side_effects=True, vmem_limit_bytes=48 * 2**20
        ),
        cost_estimate=FREE,
    )(q, kv, keys, rows_at, starts, *[move[0] for move in moves])
    return got[0], got[1], list(got[2:])


def swap(operand, axis, bit):
    n = lax.axis_size(axis)
    return lax.ppermute(operand, axis, [(i, i ^ bit) for i in range(n)])


MESH_ID = pl.DeviceIdType.MESH


def cut(ref, how, index, size):
    if how == "all":
        return ref
    if how == "major":
        return ref.at[index]
    return ref.at[:, pl.ds(pl.multiple_of(index * size, 128), size)]


WORLD = ("dp", "row", "col")
HBM = pl.BlockSpec(memory_space=pl.ANY)
FREE = pl.CostEstimate(flops=1024, bytes_accessed=1024, transcendentals=0)


def size_of(axis):
    return lax.axis_size(WORLD) if axis == "world" else lax.axis_size(axis)


def place_of(axis):
    return lax.axis_index(WORLD) if axis == "world" else lax.axis_index(axis)


def at_place(axis, index):
    if axis != "world":
        return {axis: index}
    nr, nc = lax.axis_size("row"), lax.axis_size("col")
    return {"dp": index // (nr * nc), "row": index // nc % nr, "col": index % nc}


def two_step(plan):
    axis, src, _, n, _ = plan
    return axis == "row" and src == "all" and n == 4


def partners(plans):
    found = []
    for plan in plans:
        axis, src, _, n, _ = plan
        if src[0] == "swap":
            ways = [(axis, src[1])]
        elif src == "pair":
            ways = [("dp", 1)]
        else:
            ways = [(axis, k) for k in range(1, 3 if two_step(plan) else n)]
        if src == "shared":
            ways.append(("dp", 1))
        found += [way for way in ways if way not in found]
    if any(axis == "world" for axis, _ in found):
        found = [way for way in found if way[0] == "world"]
    return found


def greet(ways):
    barrier = pltpu.get_barrier_semaphore()
    for axis, k in ways:
        peer = at_place(axis, place_of(axis) ^ k)
        pl.semaphore_signal(barrier, inc=1, device_id=peer, device_id_type=MESH_ID)
    pl.semaphore_wait(barrier, len(ways))


def remote(src, dst, sems, at, device):
    return pltpu.make_async_remote_copy(
        src_ref=src,
        dst_ref=dst,
        send_sem=sems[0].at[at],
        recv_sem=sems[1].at[at],
        device_id=device,
        device_id_type=MESH_ID,
    )


def slots_of(plan):
    _, src, _, n, _ = plan
    if src[0] == "swap" or src == "pair":
        return 1
    return 2 * (n - 1) if src == "shared" else n - 1


class Move:
    def __init__(self, plan, x, out, sems, base, which, buffer):
        axis, src, dst, n, _ = plan
        i, di = place_of(axis), place_of("dp")
        self.near, self.back, self.far, self.relays = [], [], [], []

        def near(source, target):
            self.near.append(pltpu.make_async_copy(source, buffer, sems[2].at[which]))
            self.back.append(pltpu.make_async_copy(buffer, target, sems[2].at[which]))

        def far(source, target, device):
            at = base + len(self.far) + len(self.relays)
            return remote(source, target, sems, at, device)

        if src[0] == "swap":
            self.far.append(far(x, out, at_place(axis, i ^ src[1])))
        elif src == "pair":
            near(x, out.at[di % 2])
            self.far.append(far(x, out.at[di % 2], {"dp": di ^ 1}))
        elif src == "shared":
            part = x.shape[0] // 2
            half = pl.ds(pl.multiple_of(di % 2 * part, part), part)
            near(x, out.at[i])
            for k in range(1, n):
                self.far.append(far(x.at[half], out.at[i, half], at_place(axis, i ^ k)))
            for k in range(1, n):
                block = out.at[i ^ k, half]
                self.relays.append((self.far[k - 1], far(block, block, {"dp": di ^ 1})))
        elif src[0] == "spread":
            first, local, count = src[1:]

            def block(c):
                return x.at[pl.ds((di % 2 * n + c) * local + first, count)]

            near(block(i), out.at[i])
            for k in range(1, n):
                self.far.append(far(block(i ^ k), out.at[i], at_place(axis, i ^ k)))
        elif src == "second":
            size = x.shape[1] // n

            def cols(c):
                return x.at[:, pl.ds(pl.multiple_of(c * size, size), size)]

            near(cols(i), out.at[i])
            for k in range(1, n):
                self.far.append(far(cols(i ^ k), out.at[i], at_place(axis, i ^ k)))
        else:
            in_size, out_size = x.shape[-1] // n, out.shape[-1] // n
            near(cut(x, src, i, in_size), cut(out, dst, i, out_size))
            for k in range(1, 3 if two_step(plan) else n):
                self.far.append(
                    far(
                        cut(x, src, i ^ k, in_size),
                        cut(out, dst, i, out_size),
                        at_place(axis, i ^ k),
                    )
                )
            if two_step(plan):
                block = out.at[i ^ 2]
                self.relays.append((self.far[1], far(block, block, {"row": i ^ 1})))

    def start(self):
        for copy in self.far + self.near:
            copy.start()

    def relay(self):
        for copy, back in zip(self.near, self.back):
            copy.wait()
            back.start()
        for came, onward in self.relays:
            came.wait_recv()
            onward.start()

    def finish(self):
        passed = [came for came, _ in self.relays]
        for copy in self.back:
            copy.wait()
        for copy in self.far:
            if any(copy is came for came in passed):
                copy.wait_send()
            else:
                copy.wait()
        for _, onward in self.relays:
            onward.wait()


def moves_in(plans, ins, outs, sems):
    made, base, buffers = [], 0, list(sems[3:])
    for which, plan in enumerate(plans):
        buffer = None if plan[4] is None else buffers.pop(0)
        made.append(Move(plan, ins[which], outs[which], sems, base, which, buffer))
        base += slots_of(plan)
    return made


def finish_all(moves):
    for move in moves:
        move.relay()
    for move in moves:
        move.finish()


def planned(moves):
    plans, shapes = [], []
    for operand, axis, src, dst in moves:
        n = 2 if src == "pair" else size_of(axis)
        shape = operand.shape
        if src[0] == "swap":
            plans.append((axis, src, dst, n, None))
            shapes.append(jax.ShapeDtypeStruct(shape, operand.dtype))
            continue
        if src[0] == "spread":
            shape = (src[3],) + shape[1:]
        elif src == "second":
            shape = shape[:1] + (shape[1] // n,) + shape[2:]
        elif src == "major":
            shape = shape[1:]
        elif src == "lane":
            shape = shape[:-1] + (shape[-1] // n,)
        plans.append((axis, src, dst, n, (shape, operand.dtype)))
        if dst == "major":
            shape = (n,) + shape
        else:
            shape = shape[:-1] + (shape[-1] * n,)
        shapes.append(jax.ShapeDtypeStruct(shape, operand.dtype))
    return plans, shapes


def move_sems(plans):
    count = sum(slots_of(plan) for plan in plans)
    return [
        pltpu.SemaphoreType.DMA((count,)),
        pltpu.SemaphoreType.DMA((count,)),
        pltpu.SemaphoreType.DMA((len(plans),)),
    ] + [pltpu.VMEM(*plan[4]) for plan in plans if plan[4] is not None]


def exchange_kernel(plans, *refs):
    count = len(plans)
    greet(partners(plans))
    moves = moves_in(plans, refs[:count], refs[count : 2 * count], refs[2 * count :])
    for move in moves:
        move.start()
    finish_all(moves)


def exchange(number, *moves):
    plans, shapes = planned(moves)
    return pl.pallas_call(
        functools.partial(exchange_kernel, plans),
        out_shape=shapes,
        in_specs=[HBM] * len(plans),
        out_specs=[HBM] * len(plans),
        scratch_shapes=move_sems(plans),
        compiler_params=pltpu.CompilerParams(collective_id=number, has_side_effects=True),
        cost_estimate=FREE,
    )(*[move[0] for move in moves])


def gather_pass_kernel(nc, plans, *refs):
    count = len(plans)
    x_ref, ins, refs = refs[0], refs[1 : 1 + count], refs[1 + count :]
    own, core, pair, both = refs[:4]
    outs, refs = refs[4 : 4 + count], refs[4 + count :]
    sems, near_sem, move_sem = refs[:2], refs[2], refs[3:]
    ci, ri, di = lax.axis_index("col"), lax.axis_index("row"), lax.axis_index("dp")
    to_core, to_pair = {"row": ri ^ 1}, {"dp": di ^ 1}
    ways = [("col", k) for k in range(1, nc)] + [("row", 1), ("dp", 1)]
    greet(ways + [way for way in partners(plans) if way not in ways])

    def send(way, k, src, dst, device):
        copy = remote(src, dst, (sems[0].at[way], sems[1].at[way]), k, device)
        copy.start()
        return copy

    near = pltpu.make_async_copy(x_ref, own.at[ci], near_sem)
    near.start()
    far = [send(0, k, x_ref, own.at[ci], {"col": ci ^ k}) for k in range(1, nc)]
    moves = moves_in(plans, ins, outs, move_sem)
    for move in moves:
        move.start()
    paired, cored, waits = [], [], []
    for k in range(nc):
        if k > 0:
            far[k - 1].wait_recv()
            waits.append(far[k - 1].wait_send)
        block = x_ref if k == 0 else own.at[ci ^ k]
        paired.append(send(1, k, block, pair.at[ci ^ k], to_pair))
        cored.append(send(2, k, block, core.at[ci ^ k], to_core))
    for k in range(nc):
        paired[k].wait_recv()
        waits.append(paired[k].wait_send)
        waits.append(cored[k].wait)
        waits.append(send(3, k, pair.at[ci ^ k], both.at[ci ^ k], to_core).wait)
    waits.append(near.wait)
    for wait in waits:
        wait()
    finish_all(moves)


def gather_pass(number, x, *moves):
    nc = lax.axis_size("col")
    plans, shapes = planned(moves)
    made = jax.ShapeDtypeStruct((nc,) + x.shape, x.dtype)
    got = pl.pallas_call(
        functools.partial(gather_pass_kernel, nc, plans),
        out_shape=[made] * 4 + shapes,
        in_specs=[pl.BlockSpec(memory_space=pltpu.VMEM)] + [HBM] * len(plans),
        out_specs=[HBM] * (4 + len(plans)),
        scratch_shapes=[pltpu.SemaphoreType.DMA((4, nc))] * 2
        + [pltpu.SemaphoreType.DMA]
        + move_sems(plans),
        compiler_params=pltpu.CompilerParams(collective_id=number, has_side_effects=True),
        cost_estimate=FREE,
    )(x, *[move[0] for move in moves])
    got = list(got)
    return [block.reshape(nc * x.shape[0], x.shape[1]) for block in got[:4]], got[4:]


def scatter_pass_kernel(nc, parts, plans, *refs):
    count = len(plans)
    ins, more_ins, refs = refs[: 4 * parts], refs[4 * parts : 8 * parts], refs[8 * parts :]
    move_ins, out_ref, part_ref = refs[:count], refs[count], refs[count + 1]
    refs = refs[count + 2 :]
    move_outs, refs = refs[:count], refs[count:]
    made, came, more_made, more_came, total, send_sem, recv_sem = refs[:7]
    ci, ri, di = lax.axis_index("col"), lax.axis_index("row"), lax.axis_index("dp")
    to_core, to_pair = {"row": ri ^ 1}, {"dp": di ^ 1}
    ways = [("col", k) for k in range(1, nc)] + [("row", 1), ("dp", 1)]
    greet(ways + [way for way in partners(plans) if way not in ways])
    moves = moves_in(plans, move_ins, move_outs, refs[7:])
    for move in moves:
        move.start()
    order = list(range(1, nc)) + [0]

    def send(way, k, src, dst, device):
        copy = remote(src, dst, (send_sem.at[way], recv_sem.at[way]), k, device)
        copy.start()
        return copy

    def added(from_refs, from_came, which, at, *more):
        value = from_refs[which][at].astype(F32)
        for p in range(1, parts):
            value = value + from_refs[4 * p + which][at].astype(F32)
        for other in more:
            value = value + from_came[other, at].astype(F32)
        return value.astype(BF)

    groups = ((ins, made, came, 0), (more_ins, more_made, more_came, 4))
    sent = {}
    for from_refs, to_made, to_came, base in groups:
        for k in order:
            at = ci ^ k
            for way, which in ((0, 3), (1, 1)):
                to_made[way, at] = added(from_refs, to_came, which, at)
                sent[base + way, k] = send(
                    base + way, k, to_made.at[way, at], to_came.at[way, at], to_core
                )
    for from_refs, to_made, to_came, base in groups:
        for k in order:
            at = ci ^ k
            sent[base, k].wait_recv()
            to_made[2, at] = added(from_refs, to_came, 2, at, 0)
            sent[base + 2, k] = send(base + 2, k, to_made.at[2, at], to_came.at[2, at], to_pair)
    for from_refs, to_made, to_came, base in groups:
        for k in order:
            at = ci ^ k
            sent[base + 1, k].wait_recv()
            sent[base + 2, k].wait_recv()
            if base:
                part_ref[at] = added(from_refs, to_came, 0, at, 1, 2)
                continue
            total[at] = added(from_refs, to_came, 0, at, 1, 2)
            if k > 0:
                sent[3, k] = send(3, k, total.at[at], out_ref.at[ci], {"col": at})
    out_ref[ci] = total[ci]
    for _, _, _, base in groups:
        for way in range(3):
            for k in order:
                sent[base + way, k].wait_send()
    for k in range(1, nc):
        sent[3, k].wait()
    finish_all(moves)


def scatter_pass(number, parts, more, *moves):
    nc = lax.axis_size("col")
    plans, shapes = planned(moves)
    rows, width = parts[0][0].shape
    shape = (nc, rows // nc, width)
    more_shape = (nc, rows // nc, more[0][0].shape[1])
    vmem = pl.BlockSpec(memory_space=pltpu.VMEM)
    got = pl.pallas_call(
        functools.partial(scatter_pass_kernel, nc, len(parts), plans),
        out_shape=[jax.ShapeDtypeStruct(shape, BF), jax.ShapeDtypeStruct(more_shape, BF)] + shapes,
        in_specs=[vmem] * (8 * len(parts)) + [HBM] * len(plans),
        out_specs=[vmem] * 2 + [HBM] * len(plans),
        scratch_shapes=[
            pltpu.VMEM((3,) + shape, BF),
            pltpu.VMEM((3,) + shape, BF),
            pltpu.VMEM((3,) + more_shape, BF),
            pltpu.VMEM((3,) + more_shape, BF),
            pltpu.VMEM(shape, BF),
            pltpu.SemaphoreType.DMA((7, nc)),
            pltpu.SemaphoreType.DMA((7, nc)),
        ]
        + move_sems(plans),
        compiler_params=pltpu.CompilerParams(
            collective_id=number, has_side_effects=True, vmem_limit_bytes=61 * 2**20
        ),
        cost_estimate=FREE,
    )(
        *[block.reshape(shape) for part in parts for block in part],
        *[block.reshape(more_shape) for part in more for block in part],
        *[move[0] for move in moves],
    )
    return got[0], got[1], list(got[2:])


def rotated(first, second, cosine, sine):
    return first * cosine - second * sine, second * cosine + first * sine


def back_kernel(names, sizes, *refs):
    r = dict(zip(names, refs))
    nc, nr, ndp, kv_heads, counts = sizes
    ci, ri, di = lax.axis_index("col"), lax.axis_index("row"), lax.axis_index("dp")
    me = place_of("world")
    world = nc * nr * ndp
    half = di % 2
    share, width = r["hidden"].shape
    feat = width // nc
    count = nr * share
    size = HEAD_SIZE
    q_rows = r["q"].shape[0]
    heads = q_rows // size
    per = heads // kv_heads
    kv_rows = kv_heads * size
    used = [0, 0]

    def send(src, dst, device):
        copy = remote(src, dst, (r["send"], r["recv"]), used[0], device)
        used[0] += 1
        copy.start()
        return copy

    def load(src, dst):
        copy = pltpu.make_async_copy(src, dst, r["near"].at[used[1]])
        used[1] += 1
        copy.start()
        return copy

    waits = []

    def lanes_of(c):
        return pl.ds(pl.multiple_of(c * feat, feat), feat)

    def over_col(dst, block):
        return [send(block(ci ^ k), dst.at[ci], {"col": ci ^ k}) for k in range(1, nc)]

    greet([("world", k) for k in range(1, world)])

    pending = {}

    def add_and_send(tensor, part, buffer):
        name = tensor + "_" + part
        own, came = r["own_" + name], r["came_" + name]
        n = counts[part]
        total = r[buffer].at[:, :n] if tensor == "down" else r[buffer].at[:n]
        other = r["add_down" if tensor == "down" else "add_up"]
        other = other.at[:, :n] if tensor == "down" else other.at[:n]
        loads = [load(own, total), load(came, other)]
        for copy in loads:
            copy.wait()
        if tensor == "down":
            for c in range(nc):
                for i in range(n):
                    total[c, i] = (total[c, i].astype(F32) + other[c, i].astype(F32)).astype(BF)
        else:

            @pl.loop(0, nc)
            def _(c):
                for i in range(n):
                    total[i, lanes_of(c)] = (
                        total[i, lanes_of(c)].astype(F32) + other[i, lanes_of(c)].astype(F32)
                    ).astype(BF)

        out = r["out_" + name]
        out = out.at[half] if ndp == 2 else out

        def block(c):
            return total.at[c] if tensor == "down" else total.at[:, lanes_of(c)]

        copies = over_col(out, block)
        near = load(block(ci), out.at[ci])
        pending[name] = (copies, near, out)

    def over_dp(name):
        copies, near, out = pending[name]
        for copy in copies:
            copy.wait()
        near.wait()
        if ndp == 2:
            waits.append(send(out, out, {"dp": di ^ 1}).wait)

    add_and_send("gate", "a", "sum_up_0")
    if ndp == 2:
        own = r["in_down_a"]
        mine = r["out_down_a"].at[half]
        first_load = load(own, r["sum_down"])
        waits.append(send(own, mine, {"dp": di ^ 1}).wait)

    d_sum = r["d_parts"][0].astype(F32)
    for c in range(1, nc):
        d_sum = d_sum + r["d_parts"][c].astype(F32)
    hidden = r["hidden"][...]
    g_one, g_two = r["gains"][0:1, :], r["gains"][1:2, :]
    inv_two = lax.rsqrt(jnp.mean(hidden * hidden, axis=1, keepdims=True) + NORM_EPSILON)
    hat_two = hidden * inv_two
    normed_two = (hat_two * g_two).astype(BF)
    gates = r["gates"][...]
    d_gates = d_sum[:, width:]
    d_logits = (gates * (d_gates - jnp.sum(gates * d_gates, axis=1, keepdims=True))).astype(BF)
    r["rt"][...] = tn(d_logits, normed_two)[: r["rt"].shape[0]].astype(BF)
    d_normed = d_sum[:, :width] + nt(d_logits, r["router"][...])
    gain_two = jnp.sum(d_normed * hat_two, axis=0, keepdims=True)
    r["gain_send"][...] = jnp.zeros_like(r["gain_send"])
    chunks = feat // 128

    def put_gain(gain, low):
        for c in range(nc):
            for j in range(chunks):
                at = c * feat + j * 128
                r["gain_send"][c, low + j : low + j + 1, :] = gain[:, at : at + 128]

    put_gain(gain_two, chunks)
    d_hat = d_normed * g_two
    inner = jnp.mean(d_hat * hat_two, axis=1, keepdims=True)
    d_hidden = r["dy"][...].astype(F32) + inv_two * (d_hat - hat_two * inner)
    r["dh"][...] = d_hidden
    branch = r["branch"]
    branch[ri] = d_hidden.astype(BF)
    mine = branch.at[ri]
    to_core = send(mine, mine, {"row": ri ^ 1})
    to_other = send(mine, mine, {"row": ri ^ 2})
    rowed = {}
    for name in ("down_b", "gate_b", "up_b"):
        rowed[name] = send(r["go_" + name], r["came_" + name], {"row": ri ^ 2})
    add_and_send("up", "a", "sum_up_1")
    if ndp == 2:
        first_load.wait()
        first_store = load(r["sum_down"], r["out_down_a"].at[half])
    to_other.wait_recv()
    block = branch.at[ri ^ 2]
    passed = send(block, block, {"row": ri ^ 1})
    bias, k_s, v_s, dk_s, dv_s = r["bias"], r["k_s"], r["v_s"], r["dk_s"], r["dv_s"]
    bias_into(bias, r["key_orders"], r["row_orders"], r["row_starts"], 256)
    kv = r["kv"]
    for g in range(kv_heads):
        k_s[g] = kv[g * size : (g + 1) * size, :].T
        v_s[g] = kv[kv_rows + g * size : kv_rows + (g + 1) * size, :].T
    dk_s[...] = jnp.zeros_like(dk_s)
    dv_s[...] = jnp.zeros_like(dv_s)
    to_core.wait()
    to_other.wait_send()
    passed.wait()
    for row in range(nr):
        r["do"][:, row * share : (row + 1) * share] = nt(r["w_out"][...], branch[row]).astype(BF)

    tile = min(256, count)

    def heads_part(low, high):
        @pl.loop(low, high)
        def _(h):
            g = h // per
            at = pl.ds(pl.multiple_of(h * size, size), size)
            k_at = pl.ds(pl.multiple_of(g * size, size), size)
            for t in range(count // tile):
                cut_at = slice(t * tile, (t + 1) * tile)
                q_part, do_part = r["q"][at, cut_at], r["do"][at, cut_at]
                scores = nn(k_s[g], q_part) + bias[:, cut_at]
                probs = jnp.exp(scores - r["lse"][h, :, cut_at])
                d_chances = nn(v_s[g], do_part)
                dv_s[g] += nt(probs.astype(BF), do_part)
                both = probs * d_chances
                d_scores = (both - probs * jnp.sum(both, axis=0, keepdims=True)).astype(BF)
                dk_s[g] += nt(d_scores, q_part)
                r["dq"][at, cut_at] = nn(kv[k_at, :], d_scores)

    heads_part(0, heads // 2)
    over_dp("gate_a")
    rowed["down_b"].wait()
    if ndp == 2:
        first_store.wait()
    add_and_send("down", "b", "sum_down")
    heads_part(heads // 2, heads)
    for g in range(kv_heads):
        r["dkv"][g * size : (g + 1) * size, :] = dk_s[g].T.astype(BF)
        r["dkv"][kv_rows + g * size : kv_rows + (g + 1) * size, :] = dv_s[g].T.astype(BF)

    def part_of(c):
        return r["dkv"].at[:, pl.ds(pl.multiple_of(c * count, count), count)]

    kv_copies = over_col(r["kv_came"], part_of)
    kv_near = load(part_of(ci), r["kv_came"].at[ci])
    rt_copies = over_col(r["rt_came"], lambda c: r["rt"].at[:, lanes_of(c)])
    rt_near = load(r["rt"].at[:, lanes_of(ci)], r["rt_came"].at[ci])
    other_half = 1 - half
    branches = branch[...].reshape(count, width)
    q_half = q_rows // 2
    w_half = r["w_keep"].shape[0]

    def halves_of(lhs, rows_half, rhs, came):
        for which, name in ((other_half, "w_go"), (half, "w_keep")):
            at = pl.ds(pl.multiple_of(which * rows_half, rows_half), rows_half)
            r[name][:rows_half] = nn(lhs[at, :], rhs).astype(BF)
        return send(r["w_go"].at[:rows_half], r[came], {"dp": di ^ 1})

    def halves_sum(copy, rows_half, came, out):
        copy.wait()
        total = r["w_keep"].at[:rows_half]
        total[...] = (total[...].astype(F32) + r[came][...].astype(F32)).astype(BF)
        copies = over_col(r[out], lambda c: total.at[:, lanes_of(c)])
        near = load(total.at[:, lanes_of(ci)], r[out].at[ci])
        return copies + [near]

    out_copy = halves_of(r["mixed"], q_half, branches, "came_w_out")
    rowed["gate_b"].wait()
    add_and_send("gate", "b", "sum_up_0")
    over_dp("up_a")
    for copy in kv_copies + [kv_near]:
        copy.wait()
    grads = r["kv_came"][0].astype(F32)
    for c in range(1, nc):
        grads = grads + r["kv_came"][c].astype(F32)
    cosine, sine = r["cosine"][...], -r["sine"][...]
    scale = 1.0 / math.sqrt(size)
    hop = size // 2
    for h in range(heads):
        a = r["dq"][h * size : h * size + hop, :] * scale
        b = r["dq"][h * size + hop : (h + 1) * size, :] * scale
        a, b = rotated(a, b, cosine, sine)
        r["dqkv"][h * size : h * size + hop, :] = a.astype(BF)
        r["dqkv"][h * size + hop : (h + 1) * size, :] = b.astype(BF)
    for g in range(kv_heads):
        a, b = rotated(
            grads[g * size : g * size + hop], grads[g * size + hop : (g + 1) * size], cosine, sine
        )
        low = q_rows + g * size
        r["dqkv"][low : low + hop, :] = a.astype(BF)
        r["dqkv"][low + hop : low + size, :] = b.astype(BF)
    r["dqkv"][q_rows + kv_rows :, :] = grads[kv_rows:].astype(BF)
    r["turned"][...] = r["dqkv"][...].T
    parts, parts_came = r["dn"], r["dn_came"]
    row_copies = []
    for k in (2, 3, 1, 0):
        at = ri ^ k
        rows_at = pl.ds(pl.multiple_of(at * share, share), share)
        parts[at] = nt(r["turned"][rows_at, :], r["w_qkv"][...]).astype(BF)
        if k > 0:
            row_copies.append(send(parts.at[at], parts_came.at[ri], {"row": at}))
    for copy in rt_copies + [rt_near]:
        copy.wait()
    rt_sum = r["rt_came"][0].astype(F32)
    for c in range(1, nc):
        rt_sum = rt_sum + r["rt_came"][c].astype(F32)
    r["rt_row"][ri] = rt_sum.astype(BF)
    block = r["rt_row"].at[ri]
    rt_copies = [send(block, block, {"row": ri ^ k}) for k in range(1, nr)]
    out_copies = halves_sum(out_copy, q_half, "came_w_out", "out_w_out")
    rowed["up_b"].wait()
    add_and_send("up", "b", "sum_up_1")
    total = r["out_sum"]
    total[...] = r["out_part"][...]
    total[ci] = (r["out_part"][ci].astype(F32) + r["hidden"][...]).astype(BF)
    for copy in row_copies:
        copy.wait()
    d_normed = parts[ri].astype(F32)
    for k in range(1, nr):
        d_normed = d_normed + parts_came[ri ^ k].astype(F32)
    x = r["x"][...]
    inv_one = lax.rsqrt(jnp.mean(x * x, axis=1, keepdims=True) + NORM_EPSILON)
    hat_one = x * inv_one
    gain_one = jnp.sum(d_normed * hat_one, axis=0, keepdims=True)
    put_gain(gain_one, 0)
    d_hat = d_normed * g_one
    inner = jnp.mean(d_hat * hat_one, axis=1, keepdims=True)
    r["din"][...] = (r["dh"][...] + inv_one * (d_hat - hat_one * inner)).astype(BF)
    last = over_col(r["d_input"], lambda c: r["din"].at[:, lanes_of(c)])
    last.append(load(r["din"].at[:, lanes_of(ci)], r["d_input"].at[ci]))
    for k in range(1, world):
        at = me ^ k
        last.append(
            send(r["gain_send"].at[at % nc], r["gain_came"].at[me], at_place("world", at))
        )
    last.append(load(r["gain_send"].at[ci], r["gain_came"].at[me]))
    last += over_col(r["output"], lambda c: total.at[:, :, lanes_of(c)])
    last.append(load(total.at[:, :, lanes_of(ci)], r["output"].at[ci]))
    for copy in out_copies:
        copy.wait()
    qkv_copy = halves_of(r["dqkv"], w_half, r["normed"][...], "came_w_qkv")
    over_dp("down_b")
    for copy in rt_copies:
        copy.wait()
    rt_sum = r["rt_row"][0].astype(F32)
    for row in range(1, nr):
        rt_sum = rt_sum + r["rt_row"][row].astype(F32)
    r["rt_dp"][...] = rt_sum.astype(BF)
    last += [send(r["rt_dp"], r["router_grad"].at[di], {"dp": di ^ k}) for k in range(1, ndp)]
    last.append(load(r["rt_dp"], r["router_grad"].at[di]))
    over_dp("gate_b")
    last += halves_sum(qkv_copy, w_half, "came_w_qkv", "out_w_qkv")
    over_dp("up_b")
    for copy in last:
        copy.wait()
    for wait in waits:
        wait()


def back_pass(number, vmem, hbm, q_heads, kv_heads, counts):
    nc, nr, ndp = lax.axis_size("col"), lax.axis_size("row"), lax.axis_size("dp")
    world = nc * nr * ndp
    share, width = vmem["hidden"].shape
    feat, count = width // nc, nr * share
    group = vmem["kv"].shape[1]
    q_rows, kv_rows = q_heads * HEAD_SIZE, 2 * kv_heads * HEAD_SIZE
    all_rows = q_rows + kv_rows
    stack = (2, nc) if ndp == 2 else (nc,)
    hid = hbm["own_gate_a"].shape[2]

    def like(shape, dtype=BF):
        return jax.ShapeDtypeStruct(shape, dtype)

    outs = {
        "d_input": like((nc, share, feat)),
        "output": like((nc, nc, share, feat)),
        "gain_came": like((world, 8, 128), F32),
        "router_grad": like((ndp, 48, feat)),
        "out_w_out": like((nc, q_rows // 2, feat)),
        "out_w_qkv": like((nc, all_rows // 2, feat)),
    }
    for part, n in counts.items():
        outs["out_gate_" + part] = like(stack + (n, feat, hid))
        outs["out_up_" + part] = like(stack + (n, feat, hid))
        if part != "a" or ndp == 2:
            outs["out_down_" + part] = like(stack + (n, hid, feat))
    for name in ("down_b", "gate_b", "up_b"):
        outs["came_" + name] = like(hbm["go_" + name].shape)
    most = max(counts.values())
    scratch = {
        "rt": pltpu.VMEM((48, width), BF),
        "rt_came": pltpu.VMEM((nc, 48, feat), BF),
        "rt_row": pltpu.VMEM((nr, 48, feat), BF),
        "rt_dp": pltpu.VMEM((48, feat), BF),
        "gain_send": pltpu.VMEM((nc, 8, 128), F32),
        "dh": pltpu.VMEM((share, width), F32),
        "branch": pltpu.VMEM((nr, share, width), BF),
        "do": pltpu.VMEM((q_rows, count), BF),
        "bias": pltpu.VMEM((group, count), F32),
        "k_s": pltpu.VMEM((kv_heads, group, HEAD_SIZE), BF),
        "v_s": pltpu.VMEM((kv_heads, group, HEAD_SIZE), BF),
        "dk_s": pltpu.VMEM((kv_heads, group, HEAD_SIZE), F32),
        "dv_s": pltpu.VMEM((kv_heads, group, HEAD_SIZE), F32),
        "dq": pltpu.VMEM((q_rows, count), F32),
        "dkv": pltpu.VMEM((kv_rows, group), BF),
        "kv_came": pltpu.VMEM((nc, kv_rows, count), BF),
        "dqkv": pltpu.VMEM((all_rows, count), BF),
        "turned": pltpu.VMEM((count, all_rows), BF),
        "dn": pltpu.VMEM((nr, share, width), BF),
        "dn_came": pltpu.VMEM((nr, share, width), BF),
        "din": pltpu.VMEM((share, width), BF),
        "out_sum": pltpu.VMEM((nc, share, width), BF),
        "w_go": pltpu.VMEM((all_rows // 2, width), BF),
        "w_keep": pltpu.VMEM((all_rows // 2, width), BF),
        "came_w_out": pltpu.VMEM((q_rows // 2, width), BF),
        "came_w_qkv": pltpu.VMEM((all_rows // 2, width), BF),
        "sum_up_0": pltpu.VMEM((most, width, hid), BF),
        "sum_up_1": pltpu.VMEM((most, width, hid), BF),
        "add_up": pltpu.VMEM((most, width, hid), BF),
        "sum_down": pltpu.VMEM((nc, most, hid, feat), BF),
        "add_down": pltpu.VMEM((nc, most, hid, feat), BF),
        "send": pltpu.SemaphoreType.DMA((96 + world,)),
        "recv": pltpu.SemaphoreType.DMA((96 + world,)),
        "near": pltpu.SemaphoreType.DMA((64,)),
    }
    names = list(vmem) + list(hbm) + list(outs) + list(scratch)
    sizes = (nc, nr, ndp, kv_heads, counts)
    made = pl.pallas_call(
        functools.partial(back_kernel, names, sizes),
        out_shape=list(outs.values()),
        in_specs=[pl.BlockSpec(memory_space=pltpu.VMEM)] * len(vmem) + [HBM] * len(hbm),
        out_specs=[HBM] * len(outs),
        scratch_shapes=list(scratch.values()),
        compiler_params=pltpu.CompilerParams(
            collective_id=number, has_side_effects=True, vmem_limit_bytes=61 * 2**20
        ),
        cost_estimate=FREE,
    )(*vmem.values(), *hbm.values())
    return dict(zip(outs, made))


def block_sum(stack):
    return jnp.sum(stack.astype(F32), axis=0)


def col_gather(operand):
    return lax.all_gather(operand, "col", axis=0, tiled=True)


def col_scatter(operand):
    return lax.psum_scatter(operand, "col", scatter_dimension=0, tiled=True)


def pick(stack, index):
    return lax.dynamic_index_in_dim(stack, index, 0, keepdims=False)


def add_low(first, second):
    return (first.astype(F32) + second.astype(F32)).astype(BF)


def pair_sums(operand):
    ndp = lax.axis_size("dp")
    if ndp == 2:
        return operand
    return lax.psum(operand, "dp", axis_index_groups=[list(range(h, ndp, 2)) for h in range(2)])


def widen_kernel(parts, *refs):
    low = 0
    for ref in refs[:parts]:
        refs[parts][0, low : low + ref.shape[1]] = ref[0].astype(F32)
        low += ref.shape[1]


def widen(*stacks):
    blocks = [stack.reshape((-1,) + stack.shape[2:]) for stack in stacks]
    count = sum(block.shape[1] for block in blocks)
    shape = (blocks[0].shape[0], count) + blocks[0].shape[2:]

    def spec(block):
        return pl.BlockSpec((1,) + block[1:], lambda i: (i, 0, 0, 0))

    out = pl.pallas_call(
        functools.partial(widen_kernel, len(blocks)),
        grid=(shape[0],),
        out_shape=jax.ShapeDtypeStruct(shape, F32),
        in_specs=[spec(block.shape) for block in blocks],
        out_specs=spec(shape),
        compiler_params=pltpu.CompilerParams(vmem_limit_bytes=16 * 2**20),
    )(*blocks)
    return out.reshape((-1,) + shape[2:])


def dense_gates(normed, router, routes):
    experts = router.shape[1]
    logits = nn(normed, router)
    chosen = jnp.any(
        routes[:, :, None] == jnp.arange(experts, dtype=jnp.int32)[None, None, :], axis=1
    )
    top = jnp.max(jnp.where(chosen, logits, FILLER), axis=1, keepdims=True)
    weights = jnp.where(chosen, jnp.exp(jnp.where(chosen, logits - top, 0.0)), 0.0)
    return weights / jnp.sum(weights, axis=1, keepdims=True)


def bias_into(bias, key_ref, row_ref, start_ref, chunk):
    @pl.loop(0, bias.shape[0] // chunk)
    def _(c):
        at = pl.ds(pl.multiple_of(c * chunk, chunk), chunk)
        keys = key_ref[at, :]
        seen = (keys <= row_ref[...]) & (keys >= start_ref[...])
        bias[at, :] = jnp.where(seen, 0.0, FILLER)


def attend_kernel(tile, kv_heads, plans, *refs):
    count = len(plans)
    q_ref, kv_ref, key_ref, row_ref, start_ref = refs[:5]
    ins, refs = refs[5 : 5 + count], refs[5 + count :]
    o_ref, lse_ref = refs[:2]
    outs, refs = refs[2 : 2 + count], refs[2 + count :]
    bias, k_s, sems = refs[0], refs[1], refs[2:]
    greet(partners(plans))
    moves = moves_in(plans, ins, outs, sems)
    for move in moves:
        move.start()
    size = HEAD_SIZE
    heads = q_ref.shape[0] // size
    per = heads // kv_heads
    rows = q_ref.shape[1]
    bias_into(bias, key_ref, row_ref, start_ref, 256)
    for g in range(kv_heads):
        k_s[g] = kv_ref[g * size : (g + 1) * size, :].T

    @pl.loop(0, heads)
    def _(h):
        g = h // per
        at = pl.ds(pl.multiple_of(h * size, size), size)
        v_at = pl.ds(pl.multiple_of((kv_heads + g) * size, size), size)
        for t in range(rows // tile):
            cut = slice(t * tile, (t + 1) * tile)
            scores = nn(k_s[g], q_ref[at, cut]) + bias[:, cut]
            top = jnp.max(scores, axis=0, keepdims=True)
            weights = jnp.exp(scores - top)
            total = jnp.sum(weights, axis=0, keepdims=True)
            chances = (weights * (1.0 / total)).astype(BF)
            o_ref[at, cut] = nn(kv_ref[v_at, :], chances).astype(BF)
            lse_ref[h, :, cut] = top + jnp.log(total)

    finish_all(moves)


def attend(number, q, kv, keys, rows_at, starts, kv_heads, *moves):
    plans, shapes = planned(moves)
    heads, count = q.shape[0] // HEAD_SIZE, q.shape[1]
    group = kv.shape[1]
    vmem = pl.BlockSpec(memory_space=pltpu.VMEM)
    got = pl.pallas_call(
        functools.partial(attend_kernel, min(256, count), kv_heads, plans),
        out_shape=[
            jax.ShapeDtypeStruct(q.shape, BF),
            jax.ShapeDtypeStruct((heads, 1, count), F32),
        ]
        + shapes,
        in_specs=[vmem] * 5 + [HBM] * len(plans),
        out_specs=[vmem] * 2 + [HBM] * len(plans),
        scratch_shapes=[
            pltpu.VMEM((group, count), F32),
            pltpu.VMEM((kv_heads, group, HEAD_SIZE), BF),
        ]
        + move_sems(plans),
        compiler_params=pltpu.CompilerParams(
            collective_id=number, has_side_effects=True, vmem_limit_bytes=48 * 2**20
        ),
        cost_estimate=FREE,
    )(q, kv, keys, rows_at, starts, *[move[0] for move in moves])
    return got[0], got[1], list(got[2:])


def attend_back_kernel(tile, kv_heads, plans, *refs):
    count = len(plans)
    q_ref, do_ref, lse_ref, kv_ref, key_ref, row_ref, start_ref = refs[:7]
    ins, refs = refs[7 : 7 + count], refs[7 + count :]
    dq_ref, dkv_ref = refs[:2]
    outs, refs = refs[2 : 2 + count], refs[2 + count :]
    bias, k_s, v_s, dk_s, dv_s = refs[:5]
    greet(partners(plans))
    moves = moves_in(plans, ins, outs, refs[5:])
    for move in moves:
        move.start()
    size = HEAD_SIZE
    heads = q_ref.shape[0] // size
    per = heads // kv_heads
    rows = q_ref.shape[1]
    bias_into(bias, key_ref, row_ref, start_ref, 256)
    for g in range(kv_heads):
        k_s[g] = kv_ref[g * size : (g + 1) * size, :].T
        v_s[g] = kv_ref[(kv_heads + g) * size : (kv_heads + g + 1) * size, :].T
    dk_s[...] = jnp.zeros_like(dk_s)
    dv_s[...] = jnp.zeros_like(dv_s)

    @pl.loop(0, heads)
    def _(h):
        g = h // per
        at = pl.ds(pl.multiple_of(h * size, size), size)
        k_at = pl.ds(pl.multiple_of(g * size, size), size)
        for t in range(rows // tile):
            cut = slice(t * tile, (t + 1) * tile)
            q_part, do_part = q_ref[at, cut], do_ref[at, cut]
            scores = nn(k_s[g], q_part) + bias[:, cut]
            probs = jnp.exp(scores - lse_ref[h, :, cut])
            d_chances = nn(v_s[g], do_part)
            dv_s[g] += nt(probs.astype(BF), do_part)
            both = probs * d_chances
            d_scores = (both - probs * jnp.sum(both, axis=0, keepdims=True)).astype(BF)
            dk_s[g] += nt(d_scores, q_part)
            dq_ref[at, cut] = nn(kv_ref[k_at, :], d_scores)

    for g in range(kv_heads):
        dkv_ref[g * size : (g + 1) * size, :] = dk_s[g].T.astype(BF)
        dkv_ref[(kv_heads + g) * size : (kv_heads + g + 1) * size, :] = dv_s[g].T.astype(BF)
    finish_all(moves)


def attend_back(number, q, do, lse, kv, keys, rows_at, starts, kv_heads, *moves):
    plans, shapes = planned(moves)
    count = q.shape[1]
    group = kv.shape[1]
    vmem = pl.BlockSpec(memory_space=pltpu.VMEM)
    got = pl.pallas_call(
        functools.partial(attend_back_kernel, min(256, count), kv_heads, plans),
        out_shape=[jax.ShapeDtypeStruct(q.shape, F32), jax.ShapeDtypeStruct(kv.shape, BF)]
        + shapes,
        in_specs=[vmem] * 7 + [HBM] * len(plans),
        out_specs=[vmem] * 2 + [HBM] * len(plans),
        scratch_shapes=[
            pltpu.VMEM((group, count), F32),
            pltpu.VMEM((kv_heads, group, HEAD_SIZE), BF),
            pltpu.VMEM((kv_heads, group, HEAD_SIZE), BF),
            pltpu.VMEM((kv_heads, group, HEAD_SIZE), F32),
            pltpu.VMEM((kv_heads, group, HEAD_SIZE), F32),
        ]
        + move_sems(plans),
        compiler_params=pltpu.CompilerParams(
            collective_id=number, has_side_effects=True, vmem_limit_bytes=56 * 2**20
        ),
        cost_estimate=FREE,
    )(q, do, lse, kv, keys, rows_at, starts, *[move[0] for move in moves])
    return got[0], got[1], list(got[2:])


def expert_kernel(sets, nb, tile, plans, onward, *refs):
    x_refs, dy_refs = refs[:sets], refs[sets : 2 * sets]
    mark_ref, refs = refs[2 * sets], refs[2 * sets + 1 :]
    wg, wu, wd = refs[:nb], refs[nb : 2 * nb], refs[2 * nb : 3 * nb]
    refs = refs[3 * nb :]
    count = len(plans) - len(onward)
    move_ins, refs = list(refs[:count]), refs[count:]
    outs, dxs = refs[:sets], refs[sets : 2 * sets]
    refs = refs[2 * sets :]
    dwg, dwu, dwd = refs[:nb], refs[nb : 2 * nb], refs[2 * nb : 3 * nb]
    refs = refs[3 * nb :]
    move_outs, refs = refs[: len(plans)], refs[len(plans) :]
    w_in, w_out, xt, act_s, dgu_s = refs[:5]
    move_ins += [move_outs[which] for which, _ in onward]
    moves = moves_in(plans, move_ins, move_outs, refs[5:])
    done = [which for which, _ in onward]
    nc, _, feat, hid = wg[0].shape
    wide = nb * hid
    width = nc * feat
    e = pl.program_id(0)
    rows = x_refs[0].shape[0]

    @pl.when(e == 0)
    def _():
        greet(partners(plans))
        for move in moves[:count]:
            move.start()

    for later, (which, step) in enumerate(onward):

        @pl.when(e == step)
        def _():
            finish_all([moves[which]])
            moves[count + later].start()

    for j in range(nb):
        for c in range(nc):
            w_in[c * feat : (c + 1) * feat, j * hid : (j + 1) * hid] = wg[j][c, 0]
            w_in[c * feat : (c + 1) * feat, wide + j * hid : wide + (j + 1) * hid] = wu[j][c, 0]
            w_out[j * hid : (j + 1) * hid, c * feat : (c + 1) * feat] = wd[j][c, 0]

    @pl.when(e == 0)
    def _():
        for h in range(sets):
            outs[h][...] = jnp.zeros_like(outs[h])
            dxs[h][...] = jnp.zeros_like(dxs[h])
            for c in range(nc):
                cut_at = slice(c * feat, (c + 1) * feat)
                xt[cut_at, h * rows : (h + 1) * rows] = x_refs[h][:, cut_at].T

    mark, both_marks = mark_ref[0, pl.ds(e, 1), :], mark_ref[1, pl.ds(e, 1), :]
    for h in range(sets):
        x_ref, dy_ref, out_ref, dx_ref = x_refs[h], dy_refs[h], outs[h], dxs[h]

        @pl.loop(0, rows // tile)
        def _(t):
            at = pl.ds(pl.multiple_of(t * tile, tile), tile)
            here = pl.ds(pl.multiple_of(h * rows + t * tile, tile), tile)
            gu = nn(x_ref[at, :width], w_in[...])
            d_act = nt(dy_ref[at, :], w_out[...])
            gate = jnp.sum(x_ref[at, width:].astype(F32) * both_marks, axis=1, keepdims=True)
            spread = jnp.broadcast_to(gate, (tile, hid))
            total = None
            for j in range(nb):
                lo = j * hid
                g = gu[:, lo : lo + hid]
                u = gu[:, wide + lo : wide + lo + hid]
                da = d_act[:, lo : lo + hid]
                sig = 1.0 / (1.0 + jnp.exp(-g))
                swish = g * sig
                su = swish * u
                act_s[here, lo : lo + hid] = (su * spread).astype(BF)
                part = da * su
                total = part if total is None else total + part
                mid = da * spread
                dgu_s[here, lo : lo + hid] = (mid * u * (sig * (1.0 + g * (1.0 - sig)))).astype(BF)
                dgu_s[here, wide + lo : wide + lo + hid] = (mid * swish).astype(BF)
            d_gate = jnp.sum(total, axis=1, keepdims=True) * mark
            dx_ref[at, width:] = (dx_ref[at, width:].astype(F32) + d_gate).astype(BF)
            out_ref[at, :] = (out_ref[at, :].astype(F32) + nn(act_s[here, :], w_out[...])).astype(BF)
            dx_ref[at, :width] = (
                dx_ref[at, :width].astype(F32) + nt(dgu_s[here, :], w_in[...])
            ).astype(BF)

    @pl.loop(0, nc)
    def _(c):
        at = pl.ds(pl.multiple_of(c * feat, feat), feat)
        made = nn(xt[at, :], dgu_s[...])
        for j in range(nb):
            dwg[j][0, at, :] = made[:, j * hid : (j + 1) * hid].astype(BF)
            dwu[j][0, at, :] = made[:, wide + j * hid : wide + (j + 1) * hid].astype(BF)

    made = None
    for h in range(sets):
        part = tn(act_s[h * rows : (h + 1) * rows, :], dy_refs[h][...])
        made = part if made is None else made + part
    for j in range(nb):
        for c in range(nc):
            dwd[j][c, 0] = made[j * hid : (j + 1) * hid, c * feat : (c + 1) * feat].astype(BF)

    @pl.when(e == pl.num_programs(0) - 1)
    def _():
        finish_all([move for which, move in enumerate(moves) if which not in done])


def expert_pass(number, xs, dys, marks, wg, wu, wd, moves, onward=(), tile=512):
    plans, shapes = planned(moves)
    for which, _ in onward:
        plans.append(("row", ("swap", 2), None, size_of("row"), None))
        shapes.append(shapes[which])
    rows, width = dys[0].shape
    sets, nb = len(xs), len(wg)
    nc, local, feat, hid = wg[0].shape
    wide = nb * hid
    lanes = marks.shape[2]
    tile = min(tile, rows)

    def whole(shape):
        return pl.BlockSpec(shape, lambda e: (0,) * len(shape), pipeline_mode=pl.Buffered(1))

    up_spec = pl.BlockSpec((nc, 1, feat, hid), lambda e: (0, e, 0, 0))
    down_spec = pl.BlockSpec((nc, 1, hid, feat), lambda e: (0, e, 0, 0))
    made = pl.pallas_call(
        functools.partial(expert_kernel, sets, nb, tile, plans, onward),
        grid=(local,),
        in_specs=[whole((rows, width + lanes))] * sets
        + [whole((rows, width))] * sets
        + [whole(marks.shape)]
        + [up_spec] * (2 * nb)
        + [down_spec] * nb
        + [HBM] * len(moves),
        out_specs=[whole((rows, width))] * sets
        + [whole((rows, width + lanes))] * sets
        + [pl.BlockSpec((1, width, hid), lambda e: (e, 0, 0))] * (2 * nb)
        + [down_spec] * nb
        + [HBM] * len(plans),
        out_shape=[jax.ShapeDtypeStruct((rows, width), BF)] * sets
        + [jax.ShapeDtypeStruct((rows, width + lanes), BF)] * sets
        + [jax.ShapeDtypeStruct((local, width, hid), BF)] * (2 * nb)
        + [jax.ShapeDtypeStruct((nc, local, hid, feat), BF)] * nb
        + shapes,
        scratch_shapes=[
            pltpu.VMEM((width, 2 * wide), BF),
            pltpu.VMEM((wide, width), BF),
            pltpu.VMEM((width, sets * rows), BF),
            pltpu.VMEM((sets * rows, wide), BF),
            pltpu.VMEM((sets * rows, 2 * wide), BF),
        ]
        + move_sems(plans),
        compiler_params=pltpu.CompilerParams(
            collective_id=number, has_side_effects=True, vmem_limit_bytes=60 * 2**20
        ),
        cost_estimate=FREE,
    )(*xs, *dys, marks, *wg, *wu, *wd, *[move[0] for move in moves])
    made = list(made)
    outs, dxs, made = made[:sets], made[sets : 2 * sets], made[2 * sets :]
    return outs, dxs, [made[:nb], made[nb : 2 * nb], made[2 * nb : 3 * nb]], made[3 * nb :]


def body(
    block_input,
    deal_order,
    lengths,
    routes,
    first_gain,
    w_query,
    key_weight,
    value_weight,
    w_out,
    gain_two,
    w_router,
    w_gate,
    w_up,
    w_down,
    cotangent,
):
    nc, nr, ndp = lax.axis_size("col"), lax.axis_size("row"), lax.axis_size("dp")
    ci, ri, di = lax.axis_index("col"), lax.axis_index("row"), lax.axis_index("dp")
    rows, feat = block_input.shape
    width = feat * nc
    share = rows // nc
    group = rows * nr
    experts, _, hid = w_gate.shape
    halves = 2
    half = di % halves
    local = experts // (nc * halves)
    q_width = w_query.shape[1]
    kv_width = key_weight.shape[1]
    q_heads = q_width // HEAD_SIZE
    kv_heads = kv_width // HEAD_SIZE
    score_scale = 1.0 / math.sqrt(HEAD_SIZE)

    orders = deal_order[0]
    _, positions = places(orders, lengths[0])

    def dealt(a):
        return a.reshape(nr, nc, share).transpose(1, 0, 2).reshape(nc, nr * share)

    orders_all, positions_all = dealt(orders), dealt(positions)
    key_orders = orders_all.reshape(group, 1)
    row_orders = pick(orders_all, ci)[None, :]
    row_positions = pick(positions_all, ci)
    row_starts = row_orders - row_positions[None, :]
    cosine_table, sine_table = rope_tables(row_positions)

    ride = 16
    gain_rows = jnp.concatenate(
        [jnp.stack([first_gain, gain_two]), jnp.zeros((ride - 2, feat), BF)], axis=0
    )
    sent = jnp.concatenate(
        [
            block_input.reshape(nc, share, feat),
            jnp.broadcast_to(gain_rows[None], (nc, ride, feat)),
        ],
        axis=1,
    )
    (got,) = exchange(1, (sent, "col", "major", "lane"))
    got = got.astype(F32)
    x_tok, gains = got[:share], got[share : share + 2]
    inv_one = lax.rsqrt(jnp.mean(x_tok * x_tok, axis=1, keepdims=True) + NORM_EPSILON)
    x_hat = x_tok * inv_one
    w_mine = jnp.concatenate([w_query, key_weight, value_weight], axis=1)
    first_part = max(1, 3 * local // 5)
    bounds = ((0, first_part), (first_part, local))

    def spread(w, part):
        low, high = bounds[part]
        return (w, "col", ("spread", low, local, high - low), "major")

    def to_row(block):
        return (block, "row", ("swap", 2), None)

    def to_core(block):
        return (block, "row", ("swap", 1), None)

    def to_pair(block):
        return (block, "dp", ("swap", 1), None)

    normed, w_qkv, dy_own = exchange(
        2,
        ((x_hat * gains[0]).astype(BF), "row", "all", "major"),
        (w_mine, "col", "shared", "major"),
        (cotangent, "col", "all", "lane"),
    )
    normed = normed.reshape(nr * share, width)
    w_qkv = w_qkv.reshape(width, w_mine.shape[1])

    qkv = dot(w_qkv, normed, ((0,), (1,)))
    count = nr * share
    queries = (rotate(qkv[:q_width], cosine_table, sine_table) * score_scale).astype(BF)
    keys = rotate(qkv[q_width : q_width + kv_width], cosine_table, sine_table).astype(BF)
    values = qkv[q_width + kv_width :].astype(BF)
    tail = jnp.pad(w_router, ((0, 0), (0, 128 - experts)))
    pairs, w_tail, gate_own, dy_pair = exchange(
        3,
        (jnp.concatenate([keys, values], axis=0), "col", "all", "lane"),
        (jnp.concatenate([w_out.T, tail], axis=1), "col", "shared", "major"),
        spread(w_gate, 0),
        to_pair(dy_own),
    )
    w_tail = w_tail.reshape(width, -1)
    w_out_t = w_tail[:, : w_out.shape[0]]
    router = w_tail[:, w_out.shape[0] : w_out.shape[0] + experts]
    mixed, lse, (down_own, gate_row, dy_core, dy_both) = attend(
        4,
        queries,
        pairs,
        key_orders,
        row_orders,
        row_starts,
        kv_heads,
        spread(w_down, 0),
        to_row(gate_own),
        to_core(dy_own),
        to_core(dy_pair),
    )
    dys = [dy_own, dy_core, dy_pair, dy_both]
    branch, up_own = exchange(
        5,
        (
            dot(mixed, w_out_t, ((0,), (1,))).astype(BF).reshape(nr, share, width),
            "row",
            "major",
            "major",
        ),
        spread(w_up, 0),
    )
    hidden = x_tok + block_sum(branch)
    inv_two = lax.rsqrt(jnp.mean(hidden * hidden, axis=1, keepdims=True) + NORM_EPSILON)
    hidden_hat = hidden * inv_two
    normed_two = (hidden_hat * gains[1]).astype(BF)

    lanes = 128
    own_routes = lax.dynamic_slice_in_dim(routes, ri * rows + ci * share, share)
    gates = dense_gates(normed_two, router, own_routes)
    high = gates.astype(BF)
    low = (gates - high.astype(F32)).astype(BF)
    gap = jnp.zeros((share, lanes // 2 - experts), BF)
    rows_of, (down_row, up_row, down_own_b) = gather_pass(
        6,
        jnp.concatenate([normed_two, high, gap, low, gap], axis=1),
        to_row(down_own),
        to_row(up_own),
        spread(w_down, 1),
    )
    first_expert = (half * nc + ci) * local
    places_of = first_expert + jnp.arange(local, dtype=jnp.int32)[:, None]
    lane = jnp.arange(lanes, dtype=jnp.int32)[None, :]
    marks = jnp.stack(
        [lane == places_of, (lane == places_of) | (lane == places_of + lanes // 2)]
    ).astype(F32)

    def experts_of(number, part, blocks, *more):
        cut_at = slice(bounds[part][0], bounds[part][1])
        return expert_pass(number, rows_of, dys, marks[:, cut_at], *blocks, *more)

    last = first_part - 1
    outs_a, d_ins_a, made_a, (gate_own_b, up_own_b, down_row_b, gate_row_b, up_row_b) = experts_of(
        7,
        0,
        ([gate_own, gate_row], [up_own, up_row], [down_own, down_row]),
        [spread(w_gate, 1), spread(w_up, 1), to_row(down_own_b)],
        ((0, min(1, last)), (1, min(2, last))),
    )
    outs_b, d_ins_b, made_b, (down_came,) = experts_of(
        8,
        1,
        ([gate_own_b, gate_row_b], [up_own_b, up_row_b], [down_own_b, down_row_b]),
        [to_row(made_a[2][1])],
    )

    def over_col(block, came, tensor):
        return (add_low(block, came), "col", "major" if tensor == 2 else "second", "major")

    def both(block):
        return (pair_sums(block), "dp", "pair", "major")

    d_parts, out_part, (down_a, gate_came, up_came) = scatter_pass(
        9,
        (d_ins_a, d_ins_b),
        (outs_a, outs_b),
        over_col(made_a[2][0], down_came, 2),
        to_row(made_a[0][1]),
        to_row(made_a[1][1]),
    )
    vmem = {
        "d_parts": d_parts,
        "hidden": hidden,
        "x": x_tok,
        "dy": lax.dynamic_slice_in_dim(dy_own, ci * share, share),
        "gates": jnp.pad(gates, ((0, 0), (0, lanes - experts))),
        "router": w_tail[:, q_width:],
        "gains": gains,
        "w_out": w_out_t.T,
        "q": queries,
        "lse": lse,
        "kv": pairs,
        "key_orders": key_orders,
        "row_orders": row_orders,
        "row_starts": row_starts,
        "mixed": mixed,
        "normed": normed,
        "w_qkv": w_qkv,
        "cosine": cosine_table,
        "sine": sine_table,
        "out_part": out_part,
    }
    hbm = {
        "own_gate_a": made_a[0][0],
        "came_gate_a": gate_came,
        "own_up_a": made_a[1][0],
        "came_up_a": up_came,
        "own_down_b": made_b[2][0],
        "own_gate_b": made_b[0][0],
        "own_up_b": made_b[1][0],
        "go_down_b": made_b[2][1],
        "go_gate_b": made_b[0][1],
        "go_up_b": made_b[1][1],
        "in_down_a": down_a,
    }
    counts = {"a": first_part, "b": local - first_part}
    grads = back_pass(10, vmem, hbm, q_heads, kv_heads, counts)
    d_input = grads["d_input"].reshape(rows, feat).astype(F32)
    block_output = block_sum(grads["output"]).reshape(rows, feat).astype(BF)
    d_gains = block_sum(grads["gain_came"]).reshape(-1)[: 2 * feat].reshape(2, feat)
    d_router = block_sum(grads["router_grad"])[:experts].T

    d_weights = jnp.concatenate([block_sum(grads["out_w_out"]), block_sum(grads["out_w_qkv"])])
    d_weights = pair_sums(d_weights.astype(BF))
    other = swap(d_weights, "dp", 1)
    first = jnp.where(half == 0, d_weights, other).astype(F32)
    second = jnp.where(half == 0, other, d_weights).astype(F32)
    d_w_out = jnp.concatenate([first[: q_width // 2], second[: q_width // 2]])
    d_w_qkv = jnp.concatenate([first[q_width // 2 :], second[q_width // 2 :]]).T
    stacks = [grads.get("out_" + t + "_" + p) for t in ("gate", "up", "down") for p in ("a", "b")]
    if ndp > halves:
        stacks[4] = down_a
        stacks = exchange(11, *[both(stack) for stack in stacks])
    d_w_gate, d_w_up, d_w_down = [widen(*stacks[i : i + 2]) for i in (0, 2, 4)]
    return (
        block_output,
        d_input,
        d_gains[0],
        d_w_qkv[:, :q_width],
        d_w_qkv[:, q_width : q_width + kv_width],
        d_w_qkv[:, q_width + kv_width :],
        d_w_out,
        d_gains[1],
        d_router,
        d_w_gate,
        d_w_up,
        d_w_down,
    )


def solution(mesh):
    residual = P(("dp", "row"), "col")
    return jax.shard_map(
        body,
        mesh=mesh,
        in_specs=(
            residual,
            P("dp", None),
            P("dp", None),
            P("dp", None),
            P("col"),
            P("col", "row"),
            P("col", "row"),
            P("col", "row"),
            P("row", "col"),
            P("col"),
            P("col", None),
            P(None, "col", "row"),
            P(None, "col", "row"),
            P(None, "row", "col"),
            residual,
        ),
        out_specs=(
            residual,
            residual,
            P("col"),
            P("col", "row"),
            P("col", "row"),
            P("col", "row"),
            P("row", "col"),
            P("col"),
            P("col", None),
            P(None, "col", "row"),
            P(None, "col", "row"),
            P(None, "row", "col"),
        ),
        check_vma=False,
    )
```
